32 devices in a mesh: dp: 16 (over z, x, core), fsdp: 2 (over y).
Axes of the slice: x: 2, y: 2, z: 4, core: 2. Of those that a mesh axis runs over, the one named last changes fastest.
Arguments:
- adapter_in: bfloat16 [4096, 8192], P(('dp', 'fsdp')), may hold values from -6 to 6
- frozen: bfloat16 [4096, 8192], P(('dp', 'fsdp')), may hold values from -8 to 8
- gain: float32 [8192], replicated, may hold values from 0.25 to 1.75
- adapter_a: bfloat16 [8192, 64], P('fsdp'), may hold values from -0.0625 to 0.0625
- adapter_up_matrix: bfloat16 [64, 8192], P(None, 'fsdp'), may hold values from -0.75 to 0.75
- passages: bfloat16 [128, 8192], P('dp', 'fsdp'), may hold values from -8 to 8
- positive: int32 [128], P('dp'), may hold values from 0 to 127, as said below
Outputs:
- adapter_grads: float32 [2, 64, 8192], P(None, 'fsdp', 'dp')
- loss: float32 [], replicated
The draws below stay inside these ranges and needn't reach their ends.
Inputs may be any that keep to these rules, and one draw needn't show every extreme that they name: Query i of group g (i from g * 8) has its positive among the passages of the same group, and every passage is the positive of exactly one query.
All inputs are finite; a program needn't handle non-finite values.
Results may differ from the reference program's by a relative error of at most 0.017.
Values may be sent and summed in bfloat16 or wider, within the bound.
A program may use at most 64 MiB of HBM per device.

```python
import jax
import jax.numpy as jnp
from jax import lax

D = 8192
R = 64
LEN = 32
SEQ_DEV = 4
GROUP_PAIRS = 8
PAIRS = 128
TOKENS = 4096


topic_share = 0.5477226


own_share = 0.83666


passage_signal = 0.35


passage_rest = 0.9367497


frozen_signal = 0.6


frozen_rest = 0.8


def pairing(key):
    groups = PAIRS // GROUP_PAIRS
    shuffle_key = jax.random.fold_in(key, 11)
    ranks = jax.random.randint(shuffle_key, (groups, GROUP_PAIRS), 0, 2 ** 20)
    ranked = ranks * GROUP_PAIRS + jnp.arange(GROUP_PAIRS, dtype=jnp.int32)[None, :]
    owners_local = jnp.argsort(ranked, axis=1).astype(jnp.int32)
    positive_local = jnp.argsort(owners_local, axis=1).astype(jnp.int32)
    offsets = (jnp.arange(groups, dtype=jnp.int32) * GROUP_PAIRS)[:, None]
    owners = (owners_local + offsets).reshape(PAIRS)
    positive = (positive_local + offsets).reshape(PAIRS)
    return (owners, positive)


def directions(key):
    topics = PAIRS // GROUP_PAIRS
    topic_table = jax.random.normal(jax.random.fold_in(key, 21), (topics, D), jnp.float32)
    topic_ids = jax.random.randint(jax.random.fold_in(key, 22), (PAIRS,), 0, topics)
    own_part = jax.random.normal(jax.random.fold_in(key, 23), (PAIRS, D), jnp.float32)
    return topic_share * topic_table[topic_ids] + own_share * own_part


def column_profile(factor):
    place = jnp.arange(D, dtype=jnp.float32) / (D - 1.0)
    return jnp.exp(jnp.log(factor) * (place - 0.5))[None, :]


def draw_positive(key, part):
    owners, positive = pairing(key)
    return positive


def draw_frozen(key, part):
    own_key = jax.random.fold_in(key, 5)
    base_dir = directions(key)
    token_noise = jax.random.normal(own_key, (PAIRS, LEN, D), jnp.float32)
    values = frozen_signal * base_dir[:, None, :] + frozen_rest * token_noise
    return jnp.clip(values, -8.0, 8.0).reshape(TOKENS, D).astype(jnp.bfloat16)


def draw_passages(key, part):
    own_key = jax.random.fold_in(key, 7)
    owners, positive = pairing(key)
    base_dir = directions(key)
    passage_noise = jax.random.normal(own_key, (PAIRS, D), jnp.float32)
    row_scale = jnp.ones((PAIRS, 1), jnp.float32)
    profile = column_profile(3.0)
    values = row_scale * profile * (passage_signal * base_dir[owners] + passage_rest * passage_noise)
    return jnp.clip(values, -8.0, 8.0).astype(jnp.bfloat16)


def shard_levels(key, shape, shards, smallest, top_value):
    level, own = 1.0, jax.random.fold_in(key, 6)
    for axis_at, parts in shards:
        draws = jnp.exp(jax.random.uniform(jax.random.fold_in(own, axis_at), (parts,), jnp.float32, smallest / len(shards), top_value / len(shards)))
        level = level * jnp.repeat(draws, shape[axis_at] // parts).reshape([-1 if axis == axis_at else 1 for axis in range(len(shape))])
    return level


def gaussian(key, shape, scale, most, cuts=(), kind=jnp.bfloat16):
    level = shard_levels(key, shape, cuts, -0.22, 0.18) if cuts else 1.0
    drawn = jax.random.normal(key, shape, jnp.float32) * scale * level
    return jnp.minimum(jnp.maximum(drawn, -most), most).astype(kind)


def setup_inputs(seed: int = 0) -> dict:
    key_list = jax.random.split(jax.random.key(seed), 8)
    return {
        "adapter_in": gaussian(key_list[0], (TOKENS, D), 1.0, 6.0, ((0, 32),)),
        "frozen": draw_frozen(jax.random.fold_in(key_list[7], 71), 0),
        "gain": jnp.clip(1.0 + 0.15 * jax.random.normal(key_list[2], (D,), jnp.float32), 0.25, 1.75),
        "adapter_a": gaussian(key_list[3], (D, R), D ** -0.5, 0.0625, ((0, 2),)),
        "adapter_up_matrix": gaussian(key_list[4], (R, D), R ** -0.5, 0.75, ((1, 2),)),
        "passages": draw_passages(jax.random.fold_in(key_list[7], 71), 0),
        "positive": draw_positive(jax.random.fold_in(key_list[7], 71), 0),
    }


adapter_scale_factor = 0.25
inv_temp = 20.0
norm_eps = 1e-05

def forward_block(block_in, frozen_block_slice, gain, adapter_a, adapter_up_matrix):
    latent_code = jnp.dot(block_in, adapter_a, preferred_element_type=jnp.float32).astype(jnp.bfloat16)
    hidden_state = frozen_block_slice.astype(jnp.float32) + adapter_scale_factor * jnp.dot(latent_code, adapter_up_matrix, preferred_element_type=jnp.float32)
    inv_rms = lax.rsqrt(lax.optimization_barrier(jnp.mean(hidden_state * hidden_state, axis=-1, keepdims=True)) + norm_eps)
    normed = hidden_state * inv_rms * gain
    pooled = lax.optimization_barrier(jnp.mean(normed.reshape(-1, LEN, D), axis=1))
    length = jnp.sqrt(lax.optimization_barrier(jnp.sum(pooled * pooled, axis=-1, keepdims=True)))
    return (latent_code, hidden_state, inv_rms, pooled, length)

def reference(adapter_in, frozen, gain, adapter_a, adapter_up_matrix, passages, positive):
    blocks = PAIRS // SEQ_DEV
    tok_blocks = adapter_in.reshape(blocks, SEQ_DEV * LEN, D)
    frozen_blocks = frozen.reshape(blocks, SEQ_DEV * LEN, D)

    def query_of(pair):
        outs = forward_block(pair[0], pair[1], gain, adapter_a, adapter_up_matrix)
        return (outs[3] / outs[4]).astype(jnp.bfloat16)
    query_unit = lax.map(query_of, (tok_blocks, frozen_blocks)).reshape(PAIRS, D)
    pas = passages.astype(jnp.float32)
    passage_unit = (pas / jnp.sqrt(lax.optimization_barrier(jnp.sum(pas * pas, axis=-1, keepdims=True)))).astype(jnp.bfloat16)
    scores = inv_temp * jnp.dot(query_unit, passage_unit.T, preferred_element_type=jnp.float32)
    expo = jnp.exp(scores - inv_temp)
    row_sum = lax.optimization_barrier(jnp.sum(expo, axis=1))
    col_sum = lax.optimization_barrier(jnp.sum(expo, axis=0))
    onehot = (positive[:, None] == jnp.arange(PAIRS, dtype=jnp.int32)[None, :]).astype(jnp.float32)
    loss = (jnp.sum(jnp.log(row_sum)) + jnp.sum(jnp.log(col_sum)) - 2.0 * jnp.sum(scores * onehot)) / (2.0 * PAIRS) + inv_temp
    weights = (0.5 * (expo / row_sum[:, None] + expo / col_sum[None, :]) - onehot).astype(jnp.bfloat16)
    query_grad = inv_temp * jnp.dot(weights, passage_unit, preferred_element_type=jnp.float32)
    grad_blocks = query_grad.reshape(blocks, SEQ_DEV, D)

    def step(total, items):
        block_in, frozen_block_slice, block_grad = items
        latent_code, hidden_state, inv_rms, pooled, length = forward_block(block_in, frozen_block_slice, gain, adapter_a, adapter_up_matrix)
        unit = pooled / length
        pooled_grad = (block_grad - unit * lax.optimization_barrier(jnp.sum(unit * block_grad, axis=-1, keepdims=True))) / length
        normed_grad = jnp.repeat(pooled_grad / LEN, LEN, axis=0)
        scaled = normed_grad * gain
        hidden_state_gradient = (inv_rms * scaled - hidden_state * inv_rms ** 3 * lax.optimization_barrier(jnp.mean(scaled * hidden_state, axis=-1, keepdims=True))).astype(jnp.bfloat16)
        latent_code_gradient = (adapter_scale_factor * jnp.dot(hidden_state_gradient, adapter_up_matrix.T, preferred_element_type=jnp.float32)).astype(jnp.bfloat16)
        grad_a_t = jnp.dot(latent_code_gradient.T, block_in, preferred_element_type=jnp.float32)
        up_matrix_gradient = adapter_scale_factor * jnp.dot(latent_code.T, hidden_state_gradient, preferred_element_type=jnp.float32)
        part = jnp.stack([grad_a_t, up_matrix_gradient]).astype(jnp.bfloat16)
        return (total + part.astype(jnp.float32), None)
    start = jnp.zeros((2, R, D), jnp.float32)
    adapter_grads, unused = lax.scan(step, start, (tok_blocks, frozen_blocks, grad_blocks))
    return (adapter_grads, loss)
```

```python
import functools
import itertools

import jax
import jax.numpy as jnp
from jax import lax
from jax.experimental import pallas as pl
from jax.experimental.pallas import tpu as pltpu
from jax.sharding import PartitionSpec as P

LEN = 32


adapter_scale_factor = 0.25
inv_temp = 20.0
norm_eps = 1e-05


def contracted_row_product(left, right):
    return lax.dot_general(
        left, right, (((1,), (1,)), ((), ())), preferred_element_type=jnp.float32
    )


def shards(adapter_in, frozen, gain, adapter_a, adapter_up_matrix, passages, positive):
    whole_a, full_up_matrix = (
        lax.all_gather(adapter_a, "fsdp", axis=0, tiled=True),
        lax.all_gather(adapter_up_matrix, "fsdp", axis=1, tiled=True),
    )
    width = whole_a.shape[0]
    queries = adapter_in.shape[0] // LEN
    latent_code = jnp.dot(adapter_in, whole_a, preferred_element_type=jnp.float32).astype(
        jnp.bfloat16
    )
    hidden_state = frozen.astype(jnp.float32) + adapter_scale_factor * jnp.dot(
        latent_code, full_up_matrix, preferred_element_type=jnp.float32
    )
    inv_rms = lax.rsqrt(jnp.mean(hidden_state * hidden_state, axis=-1, keepdims=True) + norm_eps)
    normed = hidden_state * inv_rms * gain
    pooled = jnp.mean(normed.reshape(queries, LEN, width), axis=1)
    length = jnp.sqrt(jnp.sum(pooled * pooled, axis=-1, keepdims=True))
    unit = pooled / length
    query_feat = lax.all_to_all(
        unit.astype(jnp.bfloat16), "fsdp", split_axis=1, concat_axis=0, tiled=True
    )
    pas = passages.astype(jnp.float32)
    squares = lax.psum(jnp.sum(pas * pas, axis=-1), "fsdp")
    passage_unit = (pas / jnp.sqrt(squares)[:, None]).astype(jnp.bfloat16)
    total_pairs = passage_unit.shape[0] * lax.axis_size("dp")
    columns = jnp.arange(total_pairs, dtype=jnp.int32)
    partial_value = contracted_row_product(
        query_feat, lax.all_gather(passage_unit, "dp", axis=0, tiled=True)
    )
    scores = inv_temp * lax.psum_scatter(partial_value, "fsdp", scatter_dimension=0, tiled=True)
    own_pos = lax.dynamic_slice_in_dim(positive, lax.axis_index("fsdp") * queries, queries, 0)
    expo = jnp.exp(scores - inv_temp)
    row_sum = jnp.sum(expo, axis=1)
    onehot = (own_pos[:, None] == columns[None, :]).astype(jnp.float32)
    local_term = jnp.sum(jnp.log(row_sum)) - 2.0 * jnp.sum(scores * onehot)
    col_sum, summed = lax.psum((jnp.sum(expo, axis=0), local_term), ("dp", "fsdp"))
    loss = (summed + jnp.sum(jnp.log(col_sum))) / (2.0 * total_pairs) + inv_temp
    weights = (0.5 * (expo / row_sum[:, None] + expo / col_sum[None, :]) - onehot).astype(
        jnp.bfloat16
    )
    group_weights = lax.all_gather(weights, "fsdp", axis=0, tiled=True)
    grad_feat = jnp.dot(
        group_weights,
        lax.all_gather(passage_unit, "dp", axis=0, tiled=True),
        preferred_element_type=jnp.float32,
    )
    query_grad = lax.all_to_all(
        inv_temp * grad_feat, "fsdp", split_axis=0, concat_axis=1, tiled=True
    )
    pooled_grad = (query_grad - unit * jnp.sum(unit * query_grad, axis=-1, keepdims=True)) / length
    normed_grad = jnp.repeat(pooled_grad / LEN, LEN, axis=0)
    scaled = normed_grad * gain
    hidden_state_gradient = (
        inv_rms * scaled
        - hidden_state * inv_rms**3 * jnp.mean(scaled * hidden_state, axis=-1, keepdims=True)
    ).astype(jnp.bfloat16)
    latent_code_gradient = (
        adapter_scale_factor * contracted_row_product(hidden_state_gradient, full_up_matrix)
    ).astype(jnp.bfloat16)
    grad_a_t = jnp.dot(latent_code_gradient.T, adapter_in, preferred_element_type=jnp.float32)
    up_matrix_gradient = adapter_scale_factor * jnp.dot(
        latent_code.T, hidden_state_gradient, preferred_element_type=jnp.float32
    )
    stacked = jnp.stack([grad_a_t, up_matrix_gradient])
    group_sum = lax.psum_scatter(
        stacked.astype(jnp.bfloat16), "fsdp", scatter_dimension=1, tiled=True
    ).astype(jnp.float32)
    adapter_grads = lax.psum_scatter(group_sum, "dp", scatter_dimension=2, tiled=True)
    return (adapter_grads, loss)


WHOLE = slice(None)
MESH = pl.DeviceIdType.MESH


def fused(
    bits, sizes,
    pos_ref, gain_ref, ain_hbm, frz_hbm, a_hbm, up_hbm, pas_hbm,
    out_ref, loss_ref,
    ain, frz, a_own, at_oth, at_snd, up, pas, hid, pasm, part,
    pooled, qg, norms, near, far, rx,
    lsem, ssem, rsem,
):
    tokens, width, rank, queries, rows, chunk = sizes
    half = width // 2
    quarter = half // 4
    dp, fs = lax.axis_index("dp"), lax.axis_index("fsdp")
    groups = 2 ** bits
    pairs = groups * rows
    bit = [(dp // 2 ** b) % 2 for b in range(bits)]

    def peer(mask, flip):
        there = dp
        for b in range(bits):
            if (mask >> b) & 1:
                there = there + (1 - 2 * bit[b]) * 2 ** b
        return (there, 1 - fs if flip else fs)

    def remote(src, dst, k, device):
        return pltpu.make_async_remote_copy(
            src_ref=src, dst_ref=dst, send_sem=ssem.at[k], recv_sem=rsem.at[k],
            device_id=device, device_id_type=MESH,
        )

    started = []

    def send(src, dst, device):
        copy = remote(src, dst, len(started), device)
        copy.start()
        started.append(copy)
        return copy

    def block(number):
        return tuple((number // 2 ** b) % 2 for b in reversed(range(bits)))

    own_cols = pl.ds(pl.multiple_of(fs * half, half), half)
    mine = tuple(reversed(bit))
    loads = [
        pltpu.make_async_copy(up_hbm, up.at[:, own_cols], lsem.at[0]),
        pltpu.make_async_copy(a_hbm, a_own, lsem.at[1]),
        pltpu.make_async_copy(pas_hbm, pas.at[mine + (WHOLE, own_cols)], lsem.at[2]),
        pltpu.make_async_copy(ain_hbm, ain, lsem.at[3]),
        pltpu.make_async_copy(frz_hbm, frz, lsem.at[4]),
    ]
    for load in loads:
        load.start()

    near_masks = [(m, f) for f in (0, 1) for m in range(4) if m or f]
    far_masks = [4 * m for m in range(1, groups // 4)]
    barrier = pltpu.get_barrier_semaphore()
    for m, f in near_masks + [(m, 0) for m in far_masks]:
        pl.semaphore_signal(barrier, inc=1, device_id=peer(m, f), device_id_type=MESH)
    pl.semaphore_wait(barrier, len(near_masks) + len(far_masks))

    def q_at(q, base=0):
        return pl.ds(pl.multiple_of(base + q * quarter, quarter), quarter)

    q0 = dp % 4
    q2 = q0 + 2 - 4 * bit[1]
    other = (1 - fs) * half

    def up_at(q, base):
        return up.at[:, q_at(q, base)]

    def at_at(q):
        return at_oth.at[:, q_at(q)]

    loads[0].wait()
    up_y = send(up_at(q0, fs * half), up_at(q0, fs * half), peer(0, 1))
    loads[1].wait()
    at_snd[...] = a_own[q_at(q0), :].astype(jnp.float32).T.astype(jnp.bfloat16)
    at_y = send(at_snd, at_at(q0), peer(0, 1))

    loads[2].wait()
    upper = list(range(2, bits))
    orders = (upper + [1, "y", 0], ["y", 1] + upper + [0])
    strip = half // 2
    pas_copy = [None, None]
    pas_step = [0, 0]

    def pas_advance(s):
        if pas_copy[s] is not None:
            pas_copy[s].wait_recv()
        if pas_step[s] == len(orders[s]):
            return
        done = orders[s][: pas_step[s]]
        now = orders[s][pas_step[s]]
        index = tuple(WHOLE if b in done else bit[b] for b in reversed(range(bits)))
        if "y" in done:
            views = [pas.at[index + (WHOLE, pl.ds(h * half + s * strip, strip))] for h in (0, 1)]
        else:
            at = pl.multiple_of(fs * half + s * strip, strip)
            views = [pas.at[index + (WHOLE, pl.ds(at, strip))]]
        device = peer(0, 1) if now == "y" else peer(2 ** now, 0)
        pas_copy[s] = Several([send(v, v, device) for v in views])
        pas_step[s] += 1

    pas_advance(0)
    pas_advance(1)

    nn = (((1,), (0,)), ((), ()))
    nt = (((1,), (1,)), ((), ()))

    def mm(left, right, dims):
        return lax.dot_general(left, right, dims, preferred_element_type=jnp.float32)

    loads[3].wait()
    latent_own = mm(ain[:, own_cols], a_own[...], nn)

    up_y.wait_recv()
    up_x = send(up_at(q0, other), up_at(q0, other), peer(2, 0))
    at_y.wait_recv()
    at_x = send(at_at(q0), at_at(q0), peer(2, 0))
    pas_advance(0)
    pas_advance(1)
    up_x.wait_recv()
    up_c = [send(up_at(q, other), up_at(q, other), peer(1, 0)) for q in (q0, q2)]
    at_x.wait_recv()
    at_c = [send(at_at(q), at_at(q), peer(1, 0)) for q in (q0, q2)]
    pas_advance(0)
    pas_advance(1)
    for copy in at_c:
        copy.wait_recv()
    other_cols = pl.ds(pl.multiple_of(other, half), half)
    latent = latent_own + mm(ain[:, other_cols], at_oth[...], nt)
    code = latent.astype(jnp.bfloat16)
    code_t = code.astype(jnp.float32).T.astype(jnp.bfloat16)
    for copy in up_c:
        copy.wait_recv()
    loads[4].wait()

    chunks = width // chunk
    lanes = 128

    def cols_of(j):
        return pl.ds(pl.multiple_of(j * chunk, chunk), chunk)

    def fold(x):
        total = x[:, :lanes]
        for at in range(lanes, chunk, lanes):
            total = total + x[:, at : at + lanes]
        return total

    def forward(j, total):
        cols = cols_of(j)
        value = frz[:, cols].astype(jnp.float32) + adapter_scale_factor * mm(code, up[:, cols], nn)
        hid[:, cols] = value
        return total + fold(value * value)

    total = lax.fori_loop(0, chunks, forward, jnp.zeros((tokens, lanes), jnp.float32))
    inv_rms = lax.rsqrt(jnp.sum(total, axis=1, keepdims=True) / width + norm_eps)

    pas_advance(0)
    pas_advance(1)

    def of_query(q):
        return pl.ds(q * LEN, LEN)

    def pool(j, total):
        cols = cols_of(j)
        each = [
            jnp.sum(hid[of_query(q), cols] * inv_rms[q * LEN : (q + 1) * LEN], axis=0, keepdims=True)
            for q in range(queries)
        ]
        value = jnp.concatenate(each, axis=0) * (gain_ref[:, cols] * (1.0 / LEN))
        pooled[:, cols] = value
        return total + fold(value * value)

    total = lax.fori_loop(0, chunks, pool, jnp.zeros((queries, lanes), jnp.float32))
    length = jnp.sqrt(jnp.sum(total, axis=1, keepdims=True))
    inv_length = 1.0 / length

    while pas_step[0] < len(orders[0]):
        pas_advance(0)
        pas_advance(1)
    pas_advance(0)
    pas_advance(1)

    def gathered(i, _):
        pair = [pas[block(2 * i + c)].astype(jnp.float32) for c in (0, 1)]
        value = jnp.concatenate(pair, axis=0)
        at = pl.ds(pl.multiple_of(i * 2 * rows, 2 * rows), 2 * rows)
        pasm[at, :] = value.astype(jnp.bfloat16)
        square = jnp.sum(value * value, axis=1, keepdims=True)
        norms[at, :] = jnp.broadcast_to(square, (2 * rows, lanes))
        return 0

    lax.fori_loop(0, groups // 2, gathered, 0)
    inv_norm = 1.0 / jnp.sqrt(norms[...].T[0:1, :])

    def score(j, total):
        cols = cols_of(j)
        unit = (pooled[:, cols] * inv_length).astype(jnp.bfloat16)
        return total + mm(unit, pasm[:, cols], nt)

    scores = inv_temp * inv_norm * lax.fori_loop(
        0, chunks, score, jnp.zeros((queries, pairs), jnp.float32)
    )
    expo = jnp.exp(scores - inv_temp)
    row_sum = jnp.sum(expo, axis=1, keepdims=True)
    row_at = lax.broadcasted_iota(jnp.int32, (queries, pairs), 0)
    col_at = lax.broadcasted_iota(jnp.int32, (queries, pairs), 1)
    onehot = jnp.zeros((queries, pairs), jnp.float32)
    for q in range(queries):
        hit = jnp.where(col_at == pos_ref[fs * queries + q], 1.0, 0.0)
        onehot = onehot + jnp.where(row_at == q, hit, 0.0)
    term = jnp.log(jnp.broadcast_to(row_sum, (queries, pairs))) * (1.0 / pairs)
    term = jnp.sum(term - 2.0 * scores * onehot)
    at8 = lax.broadcasted_iota(jnp.int32, (8, pairs), 0)
    col_part = jnp.broadcast_to(jnp.sum(expo, axis=0, keepdims=True), (8, pairs))
    payload = jnp.where(at8 == 0, col_part, jnp.where(at8 == 1, term, 0.0))

    slot = fs * 4 + q0
    near[slot] = payload
    copies = [send(near.at[slot], near.at[slot], peer(m, f)) for m, f in near_masks]
    for copy in copies:
        copy.wait_recv()
    summed = near[0]
    for k in range(1, 8):
        summed = summed + near[k]
    slot = dp // 4
    far[slot] = summed
    copies = [send(far.at[slot], far.at[slot], peer(m, 0)) for m in far_masks]
    for copy in copies:
        copy.wait_recv()
    summed = far[0]
    for k in range(1, groups // 4):
        summed = summed + far[k]
    col_sum = summed[0:1]
    loss_ref[0, 0] = (
        jnp.sum(jnp.log(col_sum) + summed[1:2] * (1.0 / pairs)) / (2.0 * pairs) + inv_temp
    )
    weights = 0.5 * (expo / row_sum + expo / col_sum) - onehot
    weights = weights.astype(jnp.bfloat16).astype(jnp.float32) * (inv_norm * inv_temp)
    high = weights.astype(jnp.bfloat16).astype(jnp.float32)
    both = jnp.concatenate([high, weights - high], axis=0).astype(jnp.bfloat16)

    def query_side(j, total):
        cols = cols_of(j)
        value = mm(both, pasm[:, cols], nn)
        value = value[:queries] + value[queries:]
        qg[:, cols] = value
        return total + fold(value * (pooled[:, cols] * inv_length))

    total = lax.fori_loop(0, chunks, query_side, jnp.zeros((queries, lanes), jnp.float32))
    along = jnp.sum(total, axis=1, keepdims=True)

    def scale_side(j, totals):
        cols = cols_of(j)
        value = qg[:, cols] - pooled[:, cols] * (inv_length * along)
        value = value * (inv_length * (1.0 / LEN)) * gain_ref[:, cols]
        qg[:, cols] = value
        return tuple(
            totals[q] + fold(hid[of_query(q), cols] * value[q : q + 1]) for q in range(queries)
        )

    totals = lax.fori_loop(
        0, chunks, scale_side, tuple(jnp.zeros((LEN, lanes), jnp.float32) for _ in range(queries))
    )
    back = [
        inv_rms[q * LEN : (q + 1) * LEN] ** 3
        * (jnp.sum(totals[q], axis=1, keepdims=True) / width)
        for q in range(queries)
    ]

    def hidden_side(j, total):
        cols = cols_of(j)
        value = jnp.concatenate(
            [
                inv_rms[q * LEN : (q + 1) * LEN] * qg[q : q + 1, cols] - hid[of_query(q), cols] * back[q]
                for q in range(queries)
            ],
            axis=0,
        ).astype(jnp.bfloat16)
        grad = (adapter_scale_factor * mm(code_t, value, nn)).astype(jnp.bfloat16)
        for y in (0, 1):
            part[block(j) + (1, y)] = grad[y * rank // 2 : (y + 1) * rank // 2]
        return total + mm(value, up[:, cols], nt)

    code_grad = lax.fori_loop(0, chunks, hidden_side, jnp.zeros((tokens, rank), jnp.float32))

    grad_orders = ([0, "y", 1] + upper, [0, 1, "y"] + upper)
    grad_copy = [None, None]
    rx_at = [0, len(grad_orders[0])]

    def view(g, done, now, there):
        index = ()
        for b in reversed(range(bits)):
            if b == now:
                index += (1 - bit[b] if there else bit[b],)
            else:
                index += (bit[b] if b in done else WHOLE,)
        if now == "y":
            return index + (g, 1 - fs if there else fs)
        return index + (g, fs if "y" in done else WHOLE)

    def grad_send(g, k):
        order = grad_orders[g]
        now = order[k]
        device = peer(0, 1) if now == "y" else peer(2 ** now, 0)
        grad_copy[g] = send(part.at[view(g, order[:k], now, True)], rx[rx_at[g] + k], device)

    def grad_add(g, k):
        order = grad_orders[g]
        buffer = rx[rx_at[g] + k]
        kept = view(g, order[:k], order[k], False)
        grad_copy[g].wait_recv()
        free = [n for n, i in enumerate(kept) if isinstance(i, slice)]
        for picks in itertools.product((0, 1), repeat=len(free)):
            index = list(kept)
            for n, pick in zip(free, picks):
                index[n] = pick
            index = tuple(index)
            value = part[index].astype(jnp.float32) + buffer[picks].astype(jnp.float32)
            if k == len(order) - 1:
                out_ref[g] = value
            else:
                part[index] = value.astype(jnp.bfloat16)

    grad_send(1, 0)
    code_grad_t = (adapter_scale_factor * code_grad).astype(jnp.bfloat16)
    code_grad_t = code_grad_t.astype(jnp.float32).T.astype(jnp.bfloat16)

    def input_side(j, _):
        grad = mm(code_grad_t, ain[:, cols_of(j)], nn).astype(jnp.bfloat16)
        for y in (0, 1):
            part[block(j) + (0, y)] = grad[y * rank // 2 : (y + 1) * rank // 2]
        return 0

    lax.fori_loop(0, chunks, input_side, 0)
    grad_send(0, 0)
    steps = len(grad_orders[0])
    for k in range(steps):
        for g in (1, 0):
            grad_add(g, k)
            if k + 1 < steps:
                grad_send(g, k + 1)
    for copy in started:
        copy.wait_send()


class Several:
    def __init__(self, copies):
        self.copies = copies

    def wait_recv(self):
        for copy in self.copies:
            copy.wait_recv()


def grad_shapes(bits, rank, chunk, order):
    shapes = []
    for k in range(len(order)):
        gone = order[: k + 1]
        free = bits - len([b for b in gone if b != "y"]) + (0 if "y" in gone else 1)
        shapes.append(pltpu.VMEM((2,) * free + (rank // 2, chunk), jnp.bfloat16))
    return shapes


def fused_shards(bits, adapter_in, frozen, gain, adapter_a, adapter_up_matrix, passages, positive):
    tokens, width = adapter_in.shape
    rank = adapter_a.shape[1]
    queries = tokens // LEN
    rows = passages.shape[0]
    groups = 2 ** bits
    chunk = width // groups
    pairs = groups * rows
    half = width // 2
    bf16, f32 = jnp.bfloat16, jnp.float32
    upper = list(range(2, bits))
    rx = grad_shapes(bits, rank, chunk, [0, "y", 1] + upper)
    rx += grad_shapes(bits, rank, chunk, [0, 1, "y"] + upper)
    copies = 64
    vmem = pl.BlockSpec(memory_space=pltpu.VMEM)
    smem = pl.BlockSpec(memory_space=pltpu.SMEM)
    hbm = pl.BlockSpec(memory_space=pl.ANY)
    grads, loss = pl.pallas_call(
        functools.partial(fused, bits, (tokens, width, rank, queries, rows, chunk)),
        out_shape=(
            jax.ShapeDtypeStruct((2, rank // 2, chunk), f32),
            jax.ShapeDtypeStruct((1, 1), f32),
        ),
        in_specs=[smem, vmem, hbm, hbm, hbm, hbm, hbm],
        out_specs=(vmem, smem),
        scratch_shapes=[
            pltpu.VMEM((tokens, width), bf16),
            pltpu.VMEM((tokens, width), bf16),
            pltpu.VMEM((half, rank), bf16),
            pltpu.VMEM((rank, half), bf16),
            pltpu.VMEM((rank, half // 4), bf16),
            pltpu.VMEM((rank, width), bf16),
            pltpu.VMEM((2,) * bits + (rows, width), bf16),
            pltpu.VMEM((tokens, width), f32),
            pltpu.VMEM((pairs, width), bf16),
            pltpu.VMEM((2,) * bits + (2, 2, rank // 2, chunk), bf16),
            pltpu.VMEM((queries, width), f32),
            pltpu.VMEM((queries, width), f32),
            pltpu.VMEM((pairs, 128), f32),
            pltpu.VMEM((8, 8, pairs), f32),
            pltpu.VMEM((groups // 4, 8, pairs), f32),
            rx,
            pltpu.SemaphoreType.DMA((5,)),
            pltpu.SemaphoreType.DMA((copies,)),
            pltpu.SemaphoreType.DMA((copies,)),
        ],
        compiler_params=pltpu.CompilerParams(
            collective_id=0, has_side_effects=True, vmem_limit_bytes=56 * 2 ** 20
        ),
    )(positive, gain.reshape(1, width), adapter_in, frozen, adapter_a, adapter_up_matrix, passages)
    return grads, loss.reshape(())


def solution(mesh):
    placed = (
        P(("dp", "fsdp"), None),
        P(("dp", "fsdp"), None),
        P(),
        P("fsdp", None),
        P(None, "fsdp"),
        P("dp", "fsdp"),
        P("dp"),
    )
    groups = mesh.shape["dp"]
    bits = groups.bit_length() - 1
    body = shards
    if mesh.shape["fsdp"] == 2 and 4 < groups <= 16 and groups == 2 ** bits:
        body = functools.partial(fused_shards, bits)
    return jax.shard_map(
        body, mesh=mesh, in_specs=placed, out_specs=(P(None, "fsdp", "dp"), P()), check_vma=False
    )
```

```python
import functools
import itertools

import jax
import jax.numpy as jnp
from jax import lax
from jax.experimental import pallas as pl
from jax.experimental.pallas import tpu as pltpu
from jax.sharding import PartitionSpec as P

LEN = 32


adapter_scale_factor = 0.25
inv_temp = 20.0
norm_eps = 1e-05


def contracted_row_product(left, right):
    return lax.dot_general(
        left, right, (((1,), (1,)), ((), ())), preferred_element_type=jnp.float32
    )


def shards(adapter_in, frozen, gain, adapter_a, adapter_up_matrix, passages, positive):
    whole_a, full_up_matrix = (
        lax.all_gather(adapter_a, "fsdp", axis=0, tiled=True),
        lax.all_gather(adapter_up_matrix, "fsdp", axis=1, tiled=True),
    )
    width = whole_a.shape[0]
    queries = adapter_in.shape[0] // LEN
    latent_code = jnp.dot(adapter_in, whole_a, preferred_element_type=jnp.float32).astype(
        jnp.bfloat16
    )
    hidden_state = frozen.astype(jnp.float32) + adapter_scale_factor * jnp.dot(
        latent_code, full_up_matrix, preferred_element_type=jnp.float32
    )
    inv_rms = lax.rsqrt(jnp.mean(hidden_state * hidden_state, axis=-1, keepdims=True) + norm_eps)
    normed = hidden_state * inv_rms * gain
    pooled = jnp.mean(normed.reshape(queries, LEN, width), axis=1)
    length = jnp.sqrt(jnp.sum(pooled * pooled, axis=-1, keepdims=True))
    unit = pooled / length
    query_feat = lax.all_to_all(
        unit.astype(jnp.bfloat16), "fsdp", split_axis=1, concat_axis=0, tiled=True
    )
    pas = passages.astype(jnp.float32)
    squares = lax.psum(jnp.sum(pas * pas, axis=-1), "fsdp")
    passage_unit = (pas / jnp.sqrt(squares)[:, None]).astype(jnp.bfloat16)
    total_pairs = passage_unit.shape[0] * lax.axis_size("dp")
    columns = jnp.arange(total_pairs, dtype=jnp.int32)
    partial_value = contracted_row_product(
        query_feat, lax.all_gather(passage_unit, "dp", axis=0, tiled=True)
    )
    scores = inv_temp * lax.psum_scatter(partial_value, "fsdp", scatter_dimension=0, tiled=True)
    own_pos = lax.dynamic_slice_in_dim(positive, lax.axis_index("fsdp") * queries, queries, 0)
    expo = jnp.exp(scores - inv_temp)
    row_sum = jnp.sum(expo, axis=1)
    onehot = (own_pos[:, None] == columns[None, :]).astype(jnp.float32)
    local_term = jnp.sum(jnp.log(row_sum)) - 2.0 * jnp.sum(scores * onehot)
    col_sum, summed = lax.psum((jnp.sum(expo, axis=0), local_term), ("dp", "fsdp"))
    loss = (summed + jnp.sum(jnp.log(col_sum))) / (2.0 * total_pairs) + inv_temp
    weights = (0.5 * (expo / row_sum[:, None] + expo / col_sum[None, :]) - onehot).astype(
        jnp.bfloat16
    )
    group_weights = lax.all_gather(weights, "fsdp", axis=0, tiled=True)
    grad_feat = jnp.dot(
        group_weights,
        lax.all_gather(passage_unit, "dp", axis=0, tiled=True),
        preferred_element_type=jnp.float32,
    )
    query_grad = lax.all_to_all(
        inv_temp * grad_feat, "fsdp", split_axis=0, concat_axis=1, tiled=True
    )
    pooled_grad = (query_grad - unit * jnp.sum(unit * query_grad, axis=-1, keepdims=True)) / length
    normed_grad = jnp.repeat(pooled_grad / LEN, LEN, axis=0)
    scaled = normed_grad * gain
    hidden_state_gradient = (
        inv_rms * scaled
        - hidden_state * inv_rms**3 * jnp.mean(scaled * hidden_state, axis=-1, keepdims=True)
    ).astype(jnp.bfloat16)
    latent_code_gradient = (
        adapter_scale_factor * contracted_row_product(hidden_state_gradient, full_up_matrix)
    ).astype(jnp.bfloat16)
    grad_a_t = jnp.dot(latent_code_gradient.T, adapter_in, preferred_element_type=jnp.float32)
    up_matrix_gradient = adapter_scale_factor * jnp.dot(
        latent_code.T, hidden_state_gradient, preferred_element_type=jnp.float32
    )
    stacked = jnp.stack([grad_a_t, up_matrix_gradient])
    group_sum = lax.psum_scatter(
        stacked.astype(jnp.bfloat16), "fsdp", scatter_dimension=1, tiled=True
    ).astype(jnp.float32)
    adapter_grads = lax.psum_scatter(group_sum, "dp", scatter_dimension=2, tiled=True)
    return (adapter_grads, loss)


WHOLE = slice(None)
MESH = pl.DeviceIdType.MESH


def fused(
    bits, sizes,
    pos_ref, gain_ref, ain_hbm, frz_hbm, at_hbm, up_hbm, pas_hbm,
    out_ref, loss_ref,
    ain, frz, at, up, pas, hid, pasm, part,
    pooled, near, far, rx,
    lsem, ssem, rsem,
):
    tokens, width, rank, queries, rows, chunk = sizes
    half = width // 2
    quarter = half // 4
    dp, fs = lax.axis_index("dp"), lax.axis_index("fsdp")
    groups = 2 ** bits
    pairs = groups * rows
    bit = [(dp // 2 ** b) % 2 for b in range(bits)]

    def peer(mask, flip):
        there = dp
        for b in range(bits):
            if (mask >> b) & 1:
                there = there + (1 - 2 * bit[b]) * 2 ** b
        return (there, 1 - fs if flip else fs)

    def remote(src, dst, k, device):
        return pltpu.make_async_remote_copy(
            src_ref=src, dst_ref=dst, send_sem=ssem.at[k], recv_sem=rsem.at[k],
            device_id=device, device_id_type=MESH,
        )

    started = []

    def send(src, dst, device):
        copy = remote(src, dst, len(started), device)
        copy.start()
        started.append(copy)
        return copy

    def block(number):
        return tuple((number // 2 ** b) % 2 for b in reversed(range(bits)))

    own_cols = pl.ds(pl.multiple_of(fs * half, half), half)
    mine = tuple(reversed(bit))
    loads = [
        pltpu.make_async_copy(up_hbm, up.at[:, own_cols], lsem.at[0]),
        pltpu.make_async_copy(at_hbm, at.at[:, own_cols], lsem.at[1]),
        pltpu.make_async_copy(pas_hbm, pas.at[mine + (WHOLE, own_cols)], lsem.at[2]),
        pltpu.make_async_copy(ain_hbm, ain, lsem.at[3]),
        pltpu.make_async_copy(frz_hbm, frz, lsem.at[4]),
    ]
    for load in loads:
        load.start()

    near_masks = [(m, f) for f in (0, 1) for m in range(4) if m or f]
    far_masks = [4 * m for m in range(1, groups // 4)]
    barrier = pltpu.get_barrier_semaphore()
    for m, f in near_masks + [(m, 0) for m in far_masks]:
        pl.semaphore_signal(barrier, inc=1, device_id=peer(m, f), device_id_type=MESH)
    pl.semaphore_wait(barrier, len(near_masks) + len(far_masks))

    def q_at(q, base=0):
        return pl.ds(pl.multiple_of(base + q * quarter, quarter), quarter)

    q0 = dp % 4
    q2 = q0 + 2 - 4 * bit[1]
    other = (1 - fs) * half

    def at_at(q, base):
        return at.at[:, q_at(q, base)]

    def up_at(q, base):
        return up.at[:, q_at(q, base)]

    at_y = send(at_hbm.at[:, q_at(q0)], at_at(q0, fs * half), peer(0, 1))
    up_y = send(up_hbm.at[:, q_at(q0)], up_at(q0, fs * half), peer(0, 1))

    loads[2].wait()
    upper = list(range(2, bits))
    orders = (upper + [1, "y", 0], ["y", 1] + upper + [0])
    strip = half // 2
    pas_copy = [None, None]
    pas_step = [0, 0]

    def pas_advance(s):
        if pas_copy[s] is not None:
            pas_copy[s].wait_recv()
        if pas_step[s] == len(orders[s]):
            return
        done = orders[s][: pas_step[s]]
        now = orders[s][pas_step[s]]
        index = tuple(WHOLE if b in done else bit[b] for b in reversed(range(bits)))
        if "y" in done:
            views = [pas.at[index + (WHOLE, pl.ds(h * half + s * strip, strip))] for h in (0, 1)]
        else:
            place = pl.multiple_of(fs * half + s * strip, strip)
            views = [pas.at[index + (WHOLE, pl.ds(place, strip))]]
        device = peer(0, 1) if now == "y" else peer(2 ** now, 0)
        pas_copy[s] = Several([send(v, v, device) for v in views])
        pas_step[s] += 1

    pas_advance(0)
    pas_advance(1)

    nn = (((1,), (0,)), ((), ()))
    nt = (((1,), (1,)), ((), ()))

    def mm(left, right, dims):
        return lax.dot_general(left, right, dims, preferred_element_type=jnp.float32)

    loads[1].wait()
    loads[3].wait()
    latent_own = mm(ain[:, own_cols], at[:, own_cols], nt)

    at_y.wait_recv()
    at_x = send(at_at(q0, other), at_at(q0, other), peer(2, 0))
    up_y.wait_recv()
    up_x = send(up_at(q0, other), up_at(q0, other), peer(2, 0))
    pas_advance(0)
    pas_advance(1)
    at_x.wait_recv()
    at_c = [send(at_at(q, other), at_at(q, other), peer(1, 0)) for q in (q0, q2)]
    pas_advance(0)
    for copy in at_c:
        copy.wait_recv()
    other_cols = pl.ds(pl.multiple_of(other, half), half)
    latent = latent_own + mm(ain[:, other_cols], at[:, other_cols], nt)
    code = latent.astype(jnp.bfloat16)
    code_t = code.astype(jnp.float32).T.astype(jnp.bfloat16)
    up_x.wait_recv()
    up_c = [send(up_at(q, other), up_at(q, other), peer(1, 0)) for q in (q0, q2)]
    pas_advance(1)
    loads[0].wait()
    loads[4].wait()
    for copy in up_c:
        copy.wait_recv()

    chunks = width // chunk
    lanes = 128

    def cols_of(j):
        return pl.ds(pl.multiple_of(j * chunk, chunk), chunk)

    def fold(x):
        total = x[:, :lanes]
        for at in range(lanes, chunk, lanes):
            total = total + x[:, at : at + lanes]
        return total

    def forward(j, total):
        cols = cols_of(j)
        value = frz[:, cols].astype(jnp.float32) + adapter_scale_factor * mm(code, up[:, cols], nn)
        hid[:, cols] = value
        return total + fold(value * value)

    def loop(body, init, unroll=2):
        return lax.fori_loop(0, chunks, body, init, unroll=unroll)

    def of_query(q):
        return slice(q * LEN, (q + 1) * LEN)

    total = loop(forward, jnp.zeros((tokens, lanes), jnp.float32))
    inv_rms = lax.rsqrt(jnp.sum(total, axis=1, keepdims=True) / width + norm_eps)

    pas_advance(0)
    pas_advance(1)

    def pool(j, total):
        cols = cols_of(j)
        each = [
            jnp.sum(hid[of_query(q), cols] * inv_rms[of_query(q)], axis=0, keepdims=True)
            for q in range(queries)
        ]
        value = jnp.concatenate(each, axis=0) * (gain_ref[:, cols] * (1.0 / LEN))
        pooled[:, cols] = value
        return total + fold(value * value)

    total = loop(pool, jnp.zeros((queries, lanes), jnp.float32))
    length = jnp.sqrt(jnp.sum(total, axis=1, keepdims=True))
    inv_length = 1.0 / length

    while pas_step[0] < len(orders[0]):
        pas_advance(0)
        pas_advance(1)
    pas_advance(0)
    pas_advance(1)

    def meet(j, totals):
        meets, squares = totals
        cols = cols_of(j)
        value = jnp.concatenate(
            [pas[block(k) + (WHOLE, cols)].astype(jnp.float32) for k in range(groups)], axis=0
        )
        narrow = value.astype(jnp.bfloat16)
        pasm[:, cols] = narrow
        gained = (hid[:, cols] * gain_ref[:, cols]).astype(jnp.bfloat16)
        return meets + mm(gained, narrow, nt), squares + fold(value * value)

    meets, squares = loop(
        meet, (jnp.zeros((tokens, pairs), jnp.float32), jnp.zeros((pairs, lanes), jnp.float32))
    )
    squares = jnp.broadcast_to(jnp.sum(squares, axis=1, keepdims=True), (pairs, lanes))
    inv_norm = 1.0 / jnp.sqrt(squares.T[0:1, :])
    met = meets * inv_norm
    scores = jnp.concatenate(
        [
            jnp.sum(met[of_query(q)] * inv_rms[of_query(q)], axis=0, keepdims=True)
            for q in range(queries)
        ],
        axis=0,
    ) * (inv_length * (inv_temp / LEN))
    expo = jnp.exp(scores - inv_temp)
    row_sum = jnp.sum(expo, axis=1, keepdims=True)
    row_at = lax.broadcasted_iota(jnp.int32, (queries, pairs), 0)
    col_at = lax.broadcasted_iota(jnp.int32, (queries, pairs), 1)
    onehot = jnp.zeros((queries, pairs), jnp.float32)
    for q in range(queries):
        hit = jnp.where(col_at == pos_ref[fs * queries + q], 1.0, 0.0)
        onehot = onehot + jnp.where(row_at == q, hit, 0.0)
    term = jnp.log(jnp.broadcast_to(row_sum, (queries, pairs))) * (1.0 / pairs)
    term = jnp.sum(term - 2.0 * scores * onehot)
    at8 = lax.broadcasted_iota(jnp.int32, (8, pairs), 0)
    col_part = jnp.broadcast_to(jnp.sum(expo, axis=0, keepdims=True), (8, pairs))
    payload = jnp.where(at8 == 0, col_part, jnp.where(at8 == 1, term, 0.0))

    slot = fs * 4 + q0
    near[slot] = payload
    copies = [send(near.at[slot], near.at[slot], peer(m, f)) for m, f in near_masks]

    def own_side(j, totals):
        cols = cols_of(j)
        value = pooled[:, cols] * gain_ref[:, cols]
        return tuple(
            totals[q] + fold(hid[of_query(q), cols] * value[q : q + 1]) for q in range(queries)
        )

    own = loop(
        own_side, tuple(jnp.zeros((LEN, lanes), jnp.float32) for _ in range(queries))
    )
    own = [
        jnp.sum(own[q], axis=1, keepdims=True) * inv_length[q : q + 1] for q in range(queries)
    ]
    for copy in copies:
        copy.wait_recv()
    summed = near[0]
    for k in range(1, 8):
        summed = summed + near[k]
    slot = dp // 4
    far[slot] = summed
    copies = [send(far.at[slot], far.at[slot], peer(m, 0)) for m in far_masks]
    for copy in copies:
        copy.wait_recv()
    summed = far[0]
    for k in range(1, groups // 4):
        summed = summed + far[k]
    col_sum = summed[0:1]
    loss_ref[0, 0] = (
        jnp.sum(jnp.log(col_sum) + summed[1:2] * (1.0 / pairs)) / (2.0 * pairs) + inv_temp
    )
    weights = 0.5 * (expo / row_sum + expo / col_sum) - onehot
    weights = weights.astype(jnp.bfloat16).astype(jnp.float32)
    along = jnp.sum(weights * scores, axis=1, keepdims=True)
    shrink = inv_length * (1.0 / LEN)
    back = []
    for q in range(queries):
        across = inv_temp * jnp.sum(met[of_query(q)] * weights[q : q + 1], axis=1, keepdims=True)
        mean = (across - own[q] * along[q : q + 1]) * shrink[q : q + 1] / width
        back.append(inv_rms[of_query(q)] ** 3 * mean)
    weights = weights * (inv_norm * inv_temp)
    high = weights.astype(jnp.bfloat16).astype(jnp.float32)
    both = jnp.concatenate([high, weights - high], axis=0).astype(jnp.bfloat16)
    inward = inv_length * along

    def hidden_side(j, total):
        cols = cols_of(j)
        two = mm(both, pasm[:, cols], nn)
        scaled = two[:queries] + two[queries:] - pooled[:, cols] * inward
        scaled = scaled * shrink * gain_ref[:, cols]
        value = jnp.concatenate(
            [
                inv_rms[of_query(q)] * scaled[q : q + 1] - hid[of_query(q), cols] * back[q]
                for q in range(queries)
            ],
            axis=0,
        ).astype(jnp.bfloat16)
        put(1, j, adapter_scale_factor * mm(code_t, value, nn))
        return total + mm(value, up[:, cols], nt)

    def put(g, j, grad):
        grad = grad.astype(jnp.bfloat16)
        for n, (y, h) in enumerate(itertools.product((0, 1), repeat=2)):
            part[block(j) + (g, y, h)] = grad[n * rank // 4 : (n + 1) * rank // 4]

    code_grad = loop(hidden_side, jnp.zeros((tokens, rank), jnp.float32))

    chains = grad_chains(bits)
    grad_copy = [None] * len(chains)
    steps = bits + 1

    def view(n, k, there):
        g, h, order = chains[n]
        done, now = order[:k], order[k]
        index = ()
        for b in reversed(range(bits)):
            if b == now:
                index += (1 - bit[b] if there else bit[b],)
            else:
                index += (bit[b] if b in done else WHOLE,)
        if now == "y":
            return index + (g, 1 - fs if there else fs, h)
        return index + (g, fs if "y" in done else WHOLE, h)

    def grad_send(n, k):
        now = chains[n][2][k]
        device = peer(0, 1) if now == "y" else peer(2 ** now, 0)
        grad_copy[n] = send(part.at[view(n, k, True)], rx[n * steps + k], device)

    def grad_add(n, k):
        g, h, order = chains[n]
        buffer = rx[n * steps + k]
        kept = view(n, k, False)
        grad_copy[n].wait_recv()
        free = [at for at, i in enumerate(kept) if isinstance(i, slice)]
        for picks in itertools.product((0, 1), repeat=len(free)):
            index = list(kept)
            for at_dim, pick in zip(free, picks):
                index[at_dim] = pick
            index = tuple(index)
            value = part[index].astype(jnp.float32) + buffer[picks].astype(jnp.float32)
            if k == len(order) - 1:
                out_ref[g, h * rank // 4 : (h + 1) * rank // 4] = value
            else:
                part[index] = value.astype(jnp.bfloat16)

    early = [n for n, c in enumerate(chains) if c[0] == 1]
    late = [n for n, c in enumerate(chains) if c[0] == 0]
    for n in early:
        grad_send(n, 0)
    code_grad_t = (adapter_scale_factor * code_grad).astype(jnp.bfloat16)
    code_grad_t = code_grad_t.astype(jnp.float32).T.astype(jnp.bfloat16)

    def input_side(j, _):
        put(0, j, mm(code_grad_t, ain[:, cols_of(j)], nn))
        return 0

    loop(input_side, 0)
    for n in late:
        grad_send(n, 0)
    for k in range(steps):
        for n in early + late:
            grad_add(n, k)
            if k + 1 < steps:
                grad_send(n, k + 1)
    for copy in started:
        copy.wait_send()


class Several:
    def __init__(self, copies):
        self.copies = copies

    def wait_recv(self):
        for copy in self.copies:
            copy.wait_recv()


def grad_chains(bits):
    last = list(range(3, bits))
    return [
        (1, 0, [0, 1, "y", 2] + last),
        (1, 1, [0, 2, "y", 1] + last),
        (0, 0, [0, "y", 1, 2] + last),
        (0, 1, [0, 2, 1, "y"] + last),
    ]


def grad_shapes(bits, rank, chunk):
    shapes = []
    for _, _, order in grad_chains(bits):
        for k in range(len(order)):
            gone = order[: k + 1]
            free = bits - len([b for b in gone if b != "y"]) + (0 if "y" in gone else 1)
            shapes.append(pltpu.VMEM((2,) * free + (rank // 4, chunk), jnp.bfloat16))
    return shapes


def fused_shards(bits, adapter_in, frozen, gain, adapter_a, adapter_up_matrix, passages, positive):
    tokens, width = adapter_in.shape
    rank = adapter_a.shape[1]
    queries = tokens // LEN
    rows = passages.shape[0]
    groups = 2 ** bits
    chunk = width // groups
    pairs = groups * rows
    half = width // 2
    bf16, f32 = jnp.bfloat16, jnp.float32
    rx = grad_shapes(bits, rank, chunk)
    copies = 64
    vmem = pl.BlockSpec(memory_space=pltpu.VMEM)
    smem = pl.BlockSpec(memory_space=pltpu.SMEM)
    hbm = pl.BlockSpec(memory_space=pl.ANY)
    grads, loss = pl.pallas_call(
        functools.partial(fused, bits, (tokens, width, rank, queries, rows, chunk)),
        out_shape=(
            jax.ShapeDtypeStruct((2, rank // 2, chunk), f32),
            jax.ShapeDtypeStruct((1, 1), f32),
        ),
        in_specs=[smem, vmem, hbm, hbm, hbm, hbm, hbm],
        out_specs=(vmem, smem),
        scratch_shapes=[
            pltpu.VMEM((tokens, width), bf16),
            pltpu.VMEM((tokens, width), bf16),
            pltpu.VMEM((rank, width), bf16),
            pltpu.VMEM((rank, width), bf16),
            pltpu.VMEM((2,) * bits + (rows, width), bf16),
            pltpu.VMEM((tokens, width), f32),
            pltpu.VMEM((pairs, width), bf16),
            pltpu.VMEM((2,) * bits + (2, 2, 2, rank // 4, chunk), bf16),
            pltpu.VMEM((queries, width), f32),
            pltpu.VMEM((8, 8, pairs), f32),
            pltpu.VMEM((groups // 4, 8, pairs), f32),
            rx,
            pltpu.SemaphoreType.DMA((5,)),
            pltpu.SemaphoreType.DMA((copies,)),
            pltpu.SemaphoreType.DMA((copies,)),
        ],
        compiler_params=pltpu.CompilerParams(
            collective_id=0, has_side_effects=True, vmem_limit_bytes=56 * 2 ** 20
        ),
    )(positive, gain.reshape(1, width), adapter_in, frozen, adapter_a.T, adapter_up_matrix, passages)
    return grads, loss.reshape(())


def solution(mesh):
    placed = (
        P(("dp", "fsdp"), None),
        P(("dp", "fsdp"), None),
        P(),
        P("fsdp", None),
        P(None, "fsdp"),
        P("dp", "fsdp"),
        P("dp"),
    )
    groups = mesh.shape["dp"]
    bits = groups.bit_length() - 1
    body = shards
    if mesh.shape["fsdp"] == 2 and 4 < groups <= 16 and groups == 2 ** bits:
        body = functools.partial(fused_shards, bits)
    return jax.shard_map(
        body, mesh=mesh, in_specs=placed, out_specs=(P(None, "fsdp", "dp"), P()), check_vma=False
    )
```

```python
import functools
import itertools

import jax
import jax.numpy as jnp
from jax import lax
from jax.experimental import pallas as pl
from jax.experimental.pallas import tpu as pltpu
from jax.sharding import PartitionSpec as P

LEN = 32


adapter_scale_factor = 0.25
inv_temp = 20.0
norm_eps = 1e-05


def contracted_row_product(left, right):
    return lax.dot_general(
        left, right, (((1,), (1,)), ((), ())), preferred_element_type=jnp.float32
    )


def shards(adapter_in, frozen, gain, adapter_a, adapter_up_matrix, passages, positive):
    whole_a, full_up_matrix = (
        lax.all_gather(adapter_a, "fsdp", axis=0, tiled=True),
        lax.all_gather(adapter_up_matrix, "fsdp", axis=1, tiled=True),
    )
    width = whole_a.shape[0]
    queries = adapter_in.shape[0] // LEN
    latent_code = jnp.dot(adapter_in, whole_a, preferred_element_type=jnp.float32).astype(
        jnp.bfloat16
    )
    hidden_state = frozen.astype(jnp.float32) + adapter_scale_factor * jnp.dot(
        latent_code, full_up_matrix, preferred_element_type=jnp.float32
    )
    inv_rms = lax.rsqrt(jnp.mean(hidden_state * hidden_state, axis=-1, keepdims=True) + norm_eps)
    normed = hidden_state * inv_rms * gain
    pooled = jnp.mean(normed.reshape(queries, LEN, width), axis=1)
    length = jnp.sqrt(jnp.sum(pooled * pooled, axis=-1, keepdims=True))
    unit = pooled / length
    query_feat = lax.all_to_all(
        unit.astype(jnp.bfloat16), "fsdp", split_axis=1, concat_axis=0, tiled=True
    )
    pas = passages.astype(jnp.float32)
    squares = lax.psum(jnp.sum(pas * pas, axis=-1), "fsdp")
    passage_unit = (pas / jnp.sqrt(squares)[:, None]).astype(jnp.bfloat16)
    total_pairs = passage_unit.shape[0] * lax.axis_size("dp")
    columns = jnp.arange(total_pairs, dtype=jnp.int32)
    partial_value = contracted_row_product(
        query_feat, lax.all_gather(passage_unit, "dp", axis=0, tiled=True)
    )
    scores = inv_temp * lax.psum_scatter(partial_value, "fsdp", scatter_dimension=0, tiled=True)
    own_pos = lax.dynamic_slice_in_dim(positive, lax.axis_index("fsdp") * queries, queries, 0)
    expo = jnp.exp(scores - inv_temp)
    row_sum = jnp.sum(expo, axis=1)
    onehot = (own_pos[:, None] == columns[None, :]).astype(jnp.float32)
    local_term = jnp.sum(jnp.log(row_sum)) - 2.0 * jnp.sum(scores * onehot)
    col_sum, summed = lax.psum((jnp.sum(expo, axis=0), local_term), ("dp", "fsdp"))
    loss = (summed + jnp.sum(jnp.log(col_sum))) / (2.0 * total_pairs) + inv_temp
    weights = (0.5 * (expo / row_sum[:, None] + expo / col_sum[None, :]) - onehot).astype(
        jnp.bfloat16
    )
    group_weights = lax.all_gather(weights, "fsdp", axis=0, tiled=True)
    grad_feat = jnp.dot(
        group_weights,
        lax.all_gather(passage_unit, "dp", axis=0, tiled=True),
        preferred_element_type=jnp.float32,
    )
    query_grad = lax.all_to_all(
        inv_temp * grad_feat, "fsdp", split_axis=0, concat_axis=1, tiled=True
    )
    pooled_grad = (query_grad - unit * jnp.sum(unit * query_grad, axis=-1, keepdims=True)) / length
    normed_grad = jnp.repeat(pooled_grad / LEN, LEN, axis=0)
    scaled = normed_grad * gain
    hidden_state_gradient = (
        inv_rms * scaled
        - hidden_state * inv_rms**3 * jnp.mean(scaled * hidden_state, axis=-1, keepdims=True)
    ).astype(jnp.bfloat16)
    latent_code_gradient = (
        adapter_scale_factor * contracted_row_product(hidden_state_gradient, full_up_matrix)
    ).astype(jnp.bfloat16)
    grad_a_t = jnp.dot(latent_code_gradient.T, adapter_in, preferred_element_type=jnp.float32)
    up_matrix_gradient = adapter_scale_factor * jnp.dot(
        latent_code.T, hidden_state_gradient, preferred_element_type=jnp.float32
    )
    stacked = jnp.stack([grad_a_t, up_matrix_gradient])
    group_sum = lax.psum_scatter(
        stacked.astype(jnp.bfloat16), "fsdp", scatter_dimension=1, tiled=True
    ).astype(jnp.float32)
    adapter_grads = lax.psum_scatter(group_sum, "dp", scatter_dimension=2, tiled=True)
    return (adapter_grads, loss)


WHOLE = slice(None)
MESH = pl.DeviceIdType.MESH


def fused(
    bits, sizes,
    pos_ref, gain_ref, ain_hbm, frz_hbm, at_hbm, up_hbm, pas_hbm,
    out_ref, loss_ref,
    ain, frz, at, up, pas, hid, pasm, part,
    pooled, near, far, rx,
    lsem, ssem, rsem,
):
    tokens, width, rank, queries, rows, chunk = sizes
    half = width // 2
    quarter = half // 4
    dp, fs = lax.axis_index("dp"), lax.axis_index("fsdp")
    groups = 2 ** bits
    pairs = groups * rows
    bit = [(dp // 2 ** b) % 2 for b in range(bits)]

    def peer(mask, flip):
        there = dp
        for b in range(bits):
            if (mask >> b) & 1:
                there = there + (1 - 2 * bit[b]) * 2 ** b
        return (there, 1 - fs if flip else fs)

    def remote(src, dst, k, device):
        return pltpu.make_async_remote_copy(
            src_ref=src, dst_ref=dst, send_sem=ssem.at[k], recv_sem=rsem.at[k],
            device_id=device, device_id_type=MESH,
        )

    started = []

    def send(src, dst, device):
        copy = remote(src, dst, len(started), device)
        copy.start()
        started.append(copy)
        return copy

    def block(number):
        return tuple((number // 2 ** b) % 2 for b in reversed(range(bits)))

    own_cols = pl.ds(pl.multiple_of(fs * half, half), half)
    mine = tuple(reversed(bit))
    loads = [
        pltpu.make_async_copy(up_hbm, up.at[:, own_cols], lsem.at[0]),
        pltpu.make_async_copy(at_hbm, at.at[:, own_cols], lsem.at[1]),
        pltpu.make_async_copy(pas_hbm, pas.at[mine + (WHOLE, own_cols)], lsem.at[2]),
        pltpu.make_async_copy(ain_hbm, ain, lsem.at[3]),
        pltpu.make_async_copy(frz_hbm, frz, lsem.at[4]),
    ]
    for load in loads:
        load.start()

    near_masks = [(m, f) for f in (0, 1) for m in range(4) if m or f]
    far_masks = [4 * m for m in range(1, groups // 4)]
    barrier = pltpu.get_barrier_semaphore()
    for m, f in near_masks + [(m, 0) for m in far_masks]:
        pl.semaphore_signal(barrier, inc=1, device_id=peer(m, f), device_id_type=MESH)
    pl.semaphore_wait(barrier, len(near_masks) + len(far_masks))

    def q_at(q, base=0):
        return pl.ds(pl.multiple_of(base + q * quarter, quarter), quarter)

    q0 = dp % 4
    q2 = q0 + 2 - 4 * bit[1]
    other = (1 - fs) * half

    def at_at(q, base):
        return at.at[:, q_at(q, base)]

    def up_at(q, base):
        return up.at[:, q_at(q, base)]

    far_first = list(range(2, bits))[::-1]
    orders = (
        ["y", 1] + far_first + [0],
        [1, "y"] + far_first + [0],
        far_first + [1, "y", 0],
        far_first + ["y", 1, 0],
    )
    strips = len(orders)
    strip = half // strips
    pas_copy = [None] * strips
    pas_step = [0] * strips

    def pas_advance(*which):
        for s in which:
            if pas_copy[s] is not None:
                for copy in pas_copy[s]:
                    copy.wait_recv()
            done = orders[s][: pas_step[s]]
            pas_step[s] += 1
            if len(done) == len(orders[s]):
                continue
            now = orders[s][len(done)]
            index = tuple(WHOLE if b in done else bit[b] for b in reversed(range(bits)))
            device = peer(0, 1) if now == "y" else peer(2 ** now, 0)
            place = pl.multiple_of(fs * half + s * strip, strip)
            if not done:
                source = pas_hbm.at[:, s * strip : (s + 1) * strip]
                target = pas.at[index + (WHOLE, pl.ds(place, strip))]
                pas_copy[s] = [send(source, target, device)]
                continue
            places = [place]
            if "y" in done:
                places = [h * half + s * strip for h in (0, 1)]
            views = [pas.at[index + (WHOLE, pl.ds(p, strip))] for p in places]
            pas_copy[s] = [send(v, v, device) for v in views]

    pas_advance(0, 1, 2, 3)
    at_y = send(at_hbm.at[:, q_at(q0)], at_at(q0, fs * half), peer(0, 1))
    up_y = send(up_hbm.at[:, q_at(q0)], up_at(q0, fs * half), peer(0, 1))

    loads[2].wait()
    pas_advance(0, 1, 2, 3)

    nn = (((1,), (0,)), ((), ()))
    nt = (((1,), (1,)), ((), ()))

    def mm(left, right, dims):
        return lax.dot_general(left, right, dims, preferred_element_type=jnp.float32)

    loads[1].wait()
    loads[3].wait()
    latent_own = mm(ain[:, own_cols], at[:, own_cols], nt)

    at_y.wait_recv()
    at_x = send(at_at(q0, other), at_at(q0, other), peer(2, 0))
    up_y.wait_recv()
    up_x = send(up_at(q0, other), up_at(q0, other), peer(2, 0))
    pas_advance(0, 1, 2, 3)
    at_x.wait_recv()
    at_c = [send(at_at(q, other), at_at(q, other), peer(1, 0)) for q in (q0, q2)]
    for copy in at_c:
        copy.wait_recv()
    other_cols = pl.ds(pl.multiple_of(other, half), half)
    latent = latent_own + mm(ain[:, other_cols], at[:, other_cols], nt)
    code = latent.astype(jnp.bfloat16)
    code_t = code.astype(jnp.float32).T.astype(jnp.bfloat16)
    up_x.wait_recv()
    up_c = [send(up_at(q, other), up_at(q, other), peer(1, 0)) for q in (q0, q2)]
    for _ in range(bits - 3):
        pas_advance(0, 1, 2, 3)
    loads[0].wait()
    loads[4].wait()
    for copy in up_c:
        copy.wait_recv()

    chunks = width // chunk
    lanes = 128

    def cols_of(j):
        if isinstance(j, int):
            return slice(j * chunk, (j + 1) * chunk)
        return pl.ds(pl.multiple_of(j * chunk, chunk), chunk)

    def fold(x):
        total = x[:, :lanes]
        for at in range(lanes, chunk, lanes):
            total = total + x[:, at : at + lanes]
        return total

    def forward(j, total):
        cols = cols_of(j)
        value = frz[:, cols].astype(jnp.float32) + adapter_scale_factor * mm(code, up[:, cols], nn)
        hid[:, cols] = value
        return total + fold(value * value)

    def loop(body, init, unroll=2):
        return lax.fori_loop(0, chunks, body, init, unroll=unroll)

    def of_query(q):
        return slice(q * LEN, (q + 1) * LEN)

    total = loop(forward, jnp.zeros((tokens, lanes), jnp.float32))
    inv_rms = lax.rsqrt(jnp.sum(total, axis=1, keepdims=True) / width + norm_eps)

    pas_advance(0, 1, 2, 3)

    def pool(j, total):
        cols = cols_of(j)
        each = [
            jnp.sum(hid[of_query(q), cols] * inv_rms[of_query(q)], axis=0, keepdims=True)
            for q in range(queries)
        ]
        value = jnp.concatenate(each, axis=0) * (gain_ref[:, cols] * (1.0 / LEN))
        pooled[:, cols] = value
        return total + fold(value * value)

    total = loop(pool, jnp.zeros((queries, lanes), jnp.float32))
    length = jnp.sqrt(jnp.sum(total, axis=1, keepdims=True))
    inv_length = 1.0 / length

    def meet(j, totals):
        meets, squares = totals
        cols = cols_of(j)
        value = jnp.concatenate(
            [pas[block(k) + (WHOLE, cols)].astype(jnp.float32) for k in range(groups)], axis=0
        )
        narrow = value.astype(jnp.bfloat16)
        pasm[:, cols] = narrow
        gained = (hid[:, cols] * gain_ref[:, cols]).astype(jnp.bfloat16)
        return meets + mm(gained, narrow, nt), squares + fold(value * value)

    totals = jnp.zeros((tokens, pairs), jnp.float32), jnp.zeros((pairs, lanes), jnp.float32)
    for s in range(strips):
        pas_advance(s)
        for h, n in itertools.product((0, 1), range(strip // chunk)):
            totals = meet((h * half + s * strip) // chunk + n, totals)
    meets, squares = totals
    squares = jnp.broadcast_to(jnp.sum(squares, axis=1, keepdims=True), (pairs, lanes))
    inv_norm = 1.0 / jnp.sqrt(squares.T[0:1, :])
    met = meets * inv_norm
    scores = jnp.concatenate(
        [
            jnp.sum(met[of_query(q)] * inv_rms[of_query(q)], axis=0, keepdims=True)
            for q in range(queries)
        ],
        axis=0,
    ) * (inv_length * (inv_temp / LEN))
    expo = jnp.exp(scores - inv_temp)
    row_sum = jnp.sum(expo, axis=1, keepdims=True)
    row_at = lax.broadcasted_iota(jnp.int32, (queries, pairs), 0)
    col_at = lax.broadcasted_iota(jnp.int32, (queries, pairs), 1)
    onehot = jnp.zeros((queries, pairs), jnp.float32)
    for q in range(queries):
        hit = jnp.where(col_at == pos_ref[fs * queries + q], 1.0, 0.0)
        onehot = onehot + jnp.where(row_at == q, hit, 0.0)
    term = jnp.log(jnp.broadcast_to(row_sum, (queries, pairs))) * (1.0 / pairs)
    term = jnp.sum(term - 2.0 * scores * onehot)
    at8 = lax.broadcasted_iota(jnp.int32, (8, pairs), 0)
    col_part = jnp.broadcast_to(jnp.sum(expo, axis=0, keepdims=True), (8, pairs))
    payload = jnp.where(at8 == 0, col_part, jnp.where(at8 == 1, term, 0.0))

    slot = fs * 4 + q0
    near[slot] = payload
    copies = [send(near.at[slot], near.at[slot], peer(m, f)) for m, f in near_masks]

    def own_side(j, totals):
        cols = cols_of(j)
        value = pooled[:, cols] * gain_ref[:, cols]
        return tuple(
            totals[q] + fold(hid[of_query(q), cols] * value[q : q + 1]) for q in range(queries)
        )

    own = loop(
        own_side, tuple(jnp.zeros((LEN, lanes), jnp.float32) for _ in range(queries))
    )
    own = [
        jnp.sum(own[q], axis=1, keepdims=True) * inv_length[q : q + 1] for q in range(queries)
    ]
    for copy in copies:
        copy.wait_recv()
    summed = near[0]
    for k in range(1, 8):
        summed = summed + near[k]
    slot = dp // 4
    far[slot] = summed
    copies = [send(far.at[slot], far.at[slot], peer(m, 0)) for m in far_masks]
    for copy in copies:
        copy.wait_recv()
    summed = far[0]
    for k in range(1, groups // 4):
        summed = summed + far[k]
    col_sum = summed[0:1]
    loss_ref[0, 0] = (
        jnp.sum(jnp.log(col_sum) + summed[1:2] * (1.0 / pairs)) / (2.0 * pairs) + inv_temp
    )
    weights = 0.5 * (expo / row_sum + expo / col_sum) - onehot
    weights = weights.astype(jnp.bfloat16).astype(jnp.float32)
    along = jnp.sum(weights * scores, axis=1, keepdims=True)
    shrink = inv_length * (1.0 / LEN)
    back = []
    for q in range(queries):
        across = inv_temp * jnp.sum(met[of_query(q)] * weights[q : q + 1], axis=1, keepdims=True)
        mean = (across - own[q] * along[q : q + 1]) * shrink[q : q + 1] / width
        back.append(inv_rms[of_query(q)] ** 3 * mean)
    weights = weights * (inv_norm * inv_temp)
    high = weights.astype(jnp.bfloat16).astype(jnp.float32)
    both = jnp.concatenate([high, weights - high], axis=0).astype(jnp.bfloat16)
    inward = inv_length * along

    def hidden_side(j, total):
        cols = cols_of(j)
        two = mm(both, pasm[:, cols], nn)
        scaled = two[:queries] + two[queries:] - pooled[:, cols] * inward
        scaled = scaled * shrink * gain_ref[:, cols]
        value = jnp.concatenate(
            [
                inv_rms[of_query(q)] * scaled[q : q + 1] - hid[of_query(q), cols] * back[q]
                for q in range(queries)
            ],
            axis=0,
        ).astype(jnp.bfloat16)
        put(1, j, adapter_scale_factor * mm(code_t, value, nn))
        return total + mm(value, up[:, cols], nt)

    def put(g, j, grad):
        grad = grad.astype(jnp.bfloat16)
        for n, (y, h) in enumerate(itertools.product((0, 1), repeat=2)):
            part[block(j) + (g, y, h)] = grad[n * rank // 4 : (n + 1) * rank // 4]

    def sided(body, side, init):
        def of(i, carry):
            return body(2 * i + side, carry)

        return lax.fori_loop(0, chunks // 2, of, init, unroll=2)

    theirs, ours = 1 - bit[0], bit[0]
    code_grad = sided(hidden_side, theirs, jnp.zeros((tokens, rank), jnp.float32))

    chains = grad_chains(bits)
    grad_copy = [None] * len(chains)
    steps = bits + 1

    def view(n, k, there):
        g, h, order = chains[n]
        done, now = order[:k], order[k]
        index = ()
        for b in reversed(range(bits)):
            if b == now:
                index += (1 - bit[b] if there else bit[b],)
            else:
                index += (bit[b] if b in done else WHOLE,)
        if now == "y":
            return index + (g, 1 - fs if there else fs, h)
        return index + (g, fs if "y" in done else WHOLE, h)

    def grad_send(n, k):
        now = chains[n][2][k]
        device = peer(0, 1) if now == "y" else peer(2 ** now, 0)
        grad_copy[n] = send(part.at[view(n, k, True)], rx[n * steps + k], device)

    def grad_add(n, k):
        g, h, order = chains[n]
        buffer = rx[n * steps + k]
        kept = view(n, k, False)
        grad_copy[n].wait_recv()
        free = [at for at, i in enumerate(kept) if isinstance(i, slice)]
        for picks in itertools.product((0, 1), repeat=len(free)):
            index = list(kept)
            for at_dim, pick in zip(free, picks):
                index[at_dim] = pick
            index = tuple(index)
            value = part[index].astype(jnp.float32) + buffer[picks].astype(jnp.float32)
            if k == len(order) - 1:
                out_ref[g, h * rank // 4 : (h + 1) * rank // 4] = value
            else:
                part[index] = value.astype(jnp.bfloat16)

    early = [n for n, c in enumerate(chains) if c[0] == 1]
    late = [n for n, c in enumerate(chains) if c[0] == 0]
    for n in early:
        grad_send(n, 0)
    code_grad = sided(hidden_side, ours, code_grad)
    code_grad_t = (adapter_scale_factor * code_grad).astype(jnp.bfloat16)
    code_grad_t = code_grad_t.astype(jnp.float32).T.astype(jnp.bfloat16)

    def input_side(j, _):
        put(0, j, mm(code_grad_t, ain[:, cols_of(j)], nn))
        return 0

    sided(input_side, theirs, 0)
    for n in late:
        grad_send(n, 0)
    sided(input_side, ours, 0)
    for k in range(steps):
        for n in early + late:
            grad_add(n, k)
            if k + 1 < steps:
                grad_send(n, k + 1)
    for copy in started:
        copy.wait_send()


def grad_chains(bits):
    last = list(range(3, bits))
    return [
        (1, 0, [0, 1, "y", 2] + last),
        (1, 1, [0, 2, "y", 1] + last),
        (0, 0, [0, "y", 1, 2] + last),
        (0, 1, [0, 2, 1, "y"] + last),
    ]


def grad_shapes(bits, rank, chunk):
    shapes = []
    for _, _, order in grad_chains(bits):
        for k in range(len(order)):
            gone = order[: k + 1]
            free = bits - len([b for b in gone if b != "y"]) + (0 if "y" in gone else 1)
            shapes.append(pltpu.VMEM((2,) * free + (rank // 4, chunk), jnp.bfloat16))
    return shapes


def fused_shards(bits, adapter_in, frozen, gain, adapter_a, adapter_up_matrix, passages, positive):
    tokens, width = adapter_in.shape
    rank = adapter_a.shape[1]
    queries = tokens // LEN
    rows = passages.shape[0]
    groups = 2 ** bits
    chunk = width // groups
    pairs = groups * rows
    half = width // 2
    bf16, f32 = jnp.bfloat16, jnp.float32
    rx = grad_shapes(bits, rank, chunk)
    copies = 80
    vmem = pl.BlockSpec(memory_space=pltpu.VMEM)
    smem = pl.BlockSpec(memory_space=pltpu.SMEM)
    hbm = pl.BlockSpec(memory_space=pl.ANY)
    grads, loss = pl.pallas_call(
        functools.partial(fused, bits, (tokens, width, rank, queries, rows, chunk)),
        out_shape=(
            jax.ShapeDtypeStruct((2, rank // 2, chunk), f32),
            jax.ShapeDtypeStruct((1, 1), f32),
        ),
        in_specs=[smem, vmem, hbm, hbm, hbm, hbm, hbm],
        out_specs=(vmem, smem),
        scratch_shapes=[
            pltpu.VMEM((tokens, width), bf16),
            pltpu.VMEM((tokens, width), bf16),
            pltpu.VMEM((rank, width), bf16),
            pltpu.VMEM((rank, width), bf16),
            pltpu.VMEM((2,) * bits + (rows, width), bf16),
            pltpu.VMEM((tokens, width), f32),
            pltpu.VMEM((pairs, width), bf16),
            pltpu.VMEM((2,) * bits + (2, 2, 2, rank // 4, chunk), bf16),
            pltpu.VMEM((queries, width), f32),
            pltpu.VMEM((8, 8, pairs), f32),
            pltpu.VMEM((groups // 4, 8, pairs), f32),
            rx,
            pltpu.SemaphoreType.DMA((5,)),
            pltpu.SemaphoreType.DMA((copies,)),
            pltpu.SemaphoreType.DMA((copies,)),
        ],
        compiler_params=pltpu.CompilerParams(
            collective_id=0, has_side_effects=True, vmem_limit_bytes=56 * 2 ** 20
        ),
    )(positive, gain.reshape(1, width), adapter_in, frozen, adapter_a.T, adapter_up_matrix, passages)
    return grads, loss.reshape(())


def solution(mesh):
    placed = (
        P(("dp", "fsdp"), None),
        P(("dp", "fsdp"), None),
        P(),
        P("fsdp", None),
        P(None, "fsdp"),
        P("dp", "fsdp"),
        P("dp"),
    )
    groups = mesh.shape["dp"]
    bits = groups.bit_length() - 1
    body = shards
    if mesh.shape["fsdp"] == 2 and 8 <= groups <= 16 and groups == 2 ** bits:
        body = functools.partial(fused_shards, bits)
    return jax.shard_map(
        body, mesh=mesh, in_specs=placed, out_specs=(P(None, "fsdp", "dp"), P()), check_vma=False
    )
```

```python
import functools
import itertools

import jax
import jax.numpy as jnp
from jax import lax
from jax.experimental import pallas as pl
from jax.experimental.pallas import tpu as pltpu
from jax.sharding import PartitionSpec as P

LEN = 32


adapter_scale_factor = 0.25
inv_temp = 20.0
norm_eps = 1e-05


def contracted_row_product(left, right):
    return lax.dot_general(
        left, right, (((1,), (1,)), ((), ())), preferred_element_type=jnp.float32
    )


def shards(adapter_in, frozen, gain, adapter_a, adapter_up_matrix, passages, positive):
    whole_a, full_up_matrix = (
        lax.all_gather(adapter_a, "fsdp", axis=0, tiled=True),
        lax.all_gather(adapter_up_matrix, "fsdp", axis=1, tiled=True),
    )
    width = whole_a.shape[0]
    queries = adapter_in.shape[0] // LEN
    latent_code = jnp.dot(adapter_in, whole_a, preferred_element_type=jnp.float32).astype(
        jnp.bfloat16
    )
    hidden_state = frozen.astype(jnp.float32) + adapter_scale_factor * jnp.dot(
        latent_code, full_up_matrix, preferred_element_type=jnp.float32
    )
    inv_rms = lax.rsqrt(jnp.mean(hidden_state * hidden_state, axis=-1, keepdims=True) + norm_eps)
    normed = hidden_state * inv_rms * gain
    pooled = jnp.mean(normed.reshape(queries, LEN, width), axis=1)
    length = jnp.sqrt(jnp.sum(pooled * pooled, axis=-1, keepdims=True))
    unit = pooled / length
    query_feat = lax.all_to_all(
        unit.astype(jnp.bfloat16), "fsdp", split_axis=1, concat_axis=0, tiled=True
    )
    pas = passages.astype(jnp.float32)
    squares = lax.psum(jnp.sum(pas * pas, axis=-1), "fsdp")
    passage_unit = (pas / jnp.sqrt(squares)[:, None]).astype(jnp.bfloat16)
    total_pairs = passage_unit.shape[0] * lax.axis_size("dp")
    columns = jnp.arange(total_pairs, dtype=jnp.int32)
    partial_value = contracted_row_product(
        query_feat, lax.all_gather(passage_unit, "dp", axis=0, tiled=True)
    )
    scores = inv_temp * lax.psum_scatter(partial_value, "fsdp", scatter_dimension=0, tiled=True)
    own_pos = lax.dynamic_slice_in_dim(positive, lax.axis_index("fsdp") * queries, queries, 0)
    expo = jnp.exp(scores - inv_temp)
    row_sum = jnp.sum(expo, axis=1)
    onehot = (own_pos[:, None] == columns[None, :]).astype(jnp.float32)
    local_term = jnp.sum(jnp.log(row_sum)) - 2.0 * jnp.sum(scores * onehot)
    col_sum, summed = lax.psum((jnp.sum(expo, axis=0), local_term), ("dp", "fsdp"))
    loss = (summed + jnp.sum(jnp.log(col_sum))) / (2.0 * total_pairs) + inv_temp
    weights = (0.5 * (expo / row_sum[:, None] + expo / col_sum[None, :]) - onehot).astype(
        jnp.bfloat16
    )
    group_weights = lax.all_gather(weights, "fsdp", axis=0, tiled=True)
    grad_feat = jnp.dot(
        group_weights,
        lax.all_gather(passage_unit, "dp", axis=0, tiled=True),
        preferred_element_type=jnp.float32,
    )
    query_grad = lax.all_to_all(
        inv_temp * grad_feat, "fsdp", split_axis=0, concat_axis=1, tiled=True
    )
    pooled_grad = (query_grad - unit * jnp.sum(unit * query_grad, axis=-1, keepdims=True)) / length
    normed_grad = jnp.repeat(pooled_grad / LEN, LEN, axis=0)
    scaled = normed_grad * gain
    hidden_state_gradient = (
        inv_rms * scaled
        - hidden_state * inv_rms**3 * jnp.mean(scaled * hidden_state, axis=-1, keepdims=True)
    ).astype(jnp.bfloat16)
    latent_code_gradient = (
        adapter_scale_factor * contracted_row_product(hidden_state_gradient, full_up_matrix)
    ).astype(jnp.bfloat16)
    grad_a_t = jnp.dot(latent_code_gradient.T, adapter_in, preferred_element_type=jnp.float32)
    up_matrix_gradient = adapter_scale_factor * jnp.dot(
        latent_code.T, hidden_state_gradient, preferred_element_type=jnp.float32
    )
    stacked = jnp.stack([grad_a_t, up_matrix_gradient])
    group_sum = lax.psum_scatter(
        stacked.astype(jnp.bfloat16), "fsdp", scatter_dimension=1, tiled=True
    ).astype(jnp.float32)
    adapter_grads = lax.psum_scatter(group_sum, "dp", scatter_dimension=2, tiled=True)
    return (adapter_grads, loss)


WHOLE = slice(None)
MESH = pl.DeviceIdType.MESH


def fused(
    bits, sizes,
    pos_ref, gain_ref, ain_hbm, frz_hbm, at_hbm, up_hbm, pas_hbm,
    out_ref, loss_ref,
    ain, frz, at, up, pas, hid, pasm, part,
    pooled, scaled, near, far, rx,
    lsem, ssem, rsem,
):
    tokens, width, rank, queries, rows, chunk = sizes
    half = width // 2
    quarter = half // 4
    dp, fs = lax.axis_index("dp"), lax.axis_index("fsdp")
    groups = 2 ** bits
    pairs = groups * rows
    bit = [(dp // 2 ** b) % 2 for b in range(bits)]

    def peer(mask, flip):
        there = dp
        for b in range(bits):
            if (mask >> b) & 1:
                there = there + (1 - 2 * bit[b]) * 2 ** b
        return (there, 1 - fs if flip else fs)

    def remote(src, dst, k, device):
        return pltpu.make_async_remote_copy(
            src_ref=src, dst_ref=dst, send_sem=ssem.at[k], recv_sem=rsem.at[k],
            device_id=device, device_id_type=MESH,
        )

    started = []

    def send(src, dst, device):
        copy = remote(src, dst, len(started), device)
        copy.start()
        started.append(copy)
        return copy

    def block(number):
        return tuple((number // 2 ** b) % 2 for b in reversed(range(bits)))

    own_cols = pl.ds(pl.multiple_of(fs * half, half), half)
    mine = tuple(reversed(bit))
    loads = [
        pltpu.make_async_copy(up_hbm, up.at[:, own_cols], lsem.at[0]),
        pltpu.make_async_copy(at_hbm, at.at[:, own_cols], lsem.at[1]),
        pltpu.make_async_copy(pas_hbm, pas.at[mine + (WHOLE, own_cols)], lsem.at[2]),
        pltpu.make_async_copy(ain_hbm, ain, lsem.at[3]),
        pltpu.make_async_copy(frz_hbm, frz, lsem.at[4]),
    ]
    for load in loads:
        load.start()

    near_masks = [(m, f) for f in (0, 1) for m in range(4) if m or f]
    far_masks = [4 * m for m in range(1, groups // 4)]
    barrier = pltpu.get_barrier_semaphore()
    for m, f in near_masks + [(m, 0) for m in far_masks]:
        pl.semaphore_signal(barrier, inc=1, device_id=peer(m, f), device_id_type=MESH)
    pl.semaphore_wait(barrier, len(near_masks) + len(far_masks))

    def q_at(q, base=0, piece=None):
        if piece is None:
            return pl.ds(pl.multiple_of(base + q * quarter, quarter), quarter)
        size = quarter // 2
        return pl.ds(pl.multiple_of(base + q * quarter + piece * size, size), size)

    q0 = dp % 4
    q1 = q0 + 1 - 2 * bit[0]
    q2 = q0 + 2 - 4 * bit[1]
    q3 = q1 + 2 - 4 * bit[1]
    other = (1 - fs) * half
    pieces = (0, 1)

    def across(whole, own):
        return [
            send(own.at[:, q_at(q0, 0, i)], whole.at[:, q_at(q0, fs * half, i)], peer(0, 1))
            for i in pieces
        ]

    def pass_on(whole, q, i, mask):
        view = whole.at[:, q_at(q, other, i)]
        return send(view, view, peer(mask, 0))

    far_first = list(range(2, bits))[::-1]
    orders = (
        ["y", 1] + far_first + [0],
        [1, "y"] + far_first + [0],
        far_first + [1, "y", 0],
        far_first + ["y", 1, 0],
    )
    strips = len(orders)
    strip = half // strips
    pas_copy = [None] * strips
    pas_step = [0] * strips

    def pas_advance(*which):
        for s in which:
            if pas_copy[s] is not None:
                for copy in pas_copy[s]:
                    copy.wait_recv()
            done = orders[s][: pas_step[s]]
            pas_step[s] += 1
            if len(done) == len(orders[s]):
                continue
            now = orders[s][len(done)]
            index = tuple(WHOLE if b in done else bit[b] for b in reversed(range(bits)))
            device = peer(0, 1) if now == "y" else peer(2 ** now, 0)
            place = pl.multiple_of(fs * half + s * strip, strip)
            if not done:
                source = pas_hbm.at[:, s * strip : (s + 1) * strip]
                target = pas.at[index + (WHOLE, pl.ds(place, strip))]
                pas_copy[s] = [send(source, target, device)]
                continue
            places = [place]
            if "y" in done:
                places = [h * half + s * strip for h in (0, 1)]
            views = [pas.at[index + (WHOLE, pl.ds(p, strip))] for p in places]
            pas_copy[s] = [send(v, v, device) for v in views]

    pas_advance(0, 1, 2, 3)
    at_y = across(at, at_hbm)
    up_y = across(up, up_hbm)

    loads[2].wait()
    pas_advance(0, 1, 2, 3)

    nn = (((1,), (0,)), ((), ()))
    nt = (((1,), (1,)), ((), ()))

    def mm(left, right, dims):
        return lax.dot_general(left, right, dims, preferred_element_type=jnp.float32)

    loads[1].wait()
    loads[3].wait()
    latent = mm(ain[:, own_cols], at[:, own_cols], nt)

    def quarter_of(q):
        cols = q_at(q, other)
        return mm(ain[:, cols], at[:, cols], nt)

    at_x, at_c, up_x, up_c = [], [], [], []
    for i in pieces:
        at_y[i].wait_recv()
        at_x.append(pass_on(at, q0, i, 2))
        at_c.append(pass_on(at, q0, i, 1))
    for i in pieces:
        up_y[i].wait_recv()
        up_x.append(pass_on(up, q0, i, 2))
        up_c.append(pass_on(up, q0, i, 1))
    pas_advance(0, 1, 2, 3)
    latent = latent + quarter_of(q0)
    for i in pieces:
        at_x[i].wait_recv()
        at_c.append(pass_on(at, q2, i, 1))
    latent = latent + quarter_of(q2)
    for copy in at_c[:2]:
        copy.wait_recv()
    latent = latent + quarter_of(q1)
    for copy in at_c[2:]:
        copy.wait_recv()
    latent = latent + quarter_of(q3)
    code = latent.astype(jnp.bfloat16)
    code_t = code.astype(jnp.float32).T.astype(jnp.bfloat16)
    loads[0].wait()
    loads[4].wait()

    chunks = width // chunk
    lanes = 128

    def cols_of(j):
        if isinstance(j, int):
            return slice(j * chunk, (j + 1) * chunk)
        return pl.ds(pl.multiple_of(j * chunk, chunk), chunk)

    def fold(x):
        total = x[:, :lanes]
        for at in range(lanes, chunk, lanes):
            total = total + x[:, at : at + lanes]
        return total

    def forward(j, total):
        cols = cols_of(j)
        value = frz[:, cols].astype(jnp.float32) + adapter_scale_factor * mm(code, up[:, cols], nn)
        hid[:, cols] = value
        return total + fold(value * value)

    def loop(body, init, unroll=2):
        return lax.fori_loop(0, chunks, body, init, unroll=unroll)

    def of_query(q):
        return slice(q * LEN, (q + 1) * LEN)

    def forward_part(start, count, total):
        return lax.fori_loop(0, count, lambda j, t: forward(start + j, t), total, unroll=2)

    part_size = chunks // 4
    total = jnp.zeros((tokens, lanes), jnp.float32)
    total = forward_part(fs * (chunks // 2), part_size, total)
    for i in pieces:
        up_x[i].wait_recv()
        up_c.append(pass_on(up, q2, i, 1))
    total = forward_part(fs * (chunks // 2) + part_size, part_size, total)
    for _ in range(bits - 3):
        pas_advance(0, 1, 2, 3)
    for copy in up_c:
        copy.wait_recv()
    total = forward_part((1 - fs) * (chunks // 2), 2 * part_size, total)
    inv_rms = lax.rsqrt(jnp.sum(total, axis=1, keepdims=True) / width + norm_eps)

    pas_advance(0, 1, 2, 3)

    def pool(j, total):
        cols = cols_of(j)
        each = [
            jnp.sum(hid[of_query(q), cols] * inv_rms[of_query(q)], axis=0, keepdims=True)
            for q in range(queries)
        ]
        value = jnp.concatenate(each, axis=0) * (gain_ref[:, cols] * (1.0 / LEN))
        pooled[:, cols] = value
        return total + fold(value * value)

    total = loop(pool, jnp.zeros((queries, lanes), jnp.float32))
    length = jnp.sqrt(jnp.sum(total, axis=1, keepdims=True))
    inv_length = 1.0 / length

    def meet(j, totals):
        meets, squares = totals
        cols = cols_of(j)
        value = jnp.concatenate(
            [pas[block(k) + (WHOLE, cols)].astype(jnp.float32) for k in range(groups)], axis=0
        )
        narrow = value.astype(jnp.bfloat16)
        pasm[:, cols] = narrow
        gained = (hid[:, cols] * gain_ref[:, cols]).astype(jnp.bfloat16)
        return meets + mm(gained, narrow, nt), squares + fold(value * value)

    totals = jnp.zeros((tokens, pairs), jnp.float32), jnp.zeros((pairs, lanes), jnp.float32)
    for s in range(strips):
        pas_advance(s)
        for h, n in itertools.product((0, 1), range(strip // chunk)):
            totals = meet((h * half + s * strip) // chunk + n, totals)
    meets, squares = totals
    squares = jnp.broadcast_to(jnp.sum(squares, axis=1, keepdims=True), (pairs, lanes))
    inv_norm = 1.0 / jnp.sqrt(squares.T[0:1, :])
    met = meets * inv_norm
    scores = jnp.concatenate(
        [
            jnp.sum(met[of_query(q)] * inv_rms[of_query(q)], axis=0, keepdims=True)
            for q in range(queries)
        ],
        axis=0,
    ) * (inv_length * (inv_temp / LEN))
    expo = jnp.exp(scores - inv_temp)
    row_sum = jnp.sum(expo, axis=1, keepdims=True)
    row_at = lax.broadcasted_iota(jnp.int32, (queries, pairs), 0)
    col_at = lax.broadcasted_iota(jnp.int32, (queries, pairs), 1)
    onehot = jnp.zeros((queries, pairs), jnp.float32)
    for q in range(queries):
        hit = jnp.where(col_at == pos_ref[fs * queries + q], 1.0, 0.0)
        onehot = onehot + jnp.where(row_at == q, hit, 0.0)
    term = jnp.log(jnp.broadcast_to(row_sum, (queries, pairs))) * (1.0 / pairs)
    term = jnp.sum(term - 2.0 * scores * onehot, axis=0, keepdims=True)
    at8 = lax.broadcasted_iota(jnp.int32, (8, pairs), 0)
    col_part = jnp.broadcast_to(jnp.sum(expo, axis=0, keepdims=True), (8, pairs))
    payload = jnp.where(at8 == 0, col_part, jnp.where(at8 == 1, term, 0.0))

    slot = fs * 4 + q0
    near[slot] = payload
    copies = [send(near.at[slot], near.at[slot], peer(m, f)) for m, f in near_masks]

    def own_side(j, totals):
        totals, hidden_up = totals
        cols = cols_of(j)
        value = pooled[:, cols] * gain_ref[:, cols]
        hidden_up = hidden_up + mm(hid[:, cols].astype(jnp.bfloat16), up[:, cols], nt)
        return tuple(
            totals[q] + fold(hid[of_query(q), cols] * value[q : q + 1]) for q in range(queries)
        ), hidden_up

    own, hidden_up = loop(
        own_side,
        (
            tuple(jnp.zeros((LEN, lanes), jnp.float32) for _ in range(queries)),
            jnp.zeros((tokens, rank), jnp.float32),
        ),
    )
    own = [
        jnp.sum(own[q], axis=1, keepdims=True) * inv_length[q : q + 1] for q in range(queries)
    ]
    for copy in copies:
        copy.wait_recv()
    summed = near[0]
    for k in range(1, 8):
        summed = summed + near[k]
    slot = dp // 4
    far[slot] = summed
    copies = [send(far.at[slot], far.at[slot], peer(m, 0)) for m in far_masks]
    for copy in copies:
        copy.wait_recv()
    summed = far[0]
    for k in range(1, groups // 4):
        summed = summed + far[k]
    col_sum = summed[0:1]
    weights = 0.5 * (expo / row_sum + expo / col_sum) - onehot
    weights = weights.astype(jnp.bfloat16).astype(jnp.float32)
    along = jnp.sum(weights * scores, axis=1, keepdims=True)
    shrink = inv_length * (1.0 / LEN)
    back = []
    for q in range(queries):
        across = inv_temp * jnp.sum(met[of_query(q)] * weights[q : q + 1], axis=1, keepdims=True)
        mean = (across - own[q] * along[q : q + 1]) * shrink[q : q + 1] / width
        back.append(inv_rms[of_query(q)] ** 3 * mean)
    weights = weights * (inv_norm * inv_temp)
    high = weights.astype(jnp.bfloat16).astype(jnp.float32)
    both = jnp.concatenate([high, weights - high], axis=0).astype(jnp.bfloat16)
    inward = inv_length * along

    def query_side(j, total):
        cols = cols_of(j)
        two = mm(both, pasm[:, cols], nn)
        value = two[:queries] + two[queries:] - pooled[:, cols] * inward
        value = value * shrink * gain_ref[:, cols]
        scaled[:, cols] = value
        return total + mm(value.astype(jnp.bfloat16), up[:, cols], nt)

    def hidden_side(j, _):
        cols = cols_of(j)
        value = jnp.concatenate(
            [
                inv_rms[of_query(q)] * scaled[q : q + 1, cols] - hid[of_query(q), cols] * back[q]
                for q in range(queries)
            ],
            axis=0,
        ).astype(jnp.bfloat16)
        put(1, j, adapter_scale_factor * mm(code_t, value, nn))
        return 0

    def put(g, j, grad):
        grad = grad.astype(jnp.bfloat16)
        for n, (y, h) in enumerate(itertools.product((0, 1), repeat=2)):
            part[block(j) + (g, y, h)] = grad[n * rank // 4 : (n + 1) * rank // 4]

    def sided(body, side, init):
        def of(i, carry):
            return body(2 * i + side, carry)

        return lax.fori_loop(0, chunks // 2, of, init, unroll=2)

    theirs, ours = 1 - bit[0], bit[0]
    query_up = loop(query_side, jnp.zeros((queries, rank), jnp.float32), 4)
    code_grad = jnp.concatenate(
        [
            inv_rms[of_query(q)] * query_up[q : q + 1] - hidden_up[of_query(q)] * back[q]
            for q in range(queries)
        ],
        axis=0,
    )
    code_grad_t = (adapter_scale_factor * code_grad).astype(jnp.bfloat16)
    code_grad_t = code_grad_t.astype(jnp.float32).T.astype(jnp.bfloat16)

    def input_side(j, _):
        put(0, j, mm(code_grad_t, ain[:, cols_of(j)], nn))
        return 0

    chains = grad_chains(bits)
    grad_copy = [None] * len(chains)
    steps = bits + 1

    def view(n, k, there):
        g, h, order = chains[n]
        done, now = order[:k], order[k]
        index = ()
        for b in reversed(range(bits)):
            if b == now:
                index += (1 - bit[b] if there else bit[b],)
            else:
                index += (bit[b] if b in done else WHOLE,)
        if now == "y":
            return index + (g, 1 - fs if there else fs, h)
        return index + (g, fs if "y" in done else WHOLE, h)

    def grad_send(n, k):
        now = chains[n][2][k]
        device = peer(0, 1) if now == "y" else peer(2 ** now, 0)
        grad_copy[n] = send(part.at[view(n, k, True)], rx[n * steps + k], device)

    def grad_add(n, k):
        g, h, order = chains[n]
        buffer = rx[n * steps + k]
        kept = view(n, k, False)
        grad_copy[n].wait_recv()
        free = [at for at, i in enumerate(kept) if isinstance(i, slice)]
        for picks in itertools.product((0, 1), repeat=len(free)):
            index = list(kept)
            for at_dim, pick in zip(free, picks):
                index[at_dim] = pick
            index = tuple(index)
            value = part[index].astype(jnp.float32) + buffer[picks].astype(jnp.float32)
            if k == len(order) - 1:
                out_ref[g, h * rank // 4 : (h + 1) * rank // 4] = value
            else:
                part[index] = value.astype(jnp.bfloat16)

    early = [n for n, c in enumerate(chains) if c[0] == 0]
    late = [n for n, c in enumerate(chains) if c[0] == 1]
    sided(input_side, theirs, 0)
    for n in early:
        grad_send(n, 0)
    sided(hidden_side, theirs, 0)
    for n in late:
        grad_send(n, 0)
    sided(input_side, ours, 0)
    for n in early:
        grad_add(n, 0)
        grad_send(n, 1)
    sided(hidden_side, ours, 0)
    for n in late:
        grad_add(n, 0)
        grad_send(n, 1)
    loss_ref[0, 0] = (
        jnp.sum(jnp.log(col_sum) + summed[1:2]) / (2.0 * pairs) + inv_temp
    )
    for k in range(1, steps):
        for n in early + late:
            grad_add(n, k)
            if k + 1 < steps:
                grad_send(n, k + 1)
    for copy in started:
        copy.wait_send()


def grad_chains(bits):
    last = list(range(3, bits))
    return [
        (1, 0, [0, 1, "y", 2] + last),
        (1, 1, [0, 2, "y", 1] + last),
        (0, 0, [0, "y", 1, 2] + last),
        (0, 1, [0, 2, 1, "y"] + last),
    ]


def grad_shapes(bits, rank, chunk):
    shapes = []
    for _, _, order in grad_chains(bits):
        for k in range(len(order)):
            gone = order[: k + 1]
            free = bits - len([b for b in gone if b != "y"]) + (0 if "y" in gone else 1)
            shapes.append(pltpu.VMEM((2,) * free + (rank // 4, chunk), jnp.bfloat16))
    return shapes


def fused_shards(bits, adapter_in, frozen, gain, adapter_a, adapter_up_matrix, passages, positive):
    tokens, width = adapter_in.shape
    rank = adapter_a.shape[1]
    queries = tokens // LEN
    rows = passages.shape[0]
    groups = 2 ** bits
    chunk = width // groups
    pairs = groups * rows
    half = width // 2
    bf16, f32 = jnp.bfloat16, jnp.float32
    rx = grad_shapes(bits, rank, chunk)
    copies = 96
    vmem = pl.BlockSpec(memory_space=pltpu.VMEM)
    smem = pl.BlockSpec(memory_space=pltpu.SMEM)
    hbm = pl.BlockSpec(memory_space=pl.ANY)
    grads, loss = pl.pallas_call(
        functools.partial(fused, bits, (tokens, width, rank, queries, rows, chunk)),
        out_shape=(
            jax.ShapeDtypeStruct((2, rank // 2, chunk), f32),
            jax.ShapeDtypeStruct((1, 1), f32),
        ),
        in_specs=[smem, vmem, hbm, hbm, hbm, hbm, hbm],
        out_specs=(vmem, smem),
        scratch_shapes=[
            pltpu.VMEM((tokens, width), bf16),
            pltpu.VMEM((tokens, width), bf16),
            pltpu.VMEM((rank, width), bf16),
            pltpu.VMEM((rank, width), bf16),
            pltpu.VMEM((2,) * bits + (rows, width), bf16),
            pltpu.VMEM((tokens, width), f32),
            pltpu.VMEM((pairs, width), bf16),
            pltpu.VMEM((2,) * bits + (2, 2, 2, rank // 4, chunk), bf16),
            pltpu.VMEM((queries, width), f32),
            pltpu.VMEM((queries, width), f32),
            pltpu.VMEM((8, 8, pairs), f32),
            pltpu.VMEM((groups // 4, 8, pairs), f32),
            rx,
            pltpu.SemaphoreType.DMA((5,)),
            pltpu.SemaphoreType.DMA((copies,)),
            pltpu.SemaphoreType.DMA((copies,)),
        ],
        compiler_params=pltpu.CompilerParams(
            collective_id=0, has_side_effects=True, vmem_limit_bytes=56 * 2 ** 20
        ),
    )(positive, gain.reshape(1, width), adapter_in, frozen, adapter_a.T, adapter_up_matrix, passages)
    return grads, loss.reshape(())


def solution(mesh):
    placed = (
        P(("dp", "fsdp"), None),
        P(("dp", "fsdp"), None),
        P(),
        P("fsdp", None),
        P(None, "fsdp"),
        P("dp", "fsdp"),
        P("dp"),
    )
    groups = mesh.shape["dp"]
    bits = groups.bit_length() - 1
    body = shards
    if mesh.shape["fsdp"] == 2 and 8 <= groups <= 16 and groups == 2 ** bits:
        body = functools.partial(fused_shards, bits)
    return jax.shard_map(
        body, mesh=mesh, in_specs=placed, out_specs=(P(None, "fsdp", "dp"), P()), check_vma=False
    )
```

```python
import functools
import itertools

import jax
import jax.numpy as jnp
from jax import lax
from jax.experimental import pallas as pl
from jax.experimental.pallas import tpu as pltpu
from jax.sharding import PartitionSpec as P

LEN = 32


adapter_scale_factor = 0.25
inv_temp = 20.0
norm_eps = 1e-05


def contracted_row_product(left, right):
    return lax.dot_general(
        left, right, (((1,), (1,)), ((), ())), preferred_element_type=jnp.float32
    )


def shards(adapter_in, frozen, gain, adapter_a, adapter_up_matrix, passages, positive):
    whole_a, full_up_matrix = (
        lax.all_gather(adapter_a, "fsdp", axis=0, tiled=True),
        lax.all_gather(adapter_up_matrix, "fsdp", axis=1, tiled=True),
    )
    width = whole_a.shape[0]
    queries = adapter_in.shape[0] // LEN
    latent_code = jnp.dot(adapter_in, whole_a, preferred_element_type=jnp.float32).astype(
        jnp.bfloat16
    )
    hidden_state = frozen.astype(jnp.float32) + adapter_scale_factor * jnp.dot(
        latent_code, full_up_matrix, preferred_element_type=jnp.float32
    )
    inv_rms = lax.rsqrt(jnp.mean(hidden_state * hidden_state, axis=-1, keepdims=True) + norm_eps)
    normed = hidden_state * inv_rms * gain
    pooled = jnp.mean(normed.reshape(queries, LEN, width), axis=1)
    length = jnp.sqrt(jnp.sum(pooled * pooled, axis=-1, keepdims=True))
    unit = pooled / length
    query_feat = lax.all_to_all(
        unit.astype(jnp.bfloat16), "fsdp", split_axis=1, concat_axis=0, tiled=True
    )
    pas = passages.astype(jnp.float32)
    squares = lax.psum(jnp.sum(pas * pas, axis=-1), "fsdp")
    passage_unit = (pas / jnp.sqrt(squares)[:, None]).astype(jnp.bfloat16)
    total_pairs = passage_unit.shape[0] * lax.axis_size("dp")
    columns = jnp.arange(total_pairs, dtype=jnp.int32)
    partial_value = contracted_row_product(
        query_feat, lax.all_gather(passage_unit, "dp", axis=0, tiled=True)
    )
    scores = inv_temp * lax.psum_scatter(partial_value, "fsdp", scatter_dimension=0, tiled=True)
    own_pos = lax.dynamic_slice_in_dim(positive, lax.axis_index("fsdp") * queries, queries, 0)
    expo = jnp.exp(scores - inv_temp)
    row_sum = jnp.sum(expo, axis=1)
    onehot = (own_pos[:, None] == columns[None, :]).astype(jnp.float32)
    local_term = jnp.sum(jnp.log(row_sum)) - 2.0 * jnp.sum(scores * onehot)
    col_sum, summed = lax.psum((jnp.sum(expo, axis=0), local_term), ("dp", "fsdp"))
    loss = (summed + jnp.sum(jnp.log(col_sum))) / (2.0 * total_pairs) + inv_temp
    weights = (0.5 * (expo / row_sum[:, None] + expo / col_sum[None, :]) - onehot).astype(
        jnp.bfloat16
    )
    group_weights = lax.all_gather(weights, "fsdp", axis=0, tiled=True)
    grad_feat = jnp.dot(
        group_weights,
        lax.all_gather(passage_unit, "dp", axis=0, tiled=True),
        preferred_element_type=jnp.float32,
    )
    query_grad = lax.all_to_all(
        inv_temp * grad_feat, "fsdp", split_axis=0, concat_axis=1, tiled=True
    )
    pooled_grad = (query_grad - unit * jnp.sum(unit * query_grad, axis=-1, keepdims=True)) / length
    normed_grad = jnp.repeat(pooled_grad / LEN, LEN, axis=0)
    scaled = normed_grad * gain
    hidden_state_gradient = (
        inv_rms * scaled
        - hidden_state * inv_rms**3 * jnp.mean(scaled * hidden_state, axis=-1, keepdims=True)
    ).astype(jnp.bfloat16)
    latent_code_gradient = (
        adapter_scale_factor * contracted_row_product(hidden_state_gradient, full_up_matrix)
    ).astype(jnp.bfloat16)
    grad_a_t = jnp.dot(latent_code_gradient.T, adapter_in, preferred_element_type=jnp.float32)
    up_matrix_gradient = adapter_scale_factor * jnp.dot(
        latent_code.T, hidden_state_gradient, preferred_element_type=jnp.float32
    )
    stacked = jnp.stack([grad_a_t, up_matrix_gradient])
    group_sum = lax.psum_scatter(
        stacked.astype(jnp.bfloat16), "fsdp", scatter_dimension=1, tiled=True
    ).astype(jnp.float32)
    adapter_grads = lax.psum_scatter(group_sum, "dp", scatter_dimension=2, tiled=True)
    return (adapter_grads, loss)


WHOLE = slice(None)
MESH = pl.DeviceIdType.MESH


def fused(
    bits, sizes,
    pos_ref, gain_ref, ain_hbm, frz_hbm, at_hbm, up_hbm, pas_hbm,
    out_ref, loss_ref,
    ain, frz, at, up, pas, hid, pasm, part,
    pooled, scaled, near, far, rx,
    lsem, ssem, rsem,
):
    tokens, width, rank, queries, rows, chunk = sizes
    half = width // 2
    quarter = half // 4
    dp, fs = lax.axis_index("dp"), lax.axis_index("fsdp")
    groups = 2 ** bits
    pairs = groups * rows
    bit = [(dp // 2 ** b) % 2 for b in range(bits)]

    def peer(mask, flip):
        there = dp
        for b in range(bits):
            if (mask >> b) & 1:
                there = there + (1 - 2 * bit[b]) * 2 ** b
        return (there, 1 - fs if flip else fs)

    def remote(src, dst, k, device):
        return pltpu.make_async_remote_copy(
            src_ref=src, dst_ref=dst, send_sem=ssem.at[k], recv_sem=rsem.at[k],
            device_id=device, device_id_type=MESH,
        )

    started = []

    def send(src, dst, device):
        copy = remote(src, dst, len(started), device)
        copy.start()
        started.append(copy)
        return copy

    def block(number):
        return tuple((number // 2 ** b) % 2 for b in reversed(range(bits)))

    own_cols = pl.ds(pl.multiple_of(fs * half, half), half)
    mine = tuple(reversed(bit))
    loads = [
        pltpu.make_async_copy(up_hbm, up.at[:, own_cols], lsem.at[0]),
        pltpu.make_async_copy(at_hbm, at.at[:, own_cols], lsem.at[1]),
        pltpu.make_async_copy(pas_hbm, pas.at[mine + (WHOLE, own_cols)], lsem.at[2]),
        pltpu.make_async_copy(ain_hbm, ain, lsem.at[3]),
        pltpu.make_async_copy(frz_hbm, frz, lsem.at[4]),
    ]
    for load in loads:
        load.start()

    near_masks = [(m, f) for f in (0, 1) for m in range(4) if m or f]
    far_masks = [4 * m for m in range(1, groups // 4)]
    barrier = pltpu.get_barrier_semaphore()
    for m, f in near_masks + [(m, 0) for m in far_masks]:
        pl.semaphore_signal(barrier, inc=1, device_id=peer(m, f), device_id_type=MESH)
    pl.semaphore_wait(barrier, len(near_masks) + len(far_masks))

    def q_at(q, base=0, piece=None):
        if piece is None:
            return pl.ds(pl.multiple_of(base + q * quarter, quarter), quarter)
        size = quarter // 2
        return pl.ds(pl.multiple_of(base + q * quarter + piece * size, size), size)

    q0 = dp % 4
    q1 = q0 + 1 - 2 * bit[0]
    q2 = q0 + 2 - 4 * bit[1]
    q3 = q1 + 2 - 4 * bit[1]
    other = (1 - fs) * half
    pieces = (0, 1)

    def across(whole, own):
        return [
            send(own.at[:, q_at(q0, 0, i)], whole.at[:, q_at(q0, fs * half, i)], peer(0, 1))
            for i in pieces
        ]

    def pass_on(whole, q, i, mask):
        view = whole.at[:, q_at(q, other, i)]
        return send(view, view, peer(mask, 0))

    far_first = list(range(2, bits))[::-1]
    orders = (
        ["y", 1] + far_first + [0],
        ["y", 1] + far_first + [0],
        far_first + [1, "y", 0],
        far_first + ["y", 1, 0],
    )
    strips = len(orders)
    strip = half // strips
    pas_copy = [None] * strips
    pas_step = [0] * strips

    def pas_advance(*which):
        for s in which:
            if pas_copy[s] is not None:
                for copy in pas_copy[s]:
                    copy.wait_recv()
            done = orders[s][: pas_step[s]]
            pas_step[s] += 1
            if len(done) == len(orders[s]):
                continue
            now = orders[s][len(done)]
            index = tuple(WHOLE if b in done else bit[b] for b in reversed(range(bits)))
            device = peer(0, 1) if now == "y" else peer(2 ** now, 0)
            place = pl.multiple_of(fs * half + s * strip, strip)
            if not done:
                source = pas_hbm.at[:, s * strip : (s + 1) * strip]
                target = pas.at[index + (WHOLE, pl.ds(place, strip))]
                pas_copy[s] = [send(source, target, device)]
                continue
            places = [place]
            if "y" in done:
                places = [h * half + s * strip for h in (0, 1)]
            views = [pas.at[index + (WHOLE, pl.ds(p, strip))] for p in places]
            pas_copy[s] = [send(v, v, device) for v in views]

    pas_advance(0, 1, 2, 3)
    at_y = across(at, at_hbm)
    up_y = across(up, up_hbm)

    loads[2].wait()
    pas_advance(0, 1, 2, 3)

    nn = (((1,), (0,)), ((), ()))
    nt = (((1,), (1,)), ((), ()))

    def mm(left, right, dims):
        return lax.dot_general(left, right, dims, preferred_element_type=jnp.float32)

    loads[1].wait()
    loads[3].wait()
    latent = mm(ain[:, own_cols], at[:, own_cols], nt)

    def quarter_of(q):
        cols = q_at(q, other)
        return mm(ain[:, cols], at[:, cols], nt)

    at_x, at_c, up_x, up_c = [], [], [], []
    for i in pieces:
        at_y[i].wait_recv()
        at_x.append(pass_on(at, q0, i, 2))
        at_c.append(pass_on(at, q0, i, 1))
    pas_advance(0, 1, 3)
    for i in pieces:
        up_y[i].wait_recv()
        up_x.append(pass_on(up, q0, i, 2))
        up_c.append(pass_on(up, q0, i, 1))
    pas_advance(2)
    latent = latent + quarter_of(q0)
    for i in pieces:
        at_x[i].wait_recv()
        at_c.append(pass_on(at, q2, i, 1))
    latent = latent + quarter_of(q2)
    pas_advance(0)
    for copy in at_c[:2]:
        copy.wait_recv()
    latent = latent + quarter_of(q1)
    for copy in at_c[2:]:
        copy.wait_recv()
    latent = latent + quarter_of(q3)
    code = latent.astype(jnp.bfloat16)
    code_t = code.astype(jnp.float32).T.astype(jnp.bfloat16)
    loads[0].wait()
    loads[4].wait()

    chunks = width // chunk
    lanes = 128

    def cols_of(j):
        if isinstance(j, int):
            return slice(j * chunk, (j + 1) * chunk)
        return pl.ds(pl.multiple_of(j * chunk, chunk), chunk)

    def fold(x):
        total = x[:, :lanes]
        for at in range(lanes, chunk, lanes):
            total = total + x[:, at : at + lanes]
        return total

    def forward(j, total):
        cols = cols_of(j)
        value = frz[:, cols].astype(jnp.float32) + adapter_scale_factor * mm(code, up[:, cols], nn)
        hid[:, cols] = value
        return total + fold(value * value)

    def loop(body, init, unroll=2):
        return lax.fori_loop(0, chunks, body, init, unroll=unroll)

    def of_query(q):
        return slice(q * LEN, (q + 1) * LEN)

    def forward_part(start, count, total):
        return lax.fori_loop(0, count, lambda j, t: forward(start + j, t), total, unroll=2)

    part_size = chunks // 4
    total = jnp.zeros((tokens, lanes), jnp.float32)
    total = forward_part(fs * (chunks // 2), part_size, total)
    for i in pieces:
        up_x[i].wait_recv()
        up_c.append(pass_on(up, q2, i, 1))
    total = forward_part(fs * (chunks // 2) + part_size, part_size, total)
    pas_advance(1, 3, 2)
    for copy in up_c:
        copy.wait_recv()
    total = forward_part((1 - fs) * (chunks // 2), 2 * part_size, total)
    inv_rms = lax.rsqrt(jnp.sum(total, axis=1, keepdims=True) / width + norm_eps)

    pas_advance(0, 1, 2, 3)

    def pool(j, total):
        cols = cols_of(j)
        each = [
            jnp.sum(hid[of_query(q), cols] * inv_rms[of_query(q)], axis=0, keepdims=True)
            for q in range(queries)
        ]
        value = jnp.concatenate(each, axis=0) * (gain_ref[:, cols] * (1.0 / LEN))
        pooled[:, cols] = value
        return total + fold(value * value)

    total = loop(pool, jnp.zeros((queries, lanes), jnp.float32))
    length = jnp.sqrt(jnp.sum(total, axis=1, keepdims=True))
    inv_length = 1.0 / length

    def meet(j, totals):
        meets, squares = totals
        cols = cols_of(j)
        value = jnp.concatenate(
            [pas[block(k) + (WHOLE, cols)].astype(jnp.float32) for k in range(groups)], axis=0
        )
        narrow = value.astype(jnp.bfloat16)
        pasm[:, cols] = narrow
        gained = (hid[:, cols] * gain_ref[:, cols]).astype(jnp.bfloat16)
        return meets + mm(gained, narrow, nt), squares + fold(value * value)

    totals = jnp.zeros((tokens, pairs), jnp.float32), jnp.zeros((pairs, lanes), jnp.float32)
    for s in range(strips):
        pas_advance(s)
        for h, n in itertools.product((0, 1), range(strip // chunk)):
            totals = meet((h * half + s * strip) // chunk + n, totals)
    meets, squares = totals
    squares = jnp.broadcast_to(jnp.sum(squares, axis=1, keepdims=True), (pairs, lanes))
    inv_norm = 1.0 / jnp.sqrt(squares.T[0:1, :])
    met = meets * inv_norm
    scores = jnp.concatenate(
        [
            jnp.sum(met[of_query(q)] * inv_rms[of_query(q)], axis=0, keepdims=True)
            for q in range(queries)
        ],
        axis=0,
    ) * (inv_length * (inv_temp / LEN))
    expo = jnp.exp(scores - inv_temp)
    row_sum = jnp.sum(expo, axis=1, keepdims=True)
    row_at = lax.broadcasted_iota(jnp.int32, (queries, pairs), 0)
    col_at = lax.broadcasted_iota(jnp.int32, (queries, pairs), 1)
    onehot = jnp.zeros((queries, pairs), jnp.float32)
    for q in range(queries):
        hit = jnp.where(col_at == pos_ref[fs * queries + q], 1.0, 0.0)
        onehot = onehot + jnp.where(row_at == q, hit, 0.0)
    term = jnp.log(jnp.broadcast_to(row_sum, (queries, pairs))) * (1.0 / pairs)
    term = jnp.sum(term - 2.0 * scores * onehot, axis=0, keepdims=True)
    at8 = lax.broadcasted_iota(jnp.int32, (8, pairs), 0)
    col_part = jnp.broadcast_to(jnp.sum(expo, axis=0, keepdims=True), (8, pairs))
    payload = jnp.where(at8 == 0, col_part, jnp.where(at8 == 1, term, 0.0))

    slot = fs * 4 + q0
    near[slot] = payload
    copies = [send(near.at[slot], near.at[slot], peer(m, f)) for m, f in near_masks]

    def own_side(j, totals):
        totals, hidden_up = totals
        cols = cols_of(j)
        value = pooled[:, cols] * gain_ref[:, cols]
        hidden_up = hidden_up + mm(hid[:, cols].astype(jnp.bfloat16), up[:, cols], nt)
        return tuple(
            totals[q] + fold(hid[of_query(q), cols] * value[q : q + 1]) for q in range(queries)
        ), hidden_up

    own, hidden_up = loop(
        own_side,
        (
            tuple(jnp.zeros((LEN, lanes), jnp.float32) for _ in range(queries)),
            jnp.zeros((tokens, rank), jnp.float32),
        ),
    )
    own = [
        jnp.sum(own[q], axis=1, keepdims=True) * inv_length[q : q + 1] for q in range(queries)
    ]
    for copy in copies:
        copy.wait_recv()
    summed = near[0]
    for k in range(1, 8):
        summed = summed + near[k]
    slot = dp // 4
    far[slot] = summed
    copies = [send(far.at[slot], far.at[slot], peer(m, 0)) for m in far_masks]
    for copy in copies:
        copy.wait_recv()
    summed = far[0]
    for k in range(1, groups // 4):
        summed = summed + far[k]
    col_sum = summed[0:1]
    weights = 0.5 * (expo / row_sum + expo / col_sum) - onehot
    weights = weights.astype(jnp.bfloat16).astype(jnp.float32)
    along = jnp.sum(weights * scores, axis=1, keepdims=True)
    shrink = inv_length * (1.0 / LEN)
    back = []
    for q in range(queries):
        across = inv_temp * jnp.sum(met[of_query(q)] * weights[q : q + 1], axis=1, keepdims=True)
        mean = (across - own[q] * along[q : q + 1]) * shrink[q : q + 1] / width
        back.append(inv_rms[of_query(q)] ** 3 * mean)
    weights = weights * (inv_norm * inv_temp)
    high = weights.astype(jnp.bfloat16).astype(jnp.float32)
    both = jnp.concatenate([high, weights - high], axis=0).astype(jnp.bfloat16)
    inward = inv_length * along

    def query_side(j, total):
        cols = cols_of(j)
        two = mm(both, pasm[:, cols], nn)
        value = two[:queries] + two[queries:] - pooled[:, cols] * inward
        value = value * shrink * gain_ref[:, cols]
        scaled[:, cols] = value
        return total + mm(value.astype(jnp.bfloat16), up[:, cols], nt)

    def hidden_side(j, _):
        cols = cols_of(j)
        value = jnp.concatenate(
            [
                inv_rms[of_query(q)] * scaled[q : q + 1, cols] - hid[of_query(q), cols] * back[q]
                for q in range(queries)
            ],
            axis=0,
        ).astype(jnp.bfloat16)
        put(1, j, adapter_scale_factor * mm(code_t, value, nn))
        return 0

    def put(g, j, grad):
        grad = grad.astype(jnp.bfloat16)
        for n, (y, h) in enumerate(itertools.product((0, 1), repeat=2)):
            part[block(j) + (g, y, h)] = grad[n * rank // 4 : (n + 1) * rank // 4]

    def sided(body, side, init):
        def of(i, carry):
            return body(2 * i + side, carry)

        return lax.fori_loop(0, chunks // 2, of, init, unroll=2)

    theirs, ours = 1 - bit[0], bit[0]
    query_up = loop(query_side, jnp.zeros((queries, rank), jnp.float32), 4)
    code_grad = jnp.concatenate(
        [
            inv_rms[of_query(q)] * query_up[q : q + 1] - hidden_up[of_query(q)] * back[q]
            for q in range(queries)
        ],
        axis=0,
    )
    code_grad_t = (adapter_scale_factor * code_grad).astype(jnp.bfloat16)
    code_grad_t = code_grad_t.astype(jnp.float32).T.astype(jnp.bfloat16)

    def input_side(j, _):
        put(0, j, mm(code_grad_t, ain[:, cols_of(j)], nn))
        return 0

    chains = grad_chains(bits)
    grad_copy = [None] * len(chains)
    steps = bits + 1

    def view(n, k, there):
        g, h, order = chains[n]
        done, now = order[:k], order[k]
        index = ()
        for b in reversed(range(bits)):
            if b == now:
                index += (1 - bit[b] if there else bit[b],)
            else:
                index += (bit[b] if b in done else WHOLE,)
        if now == "y":
            return index + (g, 1 - fs if there else fs, h)
        return index + (g, fs if "y" in done else WHOLE, h)

    def grad_send(n, k):
        now = chains[n][2][k]
        device = peer(0, 1) if now == "y" else peer(2 ** now, 0)
        grad_copy[n] = send(part.at[view(n, k, True)], rx[n * steps + k], device)

    def grad_add(n, k):
        g, h, order = chains[n]
        buffer = rx[n * steps + k]
        kept = view(n, k, False)
        grad_copy[n].wait_recv()
        free = [at for at, i in enumerate(kept) if isinstance(i, slice)]
        for picks in itertools.product((0, 1), repeat=len(free)):
            index = list(kept)
            for at_dim, pick in zip(free, picks):
                index[at_dim] = pick
            index = tuple(index)
            value = part[index].astype(jnp.float32) + buffer[picks].astype(jnp.float32)
            if k == len(order) - 1:
                out_ref[g, h * rank // 4 : (h + 1) * rank // 4] = value
            else:
                part[index] = value.astype(jnp.bfloat16)

    early = [n for n, c in enumerate(chains) if c[0] == 0]
    late = [n for n, c in enumerate(chains) if c[0] == 1]
    sided(input_side, theirs, 0)
    for n in early:
        grad_send(n, 0)
    sided(hidden_side, theirs, 0)
    for n in late:
        grad_send(n, 0)
    sided(input_side, ours, 0)
    for n in early:
        grad_add(n, 0)
        grad_send(n, 1)
    sided(hidden_side, ours, 0)
    for n in late:
        grad_add(n, 0)
        grad_send(n, 1)
    loss_ref[0, 0] = (
        jnp.sum(jnp.log(col_sum) + summed[1:2]) / (2.0 * pairs) + inv_temp
    )
    for k in range(1, steps):
        for n in early + late:
            grad_add(n, k)
            if k + 1 < steps:
                grad_send(n, k + 1)
    for copy in started:
        copy.wait_send()


def grad_chains(bits):
    last = list(range(3, bits))
    return [
        (1, 0, [0, 1, "y", 2] + last),
        (1, 1, [0, 2, "y", 1] + last),
        (0, 0, [0, "y", 1, 2] + last),
        (0, 1, [0, 2, 1, "y"] + last),
    ]


def grad_shapes(bits, rank, chunk):
    shapes = []
    for _, _, order in grad_chains(bits):
        for k in range(len(order)):
            gone = order[: k + 1]
            free = bits - len([b for b in gone if b != "y"]) + (0 if "y" in gone else 1)
            shapes.append(pltpu.VMEM((2,) * free + (rank // 4, chunk), jnp.bfloat16))
    return shapes


def fused_shards(bits, adapter_in, frozen, gain, adapter_a, adapter_up_matrix, passages, positive):
    tokens, width = adapter_in.shape
    rank = adapter_a.shape[1]
    queries = tokens // LEN
    rows = passages.shape[0]
    groups = 2 ** bits
    chunk = width // groups
    pairs = groups * rows
    half = width // 2
    bf16, f32 = jnp.bfloat16, jnp.float32
    rx = grad_shapes(bits, rank, chunk)
    copies = 96
    vmem = pl.BlockSpec(memory_space=pltpu.VMEM)
    smem = pl.BlockSpec(memory_space=pltpu.SMEM)
    hbm = pl.BlockSpec(memory_space=pl.ANY)
    grads, loss = pl.pallas_call(
        functools.partial(fused, bits, (tokens, width, rank, queries, rows, chunk)),
        out_shape=(
            jax.ShapeDtypeStruct((2, rank // 2, chunk), f32),
            jax.ShapeDtypeStruct((1, 1), f32),
        ),
        in_specs=[smem, vmem, hbm, hbm, hbm, hbm, hbm],
        out_specs=(vmem, smem),
        scratch_shapes=[
            pltpu.VMEM((tokens, width), bf16),
            pltpu.VMEM((tokens, width), bf16),
            pltpu.VMEM((rank, width), bf16),
            pltpu.VMEM((rank, width), bf16),
            pltpu.VMEM((2,) * bits + (rows, width), bf16),
            pltpu.VMEM((tokens, width), f32),
            pltpu.VMEM((pairs, width), bf16),
            pltpu.VMEM((2,) * bits + (2, 2, 2, rank // 4, chunk), bf16),
            pltpu.VMEM((queries, width), f32),
            pltpu.VMEM((queries, width), f32),
            pltpu.VMEM((8, 8, pairs), f32),
            pltpu.VMEM((groups // 4, 8, pairs), f32),
            rx,
            pltpu.SemaphoreType.DMA((5,)),
            pltpu.SemaphoreType.DMA((copies,)),
            pltpu.SemaphoreType.DMA((copies,)),
        ],
        compiler_params=pltpu.CompilerParams(
            collective_id=0, has_side_effects=True, vmem_limit_bytes=56 * 2 ** 20
        ),
    )(positive, gain.reshape(1, width), adapter_in, frozen, adapter_a.T, adapter_up_matrix, passages)
    return grads, loss.reshape(())


def solution(mesh):
    placed = (
        P(("dp", "fsdp"), None),
        P(("dp", "fsdp"), None),
        P(),
        P("fsdp", None),
        P(None, "fsdp"),
        P("dp", "fsdp"),
        P("dp"),
    )
    groups = mesh.shape["dp"]
    bits = groups.bit_length() - 1
    body = shards
    if mesh.shape["fsdp"] == 2 and groups == 16:
        body = functools.partial(fused_shards, bits)
    return jax.shard_map(
        body, mesh=mesh, in_specs=placed, out_specs=(P(None, "fsdp", "dp"), P()), check_vma=False
    )
```

```python
import functools
import itertools

import jax
import jax.numpy as jnp
from jax import lax
from jax.experimental import pallas as pl
from jax.experimental.pallas import tpu as pltpu
from jax.sharding import PartitionSpec as P

LEN = 32


adapter_scale_factor = 0.25
inv_temp = 20.0
norm_eps = 1e-05


def contracted_row_product(left, right):
    return lax.dot_general(
        left, right, (((1,), (1,)), ((), ())), preferred_element_type=jnp.float32
    )


def shards(adapter_in, frozen, gain, adapter_a, adapter_up_matrix, passages, positive):
    whole_a, full_up_matrix = (
        lax.all_gather(adapter_a, "fsdp", axis=0, tiled=True),
        lax.all_gather(adapter_up_matrix, "fsdp", axis=1, tiled=True),
    )
    width = whole_a.shape[0]
    queries = adapter_in.shape[0] // LEN
    latent_code = jnp.dot(adapter_in, whole_a, preferred_element_type=jnp.float32).astype(
        jnp.bfloat16
    )
    hidden_state = frozen.astype(jnp.float32) + adapter_scale_factor * jnp.dot(
        latent_code, full_up_matrix, preferred_element_type=jnp.float32
    )
    inv_rms = lax.rsqrt(jnp.mean(hidden_state * hidden_state, axis=-1, keepdims=True) + norm_eps)
    normed = hidden_state * inv_rms * gain
    pooled = jnp.mean(normed.reshape(queries, LEN, width), axis=1)
    length = jnp.sqrt(jnp.sum(pooled * pooled, axis=-1, keepdims=True))
    unit = pooled / length
    query_feat = lax.all_to_all(
        unit.astype(jnp.bfloat16), "fsdp", split_axis=1, concat_axis=0, tiled=True
    )
    pas = passages.astype(jnp.float32)
    squares = lax.psum(jnp.sum(pas * pas, axis=-1), "fsdp")
    passage_unit = (pas / jnp.sqrt(squares)[:, None]).astype(jnp.bfloat16)
    total_pairs = passage_unit.shape[0] * lax.axis_size("dp")
    columns = jnp.arange(total_pairs, dtype=jnp.int32)
    partial_value = contracted_row_product(
        query_feat, lax.all_gather(passage_unit, "dp", axis=0, tiled=True)
    )
    scores = inv_temp * lax.psum_scatter(partial_value, "fsdp", scatter_dimension=0, tiled=True)
    own_pos = lax.dynamic_slice_in_dim(positive, lax.axis_index("fsdp") * queries, queries, 0)
    expo = jnp.exp(scores - inv_temp)
    row_sum = jnp.sum(expo, axis=1)
    onehot = (own_pos[:, None] == columns[None, :]).astype(jnp.float32)
    local_term = jnp.sum(jnp.log(row_sum)) - 2.0 * jnp.sum(scores * onehot)
    col_sum, summed = lax.psum((jnp.sum(expo, axis=0), local_term), ("dp", "fsdp"))
    loss = (summed + jnp.sum(jnp.log(col_sum))) / (2.0 * total_pairs) + inv_temp
    weights = (0.5 * (expo / row_sum[:, None] + expo / col_sum[None, :]) - onehot).astype(
        jnp.bfloat16
    )
    group_weights = lax.all_gather(weights, "fsdp", axis=0, tiled=True)
    grad_feat = jnp.dot(
        group_weights,
        lax.all_gather(passage_unit, "dp", axis=0, tiled=True),
        preferred_element_type=jnp.float32,
    )
    query_grad = lax.all_to_all(
        inv_temp * grad_feat, "fsdp", split_axis=0, concat_axis=1, tiled=True
    )
    pooled_grad = (query_grad - unit * jnp.sum(unit * query_grad, axis=-1, keepdims=True)) / length
    normed_grad = jnp.repeat(pooled_grad / LEN, LEN, axis=0)
    scaled = normed_grad * gain
    hidden_state_gradient = (
        inv_rms * scaled
        - hidden_state * inv_rms**3 * jnp.mean(scaled * hidden_state, axis=-1, keepdims=True)
    ).astype(jnp.bfloat16)
    latent_code_gradient = (
        adapter_scale_factor * contracted_row_product(hidden_state_gradient, full_up_matrix)
    ).astype(jnp.bfloat16)
    grad_a_t = jnp.dot(latent_code_gradient.T, adapter_in, preferred_element_type=jnp.float32)
    up_matrix_gradient = adapter_scale_factor * jnp.dot(
        latent_code.T, hidden_state_gradient, preferred_element_type=jnp.float32
    )
    stacked = jnp.stack([grad_a_t, up_matrix_gradient])
    group_sum = lax.psum_scatter(
        stacked.astype(jnp.bfloat16), "fsdp", scatter_dimension=1, tiled=True
    ).astype(jnp.float32)
    adapter_grads = lax.psum_scatter(group_sum, "dp", scatter_dimension=2, tiled=True)
    return (adapter_grads, loss)


WHOLE = slice(None)
MESH = pl.DeviceIdType.MESH


def fused(
    bits, sizes,
    pos_ref, gain_ref, ain_hbm, frz_hbm, at_hbm, up_hbm, pas_hbm,
    out_ref, loss_ref,
    ain, frz, at, up, pas, hid, pasm, part,
    pooled, scaled, near, far, rx,
    lsem, ssem, rsem,
):
    tokens, width, rank, queries, rows, chunk = sizes
    half = width // 2
    quarter = half // 4
    dp, fs = lax.axis_index("dp"), lax.axis_index("fsdp")
    groups = 2 ** bits
    pairs = groups * rows
    bit = [(dp // 2 ** b) % 2 for b in range(bits)]

    def peer(mask, flip):
        there = dp
        for b in range(bits):
            if (mask >> b) & 1:
                there = there + (1 - 2 * bit[b]) * 2 ** b
        return (there, 1 - fs if flip else fs)

    def remote(src, dst, k, device):
        return pltpu.make_async_remote_copy(
            src_ref=src, dst_ref=dst, send_sem=ssem.at[k], recv_sem=rsem.at[k],
            device_id=device, device_id_type=MESH,
        )

    started = []

    def send(src, dst, device):
        copy = remote(src, dst, len(started), device)
        copy.start()
        started.append(copy)
        return copy

    def block(number):
        return tuple((number // 2 ** b) % 2 for b in reversed(range(bits)))

    own_cols = pl.ds(pl.multiple_of(fs * half, half), half)
    mine = tuple(reversed(bit))
    loads = [
        pltpu.make_async_copy(up_hbm, up.at[:, own_cols], lsem.at[0]),
        pltpu.make_async_copy(at_hbm, at.at[:, own_cols], lsem.at[1]),
        pltpu.make_async_copy(pas_hbm, pas.at[mine + (WHOLE, own_cols)], lsem.at[2]),
        pltpu.make_async_copy(ain_hbm, ain, lsem.at[3]),
        pltpu.make_async_copy(frz_hbm, frz, lsem.at[4]),
    ]
    for load in loads:
        load.start()

    near_masks = [(m, f) for f in (0, 1) for m in range(4) if m or f]
    far_masks = [4 * m for m in range(1, groups // 4)]
    barrier = pltpu.get_barrier_semaphore()
    for m, f in near_masks + [(m, 0) for m in far_masks]:
        pl.semaphore_signal(barrier, inc=1, device_id=peer(m, f), device_id_type=MESH)
    pl.semaphore_wait(barrier, len(near_masks) + len(far_masks))

    def q_at(q, base=0, piece=None):
        if piece is None:
            return pl.ds(pl.multiple_of(base + q * quarter, quarter), quarter)
        size = quarter // 2
        return pl.ds(pl.multiple_of(base + q * quarter + piece * size, size), size)

    q0 = dp % 4
    q1 = q0 + 1 - 2 * bit[0]
    q2 = q0 + 2 - 4 * bit[1]
    q3 = q1 + 2 - 4 * bit[1]
    other = (1 - fs) * half
    pieces = (0, 1)

    def across(whole, own):
        return [
            send(own.at[:, q_at(q0, 0, i)], whole.at[:, q_at(q0, fs * half, i)], peer(0, 1))
            for i in pieces
        ]

    def pass_on(whole, q, i, mask):
        view = whole.at[:, q_at(q, other, i)]
        return send(view, view, peer(mask, 0))

    far_first = list(range(2, bits))[::-1]
    orders = (
        ["y", 1] + far_first + [0],
        ["y", 1] + far_first + [0],
        far_first + [1, "y", 0],
        far_first + ["y", 1, 0],
    )
    strips = len(orders)
    strip = half // strips
    pas_copy = [None] * strips
    pas_step = [0] * strips

    def pas_advance(*which):
        for s in which:
            if pas_copy[s] is not None:
                for copy in pas_copy[s]:
                    copy.wait_recv()
            done = orders[s][: pas_step[s]]
            pas_step[s] += 1
            if len(done) == len(orders[s]):
                continue
            now = orders[s][len(done)]
            index = tuple(WHOLE if b in done else bit[b] for b in reversed(range(bits)))
            device = peer(0, 1) if now == "y" else peer(2 ** now, 0)
            place = pl.multiple_of(fs * half + s * strip, strip)
            if not done:
                source = pas_hbm.at[:, s * strip : (s + 1) * strip]
                target = pas.at[index + (WHOLE, pl.ds(place, strip))]
                pas_copy[s] = [send(source, target, device)]
                continue
            places = [place]
            if "y" in done:
                places = [h * half + s * strip for h in (0, 1)]
            views = [pas.at[index + (WHOLE, pl.ds(p, strip))] for p in places]
            pas_copy[s] = [send(v, v, device) for v in views]

    pas_advance(0, 1, 2, 3)
    at_y = across(at, at_hbm)
    up_y = across(up, up_hbm)

    loads[2].wait()
    pas_advance(0, 1, 2, 3)

    nn = (((1,), (0,)), ((), ()))
    nt = (((1,), (1,)), ((), ()))

    def mm(left, right, dims):
        return lax.dot_general(left, right, dims, preferred_element_type=jnp.float32)

    loads[1].wait()
    loads[3].wait()
    latent = mm(ain[:, own_cols], at[:, own_cols], nt)

    def quarter_of(q):
        cols = q_at(q, other)
        return mm(ain[:, cols], at[:, cols], nt)

    at_x, at_c, up_x, up_c = [], [], [], []
    for i in pieces:
        at_y[i].wait_recv()
        at_x.append(pass_on(at, q0, i, 2))
        at_c.append(pass_on(at, q0, i, 1))
    pas_advance(0, 1, 3)
    for i in pieces:
        up_y[i].wait_recv()
        up_x.append(pass_on(up, q0, i, 2))
        up_c.append(pass_on(up, q0, i, 1))
    pas_advance(2)
    latent = latent + quarter_of(q0)
    for i in pieces:
        at_x[i].wait_recv()
        at_c.append(pass_on(at, q2, i, 1))
    latent = latent + quarter_of(q2)
    pas_advance(0)
    for copy in at_c[:2]:
        copy.wait_recv()
    latent = latent + quarter_of(q1)
    for copy in at_c[2:]:
        copy.wait_recv()
    latent = latent + quarter_of(q3)
    code = latent.astype(jnp.bfloat16)
    code_t = code.astype(jnp.float32).T.astype(jnp.bfloat16)
    loads[0].wait()
    loads[4].wait()

    chunks = width // chunk
    lanes = 128

    def cols_of(j):
        if isinstance(j, int):
            return slice(j * chunk, (j + 1) * chunk)
        return pl.ds(pl.multiple_of(j * chunk, chunk), chunk)

    def fold(x):
        total = x[:, :lanes]
        for at in range(lanes, chunk, lanes):
            total = total + x[:, at : at + lanes]
        return total

    def forward(j, total):
        cols = cols_of(j)
        added = mm(code, up[:, cols], nn)
        sums = []
        for at in range(0, tokens, LEN):
            rows_at = slice(at, at + LEN)
            value = frz[rows_at, cols].astype(jnp.float32) + adapter_scale_factor * added[rows_at]
            hid[rows_at, cols] = value
            sums.append(fold(value * value))
        return total + jnp.concatenate(sums, axis=0)

    def loop(body, init, unroll=2):
        return lax.fori_loop(0, chunks, body, init, unroll=unroll)

    def of_query(q):
        return slice(q * LEN, (q + 1) * LEN)

    def forward_part(start, count, total):
        return lax.fori_loop(0, count, lambda j, t: forward(start + j, t), total, unroll=2)

    part_size = chunks // 4
    total = jnp.zeros((tokens, lanes), jnp.float32)
    total = forward_part(fs * (chunks // 2), part_size, total)
    for i in pieces:
        up_x[i].wait_recv()
        up_c.append(pass_on(up, q2, i, 1))
    total = forward_part(fs * (chunks // 2) + part_size, part_size, total)
    pas_advance(1, 3, 2)
    for copy in up_c:
        copy.wait_recv()
    total = forward_part((1 - fs) * (chunks // 2), 2 * part_size, total)
    inv_rms = lax.rsqrt(jnp.sum(total, axis=1, keepdims=True) / width + norm_eps)

    pas_advance(0, 1, 2, 3)

    def pool(j, total):
        cols = cols_of(j)
        each = [
            jnp.sum(hid[of_query(q), cols] * inv_rms[of_query(q)], axis=0, keepdims=True)
            for q in range(queries)
        ]
        value = jnp.concatenate(each, axis=0) * (gain_ref[:, cols] * (1.0 / LEN))
        pooled[:, cols] = value
        return total + fold(value * value)

    total = loop(pool, jnp.zeros((queries, lanes), jnp.float32))
    length = jnp.sqrt(jnp.sum(total, axis=1, keepdims=True))
    inv_length = 1.0 / length

    def meet(j, totals):
        meets, squares = totals
        cols = cols_of(j)
        value = jnp.concatenate(
            [pas[block(k) + (WHOLE, cols)].astype(jnp.float32) for k in range(groups)], axis=0
        )
        narrow = value.astype(jnp.bfloat16)
        pasm[:, cols] = narrow
        gained = (hid[:, cols] * gain_ref[:, cols]).astype(jnp.bfloat16)
        return meets + mm(gained, narrow, nt), squares + fold(value * value)

    totals = jnp.zeros((tokens, pairs), jnp.float32), jnp.zeros((pairs, lanes), jnp.float32)
    for s in range(strips):
        pas_advance(s)
        for h, n in itertools.product((0, 1), range(strip // chunk)):
            totals = meet((h * half + s * strip) // chunk + n, totals)
    meets, squares = totals
    squares = jnp.broadcast_to(jnp.sum(squares, axis=1, keepdims=True), (pairs, lanes))
    inv_norm = 1.0 / jnp.sqrt(squares.T[0:1, :])
    met = meets * inv_norm
    scores = jnp.concatenate(
        [
            jnp.sum(met[of_query(q)] * inv_rms[of_query(q)], axis=0, keepdims=True)
            for q in range(queries)
        ],
        axis=0,
    ) * (inv_length * (inv_temp / LEN))
    expo = jnp.exp(scores - inv_temp)
    row_sum = jnp.sum(expo, axis=1, keepdims=True)
    row_at = lax.broadcasted_iota(jnp.int32, (queries, pairs), 0)
    col_at = lax.broadcasted_iota(jnp.int32, (queries, pairs), 1)
    onehot = jnp.zeros((queries, pairs), jnp.float32)
    for q in range(queries):
        hit = jnp.where(col_at == pos_ref[fs * queries + q], 1.0, 0.0)
        onehot = onehot + jnp.where(row_at == q, hit, 0.0)
    term = jnp.log(jnp.broadcast_to(row_sum, (queries, pairs))) * (1.0 / pairs)
    term = jnp.sum(term - 2.0 * scores * onehot, axis=0, keepdims=True)
    at8 = lax.broadcasted_iota(jnp.int32, (8, pairs), 0)
    col_part = jnp.broadcast_to(jnp.sum(expo, axis=0, keepdims=True), (8, pairs))
    payload = jnp.where(at8 == 0, col_part, jnp.where(at8 == 1, term, 0.0))

    slot = fs * 4 + q0
    near[slot] = payload
    copies = [send(near.at[slot], near.at[slot], peer(m, f)) for m, f in near_masks]

    def own_side(j, totals):
        totals, hidden_up = totals
        cols = cols_of(j)
        value = pooled[:, cols] * gain_ref[:, cols]
        hidden_up = hidden_up + mm(hid[:, cols].astype(jnp.bfloat16), up[:, cols], nt)
        return tuple(
            totals[q] + fold(hid[of_query(q), cols] * value[q : q + 1]) for q in range(queries)
        ), hidden_up

    own, hidden_up = loop(
        own_side,
        (
            tuple(jnp.zeros((LEN, lanes), jnp.float32) for _ in range(queries)),
            jnp.zeros((tokens, rank), jnp.float32),
        ),
    )
    own = [
        jnp.sum(own[q], axis=1, keepdims=True) * inv_length[q : q + 1] for q in range(queries)
    ]
    for copy in copies:
        copy.wait_recv()
    summed = near[0]
    for k in range(1, 8):
        summed = summed + near[k]
    slot = dp // 4
    far[slot] = summed
    copies = [send(far.at[slot], far.at[slot], peer(m, 0)) for m in far_masks]
    for copy in copies:
        copy.wait_recv()
    summed = far[0]
    for k in range(1, groups // 4):
        summed = summed + far[k]
    col_sum = summed[0:1]
    weights = 0.5 * (expo / row_sum + expo / col_sum) - onehot
    weights = weights.astype(jnp.bfloat16).astype(jnp.float32)
    along = jnp.sum(weights * scores, axis=1, keepdims=True)
    shrink = inv_length * (1.0 / LEN)
    back = []
    for q in range(queries):
        across = inv_temp * jnp.sum(met[of_query(q)] * weights[q : q + 1], axis=1, keepdims=True)
        mean = (across - own[q] * along[q : q + 1]) * shrink[q : q + 1] / width
        back.append(inv_rms[of_query(q)] ** 3 * mean)
    weights = weights * (inv_norm * inv_temp)
    high = weights.astype(jnp.bfloat16).astype(jnp.float32)
    both = jnp.concatenate([high, weights - high], axis=0).astype(jnp.bfloat16)
    inward = inv_length * along

    def query_side(j, total):
        cols = cols_of(j)
        two = mm(both, pasm[:, cols], nn)
        value = two[:queries] + two[queries:] - pooled[:, cols] * inward
        value = value * shrink * gain_ref[:, cols]
        scaled[:, cols] = value
        return total + mm(value.astype(jnp.bfloat16), up[:, cols], nt)

    def hidden_side(j, _):
        cols = cols_of(j)
        value = jnp.concatenate(
            [
                inv_rms[of_query(q)] * scaled[q : q + 1, cols] - hid[of_query(q), cols] * back[q]
                for q in range(queries)
            ],
            axis=0,
        ).astype(jnp.bfloat16)
        put(1, j, adapter_scale_factor * mm(code_t, value, nn))
        return 0

    def put(g, j, grad):
        grad = grad.astype(jnp.bfloat16)
        for n, (y, h) in enumerate(itertools.product((0, 1), repeat=2)):
            part[block(j) + (g, y, h)] = grad[n * rank // 4 : (n + 1) * rank // 4]

    def sided(body, side, init):
        def of(i, carry):
            return body(2 * i + side, carry)

        return lax.fori_loop(0, chunks // 2, of, init, unroll=2)

    theirs, ours = 1 - bit[0], bit[0]
    query_up = loop(query_side, jnp.zeros((queries, rank), jnp.float32), 4)
    code_grad = jnp.concatenate(
        [
            inv_rms[of_query(q)] * query_up[q : q + 1] - hidden_up[of_query(q)] * back[q]
            for q in range(queries)
        ],
        axis=0,
    )
    code_grad_t = (adapter_scale_factor * code_grad).astype(jnp.bfloat16)
    code_grad_t = code_grad_t.astype(jnp.float32).T.astype(jnp.bfloat16)

    def input_side(j, _):
        put(0, j, mm(code_grad_t, ain[:, cols_of(j)], nn))
        return 0

    chains = grad_chains(bits)
    grad_copies = [None] * len(chains)
    steps = len(chains[0][2])
    rx_of = iter(rx)
    rx_at = [[[next(rx_of) for _ in hop_masks(hop)] for hop in order] for _, _, order in chains]

    def view(n, k, mask):
        g, h, order = chains[n]
        fixed = [axis for hop in order[: k + 1] for axis in hop]
        flip = [axis for i, axis in enumerate(order[k]) if (mask >> i) & 1]
        index = ()
        for b in reversed(range(bits)):
            index += ((1 - bit[b] if b in flip else bit[b]) if b in fixed else WHOLE,)
        y = (1 - fs if "y" in flip else fs) if "y" in fixed else WHOLE
        return index + (g, y, h)

    def grad_send(n, k):
        hop = chains[n][2][k]
        grad_copies[n] = []
        for mask in hop_masks(hop):
            flip = [axis for i, axis in enumerate(hop) if (mask >> i) & 1]
            device = peer(sum(2 ** axis for axis in flip if axis != "y"), "y" in flip)
            source = part.at[view(n, k, mask)]
            grad_copies[n].append(send(source, rx_at[n][k][mask - 1], device))

    def grad_add(n, k):
        g, h, order = chains[n]
        kept = view(n, k, 0)
        for copy in grad_copies[n]:
            copy.wait_recv()
        free = [at for at, i in enumerate(kept) if isinstance(i, slice)]
        for picks in itertools.product((0, 1), repeat=len(free)):
            index = list(kept)
            for at_dim, pick in zip(free, picks):
                index[at_dim] = pick
            index = tuple(index)
            value = part[index].astype(jnp.float32)
            for buffer in rx_at[n][k]:
                value = value + buffer[picks].astype(jnp.float32)
            if k == len(order) - 1:
                out_ref[g, h * rank // 4 : (h + 1) * rank // 4] = value
            else:
                part[index] = value.astype(jnp.bfloat16)

    early = [n for n, c in enumerate(chains) if c[0] == 0]
    late = [n for n, c in enumerate(chains) if c[0] == 1]
    sided(input_side, theirs, 0)
    for n in early:
        grad_send(n, 0)
    sided(hidden_side, theirs, 0)
    for n in late:
        grad_send(n, 0)
    sided(input_side, ours, 0)
    for n in early:
        grad_add(n, 0)
        grad_send(n, 1)
    sided(hidden_side, ours, 0)
    for n in late:
        grad_add(n, 0)
        grad_send(n, 1)
    loss_ref[0, 0] = (
        jnp.sum(jnp.log(col_sum) + summed[1:2]) / (2.0 * pairs) + inv_temp
    )
    for k in range(1, steps):
        for n in early + late:
            grad_add(n, k)
            if k + 1 < steps:
                grad_send(n, k + 1)
    for copy in started:
        copy.wait_send()


def hop_masks(hop):
    return range(1, 2 ** len(hop))


def grad_chains(bits):
    last = tuple(range(2, bits))
    return [
        (1, 0, [(0,), (1,), ("y",), last]),
        (1, 1, [(0,), (2,), (1, "y"), last[1:]]),
        (0, 0, [(0,), ("y",), (1,), last]),
        (0, 1, [(0,), (2,), (1, "y"), last[1:]]),
    ]


def grad_shapes(bits, rank, chunk):
    shapes = []
    for _, _, order in grad_chains(bits):
        for k, hop in enumerate(order):
            fixed = sum(len(each) for each in order[: k + 1])
            shape = (2,) * (bits + 1 - fixed) + (rank // 4, chunk)
            shapes += [pltpu.VMEM(shape, jnp.bfloat16) for _ in hop_masks(hop)]
    return shapes


def fused_shards(bits, adapter_in, frozen, gain, adapter_a, adapter_up_matrix, passages, positive):
    tokens, width = adapter_in.shape
    rank = adapter_a.shape[1]
    queries = tokens // LEN
    rows = passages.shape[0]
    groups = 2 ** bits
    chunk = width // groups
    pairs = groups * rows
    half = width // 2
    bf16, f32 = jnp.bfloat16, jnp.float32
    rx = grad_shapes(bits, rank, chunk)
    copies = 96
    vmem = pl.BlockSpec(memory_space=pltpu.VMEM)
    smem = pl.BlockSpec(memory_space=pltpu.SMEM)
    hbm = pl.BlockSpec(memory_space=pl.ANY)
    grads, loss = pl.pallas_call(
        functools.partial(fused, bits, (tokens, width, rank, queries, rows, chunk)),
        out_shape=(
            jax.ShapeDtypeStruct((2, rank // 2, chunk), f32),
            jax.ShapeDtypeStruct((1, 1), f32),
        ),
        in_specs=[smem, vmem, hbm, hbm, hbm, hbm, hbm],
        out_specs=(vmem, smem),
        scratch_shapes=[
            pltpu.VMEM((tokens, width), bf16),
            pltpu.VMEM((tokens, width), bf16),
            pltpu.VMEM((rank, width), bf16),
            pltpu.VMEM((rank, width), bf16),
            pltpu.VMEM((2,) * bits + (rows, width), bf16),
            pltpu.VMEM((tokens, width), f32),
            pltpu.VMEM((pairs, width), bf16),
            pltpu.VMEM((2,) * bits + (2, 2, 2, rank // 4, chunk), bf16),
            pltpu.VMEM((queries, width), f32),
            pltpu.VMEM((queries, width), f32),
            pltpu.VMEM((8, 8, pairs), f32),
            pltpu.VMEM((groups // 4, 8, pairs), f32),
            rx,
            pltpu.SemaphoreType.DMA((5,)),
            pltpu.SemaphoreType.DMA((copies,)),
            pltpu.SemaphoreType.DMA((copies,)),
        ],
        compiler_params=pltpu.CompilerParams(
            collective_id=0, has_side_effects=True, vmem_limit_bytes=56 * 2 ** 20
        ),
    )(positive, gain.reshape(1, width), adapter_in, frozen, adapter_a.T, adapter_up_matrix, passages)
    return grads, loss.reshape(())


def solution(mesh):
    placed = (
        P(("dp", "fsdp"), None),
        P(("dp", "fsdp"), None),
        P(),
        P("fsdp", None),
        P(None, "fsdp"),
        P("dp", "fsdp"),
        P("dp"),
    )
    groups = mesh.shape["dp"]
    bits = groups.bit_length() - 1
    body = shards
    if mesh.shape["fsdp"] == 2 and groups == 16:
        body = functools.partial(fused_shards, bits)
    return jax.shard_map(
        body, mesh=mesh, in_specs=placed, out_specs=(P(None, "fsdp", "dp"), P()), check_vma=False
    )
```

```python
import functools
import itertools

import jax
import jax.numpy as jnp
from jax import lax
from jax.experimental import pallas as pl
from jax.experimental.pallas import tpu as pltpu
from jax.sharding import PartitionSpec as P

LEN = 32


adapter_scale_factor = 0.25
inv_temp = 20.0
norm_eps = 1e-05


def contracted_row_product(left, right):
    return lax.dot_general(
        left, right, (((1,), (1,)), ((), ())), preferred_element_type=jnp.float32
    )


def shards(adapter_in, frozen, gain, adapter_a, adapter_up_matrix, passages, positive):
    whole_a, full_up_matrix = (
        lax.all_gather(adapter_a, "fsdp", axis=0, tiled=True),
        lax.all_gather(adapter_up_matrix, "fsdp", axis=1, tiled=True),
    )
    width = whole_a.shape[0]
    queries = adapter_in.shape[0] // LEN
    latent_code = jnp.dot(adapter_in, whole_a, preferred_element_type=jnp.float32).astype(
        jnp.bfloat16
    )
    hidden_state = frozen.astype(jnp.float32) + adapter_scale_factor * jnp.dot(
        latent_code, full_up_matrix, preferred_element_type=jnp.float32
    )
    inv_rms = lax.rsqrt(jnp.mean(hidden_state * hidden_state, axis=-1, keepdims=True) + norm_eps)
    normed = hidden_state * inv_rms * gain
    pooled = jnp.mean(normed.reshape(queries, LEN, width), axis=1)
    length = jnp.sqrt(jnp.sum(pooled * pooled, axis=-1, keepdims=True))
    unit = pooled / length
    query_feat = lax.all_to_all(
        unit.astype(jnp.bfloat16), "fsdp", split_axis=1, concat_axis=0, tiled=True
    )
    pas = passages.astype(jnp.float32)
    squares = lax.psum(jnp.sum(pas * pas, axis=-1), "fsdp")
    passage_unit = (pas / jnp.sqrt(squares)[:, None]).astype(jnp.bfloat16)
    total_pairs = passage_unit.shape[0] * lax.axis_size("dp")
    columns = jnp.arange(total_pairs, dtype=jnp.int32)
    partial_value = contracted_row_product(
        query_feat, lax.all_gather(passage_unit, "dp", axis=0, tiled=True)
    )
    scores = inv_temp * lax.psum_scatter(partial_value, "fsdp", scatter_dimension=0, tiled=True)
    own_pos = lax.dynamic_slice_in_dim(positive, lax.axis_index("fsdp") * queries, queries, 0)
    expo = jnp.exp(scores - inv_temp)
    row_sum = jnp.sum(expo, axis=1)
    onehot = (own_pos[:, None] == columns[None, :]).astype(jnp.float32)
    local_term = jnp.sum(jnp.log(row_sum)) - 2.0 * jnp.sum(scores * onehot)
    col_sum, summed = lax.psum((jnp.sum(expo, axis=0), local_term), ("dp", "fsdp"))
    loss = (summed + jnp.sum(jnp.log(col_sum))) / (2.0 * total_pairs) + inv_temp
    weights = (0.5 * (expo / row_sum[:, None] + expo / col_sum[None, :]) - onehot).astype(
        jnp.bfloat16
    )
    group_weights = lax.all_gather(weights, "fsdp", axis=0, tiled=True)
    grad_feat = jnp.dot(
        group_weights,
        lax.all_gather(passage_unit, "dp", axis=0, tiled=True),
        preferred_element_type=jnp.float32,
    )
    query_grad = lax.all_to_all(
        inv_temp * grad_feat, "fsdp", split_axis=0, concat_axis=1, tiled=True
    )
    pooled_grad = (query_grad - unit * jnp.sum(unit * query_grad, axis=-1, keepdims=True)) / length
    normed_grad = jnp.repeat(pooled_grad / LEN, LEN, axis=0)
    scaled = normed_grad * gain
    hidden_state_gradient = (
        inv_rms * scaled
        - hidden_state * inv_rms**3 * jnp.mean(scaled * hidden_state, axis=-1, keepdims=True)
    ).astype(jnp.bfloat16)
    latent_code_gradient = (
        adapter_scale_factor * contracted_row_product(hidden_state_gradient, full_up_matrix)
    ).astype(jnp.bfloat16)
    grad_a_t = jnp.dot(latent_code_gradient.T, adapter_in, preferred_element_type=jnp.float32)
    up_matrix_gradient = adapter_scale_factor * jnp.dot(
        latent_code.T, hidden_state_gradient, preferred_element_type=jnp.float32
    )
    stacked = jnp.stack([grad_a_t, up_matrix_gradient])
    group_sum = lax.psum_scatter(
        stacked.astype(jnp.bfloat16), "fsdp", scatter_dimension=1, tiled=True
    ).astype(jnp.float32)
    adapter_grads = lax.psum_scatter(group_sum, "dp", scatter_dimension=2, tiled=True)
    return (adapter_grads, loss)


WHOLE = slice(None)
MESH = pl.DeviceIdType.MESH


def fused(
    bits, sizes,
    pos_ref, gain_ref, ain_hbm, frz_hbm, at_hbm, up_hbm, pas_hbm,
    out_ref, loss_ref,
    ain, frz, at, up, pas, hid, pasm, part,
    pooled, scaled, near, far, rx,
    lsem, ssem, rsem,
):
    tokens, width, rank, queries, rows, chunk = sizes
    half = width // 2
    quarter = half // 4
    dp, fs = lax.axis_index("dp"), lax.axis_index("fsdp")
    groups = 2 ** bits
    pairs = groups * rows
    bit = [(dp // 2 ** b) % 2 for b in range(bits)]

    def peer(mask, flip):
        there = dp
        for b in range(bits):
            if (mask >> b) & 1:
                there = there + (1 - 2 * bit[b]) * 2 ** b
        return (there, 1 - fs if flip else fs)

    def remote(src, dst, k, device):
        return pltpu.make_async_remote_copy(
            src_ref=src, dst_ref=dst, send_sem=ssem.at[k], recv_sem=rsem.at[k],
            device_id=device, device_id_type=MESH,
        )

    started = []

    def send(src, dst, device):
        copy = remote(src, dst, len(started), device)
        copy.start()
        started.append(copy)
        return copy

    def block(number):
        return tuple((number // 2 ** b) % 2 for b in reversed(range(bits)))

    own_cols = pl.ds(pl.multiple_of(fs * half, half), half)
    mine = tuple(reversed(bit))
    loads = [
        pltpu.make_async_copy(up_hbm, up.at[:, own_cols], lsem.at[0]),
        pltpu.make_async_copy(at_hbm, at.at[:, own_cols], lsem.at[1]),
        pltpu.make_async_copy(pas_hbm, pas.at[mine + (WHOLE, own_cols)], lsem.at[2]),
        pltpu.make_async_copy(ain_hbm, ain, lsem.at[3]),
        pltpu.make_async_copy(frz_hbm, frz, lsem.at[4]),
    ]
    for load in loads:
        load.start()

    near_masks = [(m, f) for f in (0, 1) for m in range(4) if m or f]
    far_masks = [4 * m for m in range(1, groups // 4)]
    barrier = pltpu.get_barrier_semaphore()
    for m, f in near_masks + [(m, 0) for m in far_masks]:
        pl.semaphore_signal(barrier, inc=1, device_id=peer(m, f), device_id_type=MESH)
    pl.semaphore_wait(barrier, len(near_masks) + len(far_masks))

    def q_at(q, base=0, piece=None):
        if piece is None:
            return pl.ds(pl.multiple_of(base + q * quarter, quarter), quarter)
        size = quarter // 2
        return pl.ds(pl.multiple_of(base + q * quarter + piece * size, size), size)

    q0 = dp % 4
    q1 = q0 + 1 - 2 * bit[0]
    q2 = q0 + 2 - 4 * bit[1]
    q3 = q1 + 2 - 4 * bit[1]
    other = (1 - fs) * half
    pieces = (0, 1)

    def across(whole, own):
        return [
            send(own.at[:, q_at(q0, 0, i)], whole.at[:, q_at(q0, fs * half, i)], peer(0, 1))
            for i in pieces
        ]

    def pass_on(whole, q, i, mask):
        view = whole.at[:, q_at(q, other, i)]
        return send(view, view, peer(mask, 0))

    far_first = tuple(range(2, bits))[::-1]
    apart = [(b,) for b in far_first]
    orders = (
        [("y", 1)] + apart + [(0,)],
        [("y", 1)] + apart + [(0,)],
        [far_first, (1,), ("y",), (0,)],
        [far_first, ("y",), (1,), (0,)],
    )
    strips = len(orders)
    strip = half // strips
    pas_copy = [None] * strips
    pas_step = [0] * strips

    def pas_advance(*which):
        for s in which:
            if pas_copy[s] is not None:
                for copy in pas_copy[s]:
                    copy.wait_recv()
            hops = orders[s][: pas_step[s]]
            pas_step[s] += 1
            if len(hops) == len(orders[s]):
                continue
            done = [axis for hop in hops for axis in hop]
            hop = orders[s][len(hops)]
            index = tuple(WHOLE if b in done else bit[b] for b in reversed(range(bits)))
            place = pl.multiple_of(fs * half + s * strip, strip)
            places = [h * half + s * strip for h in (0, 1)] if "y" in done else [place]
            pas_copy[s] = []
            for mask in hop_masks(hop):
                flip = [axis for i, axis in enumerate(hop) if (mask >> i) & 1]
                device = peer(sum(2 ** axis for axis in flip if axis != "y"), "y" in flip)
                for p in places:
                    target = pas.at[index + (WHOLE, pl.ds(p, strip))]
                    source = target if done else pas_hbm.at[:, s * strip : (s + 1) * strip]
                    pas_copy[s].append(send(source, target, device))

    pas_advance(0, 1, 2, 3)
    at_y = across(at, at_hbm)
    up_y = across(up, up_hbm)

    loads[2].wait()
    pas_advance(0, 1)

    nn = (((1,), (0,)), ((), ()))
    nt = (((1,), (1,)), ((), ()))

    def mm(left, right, dims):
        return lax.dot_general(left, right, dims, preferred_element_type=jnp.float32)

    loads[1].wait()
    loads[3].wait()
    latent = mm(ain[:, own_cols], at[:, own_cols], nt)

    def quarter_of(q):
        cols = q_at(q, other)
        return mm(ain[:, cols], at[:, cols], nt)

    at_x, at_c, up_x, up_c = [], [], [], []
    for i in pieces:
        at_y[i].wait_recv()
        at_x.append(pass_on(at, q0, i, 2))
        at_c.append(pass_on(at, q0, i, 1))
    pas_advance(3)
    for i in pieces:
        up_y[i].wait_recv()
        up_x.append(pass_on(up, q0, i, 2))
        up_c.append(pass_on(up, q0, i, 1))
    pas_advance(2, 0)
    latent = latent + quarter_of(q0)
    for i in pieces:
        at_x[i].wait_recv()
        at_c.append(pass_on(at, q2, i, 1))
    latent = latent + quarter_of(q2)
    pas_advance(1)
    for copy in at_c[:2]:
        copy.wait_recv()
    latent = latent + quarter_of(q1)
    for copy in at_c[2:]:
        copy.wait_recv()
    latent = latent + quarter_of(q3)
    code = latent.astype(jnp.bfloat16)
    code_t = code.astype(jnp.float32).T.astype(jnp.bfloat16)
    loads[0].wait()
    loads[4].wait()

    chunks = width // chunk
    lanes = 128

    def cols_of(j):
        if isinstance(j, int):
            return slice(j * chunk, (j + 1) * chunk)
        return pl.ds(pl.multiple_of(j * chunk, chunk), chunk)

    def fold(x):
        total = x[:, :lanes]
        for at in range(lanes, chunk, lanes):
            total = total + x[:, at : at + lanes]
        return total

    def forward(j, total):
        cols = cols_of(j)
        added = mm(code, up[:, cols], nn)
        sums = []
        for at in range(0, tokens, LEN):
            rows_at = slice(at, at + LEN)
            value = frz[rows_at, cols].astype(jnp.float32) + adapter_scale_factor * added[rows_at]
            hid[rows_at, cols] = value
            sums.append(fold(value * value))
        return total + jnp.concatenate(sums, axis=0)

    def loop(body, init, unroll=2):
        return lax.fori_loop(0, chunks, body, init, unroll=unroll)

    def of_query(q):
        return slice(q * LEN, (q + 1) * LEN)

    def forward_part(start, count, total):
        return lax.fori_loop(0, count, lambda j, t: forward(start + j, t), total, unroll=2)

    part_size = chunks // 4
    total = jnp.zeros((tokens, lanes), jnp.float32)
    total = forward_part(fs * (chunks // 2), part_size, total)
    for i in pieces:
        up_x[i].wait_recv()
        up_c.append(pass_on(up, q2, i, 1))
    total = forward_part(fs * (chunks // 2) + part_size, part_size, total)
    pas_advance(3, 2)
    for copy in up_c:
        copy.wait_recv()
    total = forward_part((1 - fs) * (chunks // 2), 2 * part_size, total)
    inv_rms = lax.rsqrt(jnp.sum(total, axis=1, keepdims=True) / width + norm_eps)

    pas_advance(0, 1, 2, 3)

    def pool(j, total):
        cols = cols_of(j)
        each = [
            jnp.sum(hid[of_query(q), cols] * inv_rms[of_query(q)], axis=0, keepdims=True)
            for q in range(queries)
        ]
        value = jnp.concatenate(each, axis=0) * (gain_ref[:, cols] * (1.0 / LEN))
        pooled[:, cols] = value
        return total + fold(value * value)

    total = loop(pool, jnp.zeros((queries, lanes), jnp.float32))
    length = jnp.sqrt(jnp.sum(total, axis=1, keepdims=True))
    inv_length = 1.0 / length

    def meet(j, totals):
        meets, squares = totals
        cols = cols_of(j)
        value = jnp.concatenate(
            [pas[block(k) + (WHOLE, cols)].astype(jnp.float32) for k in range(groups)], axis=0
        )
        narrow = value.astype(jnp.bfloat16)
        pasm[:, cols] = narrow
        gained = (hid[:, cols] * gain_ref[:, cols]).astype(jnp.bfloat16)
        return meets + mm(gained, narrow, nt), squares + fold(value * value)

    totals = jnp.zeros((tokens, pairs), jnp.float32), jnp.zeros((pairs, lanes), jnp.float32)
    for s in range(strips):
        pas_advance(s)
        for h, n in itertools.product((0, 1), range(strip // chunk)):
            totals = meet((h * half + s * strip) // chunk + n, totals)
    meets, squares = totals
    squares = jnp.broadcast_to(jnp.sum(squares, axis=1, keepdims=True), (pairs, lanes))
    inv_norm = 1.0 / jnp.sqrt(squares.T[0:1, :])
    met = meets * inv_norm
    scores = jnp.concatenate(
        [
            jnp.sum(met[of_query(q)] * inv_rms[of_query(q)], axis=0, keepdims=True)
            for q in range(queries)
        ],
        axis=0,
    ) * (inv_length * (inv_temp / LEN))
    expo = jnp.exp(scores - inv_temp)
    row_sum = jnp.sum(expo, axis=1, keepdims=True)
    row_at = lax.broadcasted_iota(jnp.int32, (queries, pairs), 0)
    col_at = lax.broadcasted_iota(jnp.int32, (queries, pairs), 1)
    onehot = jnp.zeros((queries, pairs), jnp.float32)
    for q in range(queries):
        hit = jnp.where(col_at == pos_ref[fs * queries + q], 1.0, 0.0)
        onehot = onehot + jnp.where(row_at == q, hit, 0.0)
    term = jnp.log(jnp.broadcast_to(row_sum, (queries, pairs))) * (1.0 / pairs)
    term = jnp.sum(term - 2.0 * scores * onehot, axis=0, keepdims=True)
    at8 = lax.broadcasted_iota(jnp.int32, (8, pairs), 0)
    col_part = jnp.broadcast_to(jnp.sum(expo, axis=0, keepdims=True), (8, pairs))
    payload = jnp.where(at8 == 0, col_part, jnp.where(at8 == 1, term, 0.0))

    slot = fs * 4 + q0
    near[slot] = payload
    copies = [send(near.at[slot], near.at[slot], peer(m, f)) for m, f in near_masks]

    def own_side(j, totals):
        totals, hidden_up = totals
        cols = cols_of(j)
        value = pooled[:, cols] * gain_ref[:, cols]
        hidden_up = hidden_up + mm(hid[:, cols].astype(jnp.bfloat16), up[:, cols], nt)
        return tuple(
            totals[q] + fold(hid[of_query(q), cols] * value[q : q + 1]) for q in range(queries)
        ), hidden_up

    own, hidden_up = loop(
        own_side,
        (
            tuple(jnp.zeros((LEN, lanes), jnp.float32) for _ in range(queries)),
            jnp.zeros((tokens, rank), jnp.float32),
        ),
    )
    own = [
        jnp.sum(own[q], axis=1, keepdims=True) * inv_length[q : q + 1] for q in range(queries)
    ]
    for copy in copies:
        copy.wait_recv()
    summed = near[0]
    for k in range(1, 8):
        summed = summed + near[k]
    slot = dp // 4
    far[slot] = summed
    copies = [send(far.at[slot], far.at[slot], peer(m, 0)) for m in far_masks]
    for copy in copies:
        copy.wait_recv()
    summed = far[0]
    for k in range(1, groups // 4):
        summed = summed + far[k]
    col_sum = summed[0:1]
    weights = 0.5 * (expo / row_sum + expo / col_sum) - onehot
    weights = weights.astype(jnp.bfloat16).astype(jnp.float32)
    along = jnp.sum(weights * scores, axis=1, keepdims=True)
    shrink = inv_length * (1.0 / LEN)
    back = []
    for q in range(queries):
        across = inv_temp * jnp.sum(met[of_query(q)] * weights[q : q + 1], axis=1, keepdims=True)
        mean = (across - own[q] * along[q : q + 1]) * shrink[q : q + 1] / width
        back.append(inv_rms[of_query(q)] ** 3 * mean)
    weights = weights * (inv_norm * inv_temp)
    high = weights.astype(jnp.bfloat16).astype(jnp.float32)
    both = jnp.concatenate([high, weights - high], axis=0).astype(jnp.bfloat16)
    inward = inv_length * along

    def query_side(j, total):
        cols = cols_of(j)
        two = mm(both, pasm[:, cols], nn)
        value = two[:queries] + two[queries:] - pooled[:, cols] * inward
        value = value * shrink * gain_ref[:, cols]
        scaled[:, cols] = value
        return total + mm(value.astype(jnp.bfloat16), up[:, cols], nt)

    def hidden_side(j, _):
        cols = cols_of(j)
        value = jnp.concatenate(
            [
                inv_rms[of_query(q)] * scaled[q : q + 1, cols] - hid[of_query(q), cols] * back[q]
                for q in range(queries)
            ],
            axis=0,
        ).astype(jnp.bfloat16)
        put(1, j, adapter_scale_factor * mm(code_t, value, nn))
        return 0

    def put(g, j, grad):
        grad = grad.astype(jnp.bfloat16)
        for n, (y, h) in enumerate(itertools.product((0, 1), repeat=2)):
            part[block(j) + (g, y, h)] = grad[n * rank // 4 : (n + 1) * rank // 4]

    def sided(body, side, init):
        def of(i, carry):
            return body(2 * i + side, carry)

        return lax.fori_loop(0, chunks // 2, of, init, unroll=2)

    theirs, ours = 1 - bit[0], bit[0]
    query_up = loop(query_side, jnp.zeros((queries, rank), jnp.float32), 4)
    code_grad = jnp.concatenate(
        [
            inv_rms[of_query(q)] * query_up[q : q + 1] - hidden_up[of_query(q)] * back[q]
            for q in range(queries)
        ],
        axis=0,
    )
    code_grad_t = (adapter_scale_factor * code_grad).astype(jnp.bfloat16)
    code_grad_t = code_grad_t.astype(jnp.float32).T.astype(jnp.bfloat16)

    def input_side(j, _):
        put(0, j, mm(code_grad_t, ain[:, cols_of(j)], nn))
        return 0

    chains = grad_chains(bits)
    grad_copies = [None] * len(chains)
    steps = len(chains[0][2])
    rx_of = iter(rx)
    rx_at = [[[next(rx_of) for _ in hop_masks(hop)] for hop in order] for _, _, order in chains]

    def view(n, k, mask):
        g, h, order = chains[n]
        fixed = [axis for hop in order[: k + 1] for axis in hop]
        flip = [axis for i, axis in enumerate(order[k]) if (mask >> i) & 1]
        index = ()
        for b in reversed(range(bits)):
            index += ((1 - bit[b] if b in flip else bit[b]) if b in fixed else WHOLE,)
        y = (1 - fs if "y" in flip else fs) if "y" in fixed else WHOLE
        return index + (g, y, h)

    def grad_send(n, k):
        hop = chains[n][2][k]
        grad_copies[n] = []
        for mask in hop_masks(hop):
            flip = [axis for i, axis in enumerate(hop) if (mask >> i) & 1]
            device = peer(sum(2 ** axis for axis in flip if axis != "y"), "y" in flip)
            source = part.at[view(n, k, mask)]
            grad_copies[n].append(send(source, rx_at[n][k][mask - 1], device))

    def grad_add(n, k):
        g, h, order = chains[n]
        kept = view(n, k, 0)
        for copy in grad_copies[n]:
            copy.wait_recv()
        free = [at for at, i in enumerate(kept) if isinstance(i, slice)]
        for picks in itertools.product((0, 1), repeat=len(free)):
            index = list(kept)
            for at_dim, pick in zip(free, picks):
                index[at_dim] = pick
            index = tuple(index)
            value = part[index].astype(jnp.float32)
            for buffer in rx_at[n][k]:
                value = value + buffer[picks].astype(jnp.float32)
            if k == len(order) - 1:
                out_ref[g, h * rank // 4 : (h + 1) * rank // 4] = value
            else:
                part[index] = value.astype(jnp.bfloat16)

    early = [n for n, c in enumerate(chains) if c[0] == 0]
    late = [n for n, c in enumerate(chains) if c[0] == 1]
    sided(input_side, theirs, 0)
    for n in early:
        grad_send(n, 0)
    sided(hidden_side, theirs, 0)
    for n in late:
        grad_send(n, 0)
    sided(input_side, ours, 0)
    for n in early:
        grad_add(n, 0)
        grad_send(n, 1)
    sided(hidden_side, ours, 0)
    for n in late:
        grad_add(n, 0)
        grad_send(n, 1)
    loss_ref[0, 0] = (
        jnp.sum(jnp.log(col_sum) + summed[1:2]) / (2.0 * pairs) + inv_temp
    )
    for k in range(1, steps):
        for n in early + late:
            grad_add(n, k)
            if k + 1 < steps:
                grad_send(n, k + 1)
    for copy in started:
        copy.wait_send()


def hop_masks(hop):
    return range(1, 2 ** len(hop))


def grad_chains(bits):
    last = tuple(range(2, bits))
    return [
        (1, 0, [(0,), (1,), ("y",), last]),
        (1, 1, [(0,), (2,), (1, "y"), last[1:]]),
        (0, 0, [(0,), ("y",), (1,), last]),
        (0, 1, [(0,), (2,), (1, "y"), last[1:]]),
    ]


def grad_shapes(bits, rank, chunk):
    shapes = []
    for _, _, order in grad_chains(bits):
        for k, hop in enumerate(order):
            fixed = sum(len(each) for each in order[: k + 1])
            shape = (2,) * (bits + 1 - fixed) + (rank // 4, chunk)
            shapes += [pltpu.VMEM(shape, jnp.bfloat16) for _ in hop_masks(hop)]
    return shapes


def fused_shards(bits, adapter_in, frozen, gain, adapter_a, adapter_up_matrix, passages, positive):
    tokens, width = adapter_in.shape
    rank = adapter_a.shape[1]
    queries = tokens // LEN
    rows = passages.shape[0]
    groups = 2 ** bits
    chunk = width // groups
    pairs = groups * rows
    half = width // 2
    bf16, f32 = jnp.bfloat16, jnp.float32
    rx = grad_shapes(bits, rank, chunk)
    copies = 96
    vmem = pl.BlockSpec(memory_space=pltpu.VMEM)
    smem = pl.BlockSpec(memory_space=pltpu.SMEM)
    hbm = pl.BlockSpec(memory_space=pl.ANY)
    grads, loss = pl.pallas_call(
        functools.partial(fused, bits, (tokens, width, rank, queries, rows, chunk)),
        out_shape=(
            jax.ShapeDtypeStruct((2, rank // 2, chunk), f32),
            jax.ShapeDtypeStruct((1, 1), f32),
        ),
        in_specs=[smem, vmem, hbm, hbm, hbm, hbm, hbm],
        out_specs=(vmem, smem),
        scratch_shapes=[
            pltpu.VMEM((tokens, width), bf16),
            pltpu.VMEM((tokens, width), bf16),
            pltpu.VMEM((rank, width), bf16),
            pltpu.VMEM((rank, width), bf16),
            pltpu.VMEM((2,) * bits + (rows, width), bf16),
            pltpu.VMEM((tokens, width), f32),
            pltpu.VMEM((pairs, width), bf16),
            pltpu.VMEM((2,) * bits + (2, 2, 2, rank // 4, chunk), bf16),
            pltpu.VMEM((queries, width), f32),
            pltpu.VMEM((queries, width), f32),
            pltpu.VMEM((8, 8, pairs), f32),
            pltpu.VMEM((groups // 4, 8, pairs), f32),
            rx,
            pltpu.SemaphoreType.DMA((5,)),
            pltpu.SemaphoreType.DMA((copies,)),
            pltpu.SemaphoreType.DMA((copies,)),
        ],
        compiler_params=pltpu.CompilerParams(
            collective_id=0, has_side_effects=True, vmem_limit_bytes=56 * 2 ** 20
        ),
    )(positive, gain.reshape(1, width), adapter_in, frozen, adapter_a.T, adapter_up_matrix, passages)
    return grads, loss.reshape(())


def solution(mesh):
    placed = (
        P(("dp", "fsdp"), None),
        P(("dp", "fsdp"), None),
        P(),
        P("fsdp", None),
        P(None, "fsdp"),
        P("dp", "fsdp"),
        P("dp"),
    )
    groups = mesh.shape["dp"]
    bits = groups.bit_length() - 1
    body = shards
    if mesh.shape["fsdp"] == 2 and groups == 16:
        body = functools.partial(fused_shards, bits)
    return jax.shard_map(
        body, mesh=mesh, in_specs=placed, out_specs=(P(None, "fsdp", "dp"), P()), check_vma=False
    )
```

```python
import functools
import itertools

import jax
import jax.numpy as jnp
from jax import lax
from jax.experimental import pallas as pl
from jax.experimental.pallas import tpu as pltpu
from jax.sharding import PartitionSpec as P

LEN = 32


adapter_scale_factor = 0.25
inv_temp = 20.0
norm_eps = 1e-05


def contracted_row_product(left, right):
    return lax.dot_general(
        left, right, (((1,), (1,)), ((), ())), preferred_element_type=jnp.float32
    )


def shards(adapter_in, frozen, gain, adapter_a, adapter_up_matrix, passages, positive):
    whole_a, full_up_matrix = (
        lax.all_gather(adapter_a, "fsdp", axis=0, tiled=True),
        lax.all_gather(adapter_up_matrix, "fsdp", axis=1, tiled=True),
    )
    width = whole_a.shape[0]
    queries = adapter_in.shape[0] // LEN
    latent_code = jnp.dot(adapter_in, whole_a, preferred_element_type=jnp.float32).astype(
        jnp.bfloat16
    )
    hidden_state = frozen.astype(jnp.float32) + adapter_scale_factor * jnp.dot(
        latent_code, full_up_matrix, preferred_element_type=jnp.float32
    )
    inv_rms = lax.rsqrt(jnp.mean(hidden_state * hidden_state, axis=-1, keepdims=True) + norm_eps)
    normed = hidden_state * inv_rms * gain
    pooled = jnp.mean(normed.reshape(queries, LEN, width), axis=1)
    length = jnp.sqrt(jnp.sum(pooled * pooled, axis=-1, keepdims=True))
    unit = pooled / length
    query_feat = lax.all_to_all(
        unit.astype(jnp.bfloat16), "fsdp", split_axis=1, concat_axis=0, tiled=True
    )
    pas = passages.astype(jnp.float32)
    squares = lax.psum(jnp.sum(pas * pas, axis=-1), "fsdp")
    passage_unit = (pas / jnp.sqrt(squares)[:, None]).astype(jnp.bfloat16)
    total_pairs = passage_unit.shape[0] * lax.axis_size("dp")
    columns = jnp.arange(total_pairs, dtype=jnp.int32)
    partial_value = contracted_row_product(
        query_feat, lax.all_gather(passage_unit, "dp", axis=0, tiled=True)
    )
    scores = inv_temp * lax.psum_scatter(partial_value, "fsdp", scatter_dimension=0, tiled=True)
    own_pos = lax.dynamic_slice_in_dim(positive, lax.axis_index("fsdp") * queries, queries, 0)
    expo = jnp.exp(scores - inv_temp)
    row_sum = jnp.sum(expo, axis=1)
    onehot = (own_pos[:, None] == columns[None, :]).astype(jnp.float32)
    local_term = jnp.sum(jnp.log(row_sum)) - 2.0 * jnp.sum(scores * onehot)
    col_sum, summed = lax.psum((jnp.sum(expo, axis=0), local_term), ("dp", "fsdp"))
    loss = (summed + jnp.sum(jnp.log(col_sum))) / (2.0 * total_pairs) + inv_temp
    weights = (0.5 * (expo / row_sum[:, None] + expo / col_sum[None, :]) - onehot).astype(
        jnp.bfloat16
    )
    group_weights = lax.all_gather(weights, "fsdp", axis=0, tiled=True)
    grad_feat = jnp.dot(
        group_weights,
        lax.all_gather(passage_unit, "dp", axis=0, tiled=True),
        preferred_element_type=jnp.float32,
    )
    query_grad = lax.all_to_all(
        inv_temp * grad_feat, "fsdp", split_axis=0, concat_axis=1, tiled=True
    )
    pooled_grad = (query_grad - unit * jnp.sum(unit * query_grad, axis=-1, keepdims=True)) / length
    normed_grad = jnp.repeat(pooled_grad / LEN, LEN, axis=0)
    scaled = normed_grad * gain
    hidden_state_gradient = (
        inv_rms * scaled
        - hidden_state * inv_rms**3 * jnp.mean(scaled * hidden_state, axis=-1, keepdims=True)
    ).astype(jnp.bfloat16)
    latent_code_gradient = (
        adapter_scale_factor * contracted_row_product(hidden_state_gradient, full_up_matrix)
    ).astype(jnp.bfloat16)
    grad_a_t = jnp.dot(latent_code_gradient.T, adapter_in, preferred_element_type=jnp.float32)
    up_matrix_gradient = adapter_scale_factor * jnp.dot(
        latent_code.T, hidden_state_gradient, preferred_element_type=jnp.float32
    )
    stacked = jnp.stack([grad_a_t, up_matrix_gradient])
    group_sum = lax.psum_scatter(
        stacked.astype(jnp.bfloat16), "fsdp", scatter_dimension=1, tiled=True
    ).astype(jnp.float32)
    adapter_grads = lax.psum_scatter(group_sum, "dp", scatter_dimension=2, tiled=True)
    return (adapter_grads, loss)


WHOLE = slice(None)
MESH = pl.DeviceIdType.MESH


def fused(
    bits, sizes,
    pos_ref, gain_ref, ain_hbm, frz_hbm, at_hbm, up_hbm, pas_hbm,
    out_ref, loss_ref,
    ain, frz, at, up, pas, hid, pasm, part,
    pooled, scaled, near, far, rx,
    lsem, ssem, rsem,
):
    tokens, width, rank, queries, rows, chunk = sizes
    half = width // 2
    quarter = half // 4
    dp, fs = lax.axis_index("dp"), lax.axis_index("fsdp")
    groups = 2 ** bits
    pairs = groups * rows
    bit = [(dp // 2 ** b) % 2 for b in range(bits)]

    def peer(mask, flip):
        there = dp
        for b in range(bits):
            if (mask >> b) & 1:
                there = there + (1 - 2 * bit[b]) * 2 ** b
        return (there, 1 - fs if flip else fs)

    def remote(src, dst, k, device):
        return pltpu.make_async_remote_copy(
            src_ref=src, dst_ref=dst, send_sem=ssem.at[k], recv_sem=rsem.at[k],
            device_id=device, device_id_type=MESH,
        )

    started = []

    def send(src, dst, device):
        copy = remote(src, dst, len(started), device)
        copy.start()
        started.append(copy)
        return copy

    def block(number):
        return tuple((number // 2 ** b) % 2 for b in reversed(range(bits)))

    own_cols = pl.ds(pl.multiple_of(fs * half, half), half)
    mine = tuple(reversed(bit))
    loads = [
        pltpu.make_async_copy(up_hbm, up.at[:, own_cols], lsem.at[0]),
        pltpu.make_async_copy(at_hbm, at.at[:, own_cols], lsem.at[1]),
        pltpu.make_async_copy(pas_hbm, pas.at[mine + (WHOLE, own_cols)], lsem.at[2]),
        pltpu.make_async_copy(ain_hbm, ain, lsem.at[3]),
        pltpu.make_async_copy(frz_hbm, frz, lsem.at[4]),
    ]
    for load in loads:
        load.start()

    near_masks = [(m, f) for f in (0, 1) for m in range(4) if m or f]
    far_masks = [4 * m for m in range(1, groups // 4)]
    barrier = pltpu.get_barrier_semaphore()
    for m, f in near_masks + [(m, 0) for m in far_masks]:
        pl.semaphore_signal(barrier, inc=1, device_id=peer(m, f), device_id_type=MESH)
    pl.semaphore_wait(barrier, len(near_masks) + len(far_masks))

    def q_at(q, base=0, piece=None):
        if piece is None:
            return pl.ds(pl.multiple_of(base + q * quarter, quarter), quarter)
        size = quarter // 2
        return pl.ds(pl.multiple_of(base + q * quarter + piece * size, size), size)

    q0 = dp % 4
    q1 = q0 + 1 - 2 * bit[0]
    q2 = q0 + 2 - 4 * bit[1]
    q3 = q1 + 2 - 4 * bit[1]
    other = (1 - fs) * half
    pieces = (0, 1)

    def across(whole, own):
        return [
            send(own.at[:, q_at(q0, 0, i)], whole.at[:, q_at(q0, fs * half, i)], peer(0, 1))
            for i in pieces
        ]

    def pass_on(whole, q, i, mask):
        view = whole.at[:, q_at(q, other, i)]
        return send(view, view, peer(mask, 0))

    far_first = tuple(range(2, bits))[::-1]
    apart = [(b,) for b in far_first]
    orders = (
        [("y", 1)] + apart + [(0,)],
        [("y", 1)] + apart + [(0,)],
        apart + [(1,), ("y",), (0,)],
        apart + [("y",), (1,), (0,)],
    )
    strips = len(orders)
    strip = half // strips
    pas_copy = [None] * strips
    pas_step = [0] * strips

    def pas_advance(*which):
        for s in which:
            if pas_copy[s] is not None:
                for copy in pas_copy[s]:
                    copy.wait_recv()
            hops = orders[s][: pas_step[s]]
            pas_step[s] += 1
            if len(hops) == len(orders[s]):
                continue
            done = [axis for hop in hops for axis in hop]
            hop = orders[s][len(hops)]
            index = tuple(WHOLE if b in done else bit[b] for b in reversed(range(bits)))
            place = pl.multiple_of(fs * half + s * strip, strip)
            places = [h * half + s * strip for h in (0, 1)] if "y" in done else [place]
            pas_copy[s] = []
            for mask in hop_masks(hop):
                flip = [axis for i, axis in enumerate(hop) if (mask >> i) & 1]
                device = peer(sum(2 ** axis for axis in flip if axis != "y"), "y" in flip)
                for p in places:
                    target = pas.at[index + (WHOLE, pl.ds(p, strip))]
                    source = target if done else pas_hbm.at[:, s * strip : (s + 1) * strip]
                    pas_copy[s].append(send(source, target, device))

    pas_advance(0, 1, 2, 3)
    at_y = across(at, at_hbm)
    up_y = across(up, up_hbm)

    loads[2].wait()
    pas_advance(0, 1, 2, 3)

    nn = (((1,), (0,)), ((), ()))
    nt = (((1,), (1,)), ((), ()))

    def mm(left, right, dims):
        return lax.dot_general(left, right, dims, preferred_element_type=jnp.float32)

    loads[1].wait()
    loads[3].wait()
    latent = mm(ain[:, own_cols], at[:, own_cols], nt)

    def quarter_of(q):
        cols = q_at(q, other)
        return mm(ain[:, cols], at[:, cols], nt)

    at_x, at_c, up_x, up_c = [], [], [], []
    for i in pieces:
        at_y[i].wait_recv()
        at_x.append(pass_on(at, q0, i, 2))
        at_c.append(pass_on(at, q0, i, 1))
    pas_advance(3)
    for i in pieces:
        up_y[i].wait_recv()
        up_x.append(pass_on(up, q0, i, 2))
        up_c.append(pass_on(up, q0, i, 1))
    pas_advance(2, 0)
    latent = latent + quarter_of(q0)
    for i in pieces:
        at_x[i].wait_recv()
        at_c.append(pass_on(at, q2, i, 1))
    latent = latent + quarter_of(q2)
    pas_advance(1)
    for copy in at_c[:2]:
        copy.wait_recv()
    latent = latent + quarter_of(q1)
    for copy in at_c[2:]:
        copy.wait_recv()
    latent = latent + quarter_of(q3)
    code = latent.astype(jnp.bfloat16)
    code_t = code.astype(jnp.float32).T.astype(jnp.bfloat16)
    loads[0].wait()
    loads[4].wait()

    chunks = width // chunk
    lanes = 128

    def cols_of(j):
        if isinstance(j, int):
            return slice(j * chunk, (j + 1) * chunk)
        return pl.ds(pl.multiple_of(j * chunk, chunk), chunk)

    def fold(x):
        total = x[:, :lanes]
        for at in range(lanes, chunk, lanes):
            total = total + x[:, at : at + lanes]
        return total

    def forward(j, total):
        cols = cols_of(j)
        added = mm(code, up[:, cols], nn)
        sums = []
        for at in range(0, tokens, LEN):
            rows_at = slice(at, at + LEN)
            value = frz[rows_at, cols].astype(jnp.float32) + adapter_scale_factor * added[rows_at]
            hid[rows_at, cols] = value
            sums.append(fold(value * value))
        return total + jnp.concatenate(sums, axis=0)

    def loop(body, init, unroll=2):
        return lax.fori_loop(0, chunks, body, init, unroll=unroll)

    def of_query(q):
        return slice(q * LEN, (q + 1) * LEN)

    def forward_part(start, count, total):
        return lax.fori_loop(0, count, lambda j, t: forward(start + j, t), total, unroll=2)

    part_size = chunks // 4
    total = jnp.zeros((tokens, lanes), jnp.float32)
    total = forward_part(fs * (chunks // 2), part_size, total)
    for i in pieces:
        up_x[i].wait_recv()
        up_c.append(pass_on(up, q2, i, 1))
    total = forward_part(fs * (chunks // 2) + part_size, part_size, total)
    pas_advance(3, 2)
    for copy in up_c:
        copy.wait_recv()
    total = forward_part((1 - fs) * (chunks // 2), 2 * part_size, total)
    inv_rms = lax.rsqrt(jnp.sum(total, axis=1, keepdims=True) / width + norm_eps)

    pas_advance(0, 1, 2, 3)

    def pool(j, total):
        cols = cols_of(j)
        each = [
            jnp.sum(hid[of_query(q), cols] * inv_rms[of_query(q)], axis=0, keepdims=True)
            for q in range(queries)
        ]
        value = jnp.concatenate(each, axis=0) * (gain_ref[:, cols] * (1.0 / LEN))
        pooled[:, cols] = value
        return total + fold(value * value)

    total = loop(pool, jnp.zeros((queries, lanes), jnp.float32))
    length = jnp.sqrt(jnp.sum(total, axis=1, keepdims=True))
    inv_length = 1.0 / length

    def meet(j, totals):
        meets, squares = totals
        cols = cols_of(j)
        value = jnp.concatenate(
            [pas[block(k) + (WHOLE, cols)].astype(jnp.float32) for k in range(groups)], axis=0
        )
        narrow = value.astype(jnp.bfloat16)
        pasm[:, cols] = narrow
        gained = (hid[:, cols] * gain_ref[:, cols]).astype(jnp.bfloat16)
        return meets + mm(gained, narrow, nt), squares + fold(value * value)

    totals = jnp.zeros((tokens, pairs), jnp.float32), jnp.zeros((pairs, lanes), jnp.float32)
    for s in range(strips):
        pas_advance(s)
        for h, n in itertools.product((0, 1), range(strip // chunk)):
            totals = meet((h * half + s * strip) // chunk + n, totals)
    meets, squares = totals
    squares = jnp.broadcast_to(jnp.sum(squares, axis=1, keepdims=True), (pairs, lanes))
    inv_norm = 1.0 / jnp.sqrt(squares.T[0:1, :])
    met = meets * inv_norm
    scores = jnp.concatenate(
        [
            jnp.sum(met[of_query(q)] * inv_rms[of_query(q)], axis=0, keepdims=True)
            for q in range(queries)
        ],
        axis=0,
    ) * (inv_length * (inv_temp / LEN))
    expo = jnp.exp(scores - inv_temp)
    row_sum = jnp.sum(expo, axis=1, keepdims=True)
    row_at = lax.broadcasted_iota(jnp.int32, (queries, pairs), 0)
    col_at = lax.broadcasted_iota(jnp.int32, (queries, pairs), 1)
    onehot = jnp.zeros((queries, pairs), jnp.float32)
    for q in range(queries):
        hit = jnp.where(col_at == pos_ref[fs * queries + q], 1.0, 0.0)
        onehot = onehot + jnp.where(row_at == q, hit, 0.0)
    term = jnp.log(jnp.broadcast_to(row_sum, (queries, pairs))) * (1.0 / pairs)
    term = jnp.sum(term - 2.0 * scores * onehot, axis=0, keepdims=True)
    at8 = lax.broadcasted_iota(jnp.int32, (8, pairs), 0)
    col_part = jnp.broadcast_to(jnp.sum(expo, axis=0, keepdims=True), (8, pairs))
    payload = jnp.where(at8 == 0, col_part, jnp.where(at8 == 1, term, 0.0))

    slot = fs * 4 + q0
    near[slot] = payload
    copies = [send(near.at[slot], near.at[slot], peer(m, f)) for m, f in near_masks]

    def own_side(j, totals):
        totals, hidden_up = totals
        cols = cols_of(j)
        value = pooled[:, cols] * gain_ref[:, cols]
        hidden_up = hidden_up + mm(hid[:, cols].astype(jnp.bfloat16), up[:, cols], nt)
        return tuple(
            totals[q] + fold(hid[of_query(q), cols] * value[q : q + 1]) for q in range(queries)
        ), hidden_up

    own, hidden_up = loop(
        own_side,
        (
            tuple(jnp.zeros((LEN, lanes), jnp.float32) for _ in range(queries)),
            jnp.zeros((tokens, rank), jnp.float32),
        ),
    )
    own = [
        jnp.sum(own[q], axis=1, keepdims=True) * inv_length[q : q + 1] for q in range(queries)
    ]
    for copy in copies:
        copy.wait_recv()
    summed = near[0]
    for k in range(1, 8):
        summed = summed + near[k]
    slot = dp // 4
    far[slot] = summed
    copies = [send(far.at[slot], far.at[slot], peer(m, 0)) for m in far_masks]
    for copy in copies:
        copy.wait_recv()
    summed = far[0]
    for k in range(1, groups // 4):
        summed = summed + far[k]
    col_sum = summed[0:1]
    weights = 0.5 * (expo / row_sum + expo / col_sum) - onehot
    weights = weights.astype(jnp.bfloat16).astype(jnp.float32)
    along = jnp.sum(weights * scores, axis=1, keepdims=True)
    shrink = inv_length * (1.0 / LEN)
    back = []
    for q in range(queries):
        across = inv_temp * jnp.sum(met[of_query(q)] * weights[q : q + 1], axis=1, keepdims=True)
        mean = (across - own[q] * along[q : q + 1]) * shrink[q : q + 1] / width
        back.append(inv_rms[of_query(q)] ** 3 * mean)
    weights = weights * (inv_norm * inv_temp)
    high = weights.astype(jnp.bfloat16).astype(jnp.float32)
    both = jnp.concatenate([high, weights - high], axis=0).astype(jnp.bfloat16)
    inward = inv_length * along

    def query_side(j, total):
        cols = cols_of(j)
        two = mm(both, pasm[:, cols], nn)
        value = two[:queries] + two[queries:] - pooled[:, cols] * inward
        value = value * shrink * gain_ref[:, cols]
        scaled[:, cols] = value
        return total + mm(value.astype(jnp.bfloat16), up[:, cols], nt)

    def hidden_side(j, _):
        cols = cols_of(j)
        value = jnp.concatenate(
            [
                inv_rms[of_query(q)] * scaled[q : q + 1, cols] - hid[of_query(q), cols] * back[q]
                for q in range(queries)
            ],
            axis=0,
        ).astype(jnp.bfloat16)
        put(1, j, adapter_scale_factor * mm(code_t, value, nn))
        return 0

    def put(g, j, grad):
        grad = grad.astype(jnp.bfloat16)
        for n, (y, h) in enumerate(itertools.product((0, 1), repeat=2)):
            part[block(j) + (g, y, h)] = grad[n * rank // 4 : (n + 1) * rank // 4]

    def sided(body, side, init):
        def of(i, carry):
            return body(2 * i + side, carry)

        return lax.fori_loop(0, chunks // 2, of, init, unroll=2)

    theirs, ours = 1 - bit[0], bit[0]
    query_up = loop(query_side, jnp.zeros((queries, rank), jnp.float32), 4)
    code_grad = jnp.concatenate(
        [
            inv_rms[of_query(q)] * query_up[q : q + 1] - hidden_up[of_query(q)] * back[q]
            for q in range(queries)
        ],
        axis=0,
    )
    code_grad_t = (adapter_scale_factor * code_grad).astype(jnp.bfloat16)
    code_grad_t = code_grad_t.astype(jnp.float32).T.astype(jnp.bfloat16)

    def input_side(j, _):
        put(0, j, mm(code_grad_t, ain[:, cols_of(j)], nn))
        return 0

    chains = grad_chains(bits)
    grad_copies = [None] * len(chains)
    steps = len(chains[0][2])
    rx_of = iter(rx)
    rx_at = [[[next(rx_of) for _ in hop_masks(hop)] for hop in order] for _, _, order in chains]

    def view(n, k, mask):
        g, h, order = chains[n]
        fixed = [axis for hop in order[: k + 1] for axis in hop]
        flip = [axis for i, axis in enumerate(order[k]) if (mask >> i) & 1]
        index = ()
        for b in reversed(range(bits)):
            index += ((1 - bit[b] if b in flip else bit[b]) if b in fixed else WHOLE,)
        y = (1 - fs if "y" in flip else fs) if "y" in fixed else WHOLE
        return index + (g, y, h)

    def grad_send(n, k):
        hop = chains[n][2][k]
        grad_copies[n] = []
        for mask in hop_masks(hop):
            flip = [axis for i, axis in enumerate(hop) if (mask >> i) & 1]
            device = peer(sum(2 ** axis for axis in flip if axis != "y"), "y" in flip)
            source = part.at[view(n, k, mask)]
            grad_copies[n].append(send(source, rx_at[n][k][mask - 1], device))

    def grad_add(n, k):
        g, h, order = chains[n]
        kept = view(n, k, 0)
        for copy in grad_copies[n]:
            copy.wait_recv()
        free = [at for at, i in enumerate(kept) if isinstance(i, slice)]
        for picks in itertools.product((0, 1), repeat=len(free)):
            index = list(kept)
            for at_dim, pick in zip(free, picks):
                index[at_dim] = pick
            index = tuple(index)
            value = part[index].astype(jnp.float32)
            for buffer in rx_at[n][k]:
                value = value + buffer[picks].astype(jnp.float32)
            if k == len(order) - 1:
                out_ref[g, h * rank // 4 : (h + 1) * rank // 4] = value
            else:
                part[index] = value.astype(jnp.bfloat16)

    early = [n for n, c in enumerate(chains) if c[0] == 0]
    late = [n for n, c in enumerate(chains) if c[0] == 1]
    sided(input_side, theirs, 0)
    for n in early:
        grad_send(n, 0)
    sided(hidden_side, theirs, 0)
    for n in late:
        grad_send(n, 0)
    sided(input_side, ours, 0)
    for n in early:
        grad_add(n, 0)
        grad_send(n, 1)
    sided(hidden_side, ours, 0)
    for n in late:
        grad_add(n, 0)
        grad_send(n, 1)
    loss_ref[0, 0] = (
        jnp.sum(jnp.log(col_sum) + summed[1:2]) / (2.0 * pairs) + inv_temp
    )
    for k in range(1, steps):
        for n in early + late:
            grad_add(n, k)
            if k + 1 < steps:
                grad_send(n, k + 1)
    for copy in started:
        copy.wait_send()


def hop_masks(hop):
    return range(1, 2 ** len(hop))


def grad_chains(bits):
    last = tuple(range(2, bits))
    return [
        (1, 0, [(0,), (1,), ("y",), last]),
        (1, 1, [(0,), (2,), (1, "y"), last[1:]]),
        (0, 0, [(0,), ("y",), (1,), last]),
        (0, 1, [(0,), (2,), (1, "y"), last[1:]]),
    ]


def grad_shapes(bits, rank, chunk):
    shapes = []
    for _, _, order in grad_chains(bits):
        for k, hop in enumerate(order):
            fixed = sum(len(each) for each in order[: k + 1])
            shape = (2,) * (bits + 1 - fixed) + (rank // 4, chunk)
            shapes += [pltpu.VMEM(shape, jnp.bfloat16) for _ in hop_masks(hop)]
    return shapes


def fused_shards(bits, adapter_in, frozen, gain, adapter_a, adapter_up_matrix, passages, positive):
    tokens, width = adapter_in.shape
    rank = adapter_a.shape[1]
    queries = tokens // LEN
    rows = passages.shape[0]
    groups = 2 ** bits
    chunk = width // groups
    pairs = groups * rows
    half = width // 2
    bf16, f32 = jnp.bfloat16, jnp.float32
    rx = grad_shapes(bits, rank, chunk)
    copies = 96
    vmem = pl.BlockSpec(memory_space=pltpu.VMEM)
    smem = pl.BlockSpec(memory_space=pltpu.SMEM)
    hbm = pl.BlockSpec(memory_space=pl.ANY)
    grads, loss = pl.pallas_call(
        functools.partial(fused, bits, (tokens, width, rank, queries, rows, chunk)),
        out_shape=(
            jax.ShapeDtypeStruct((2, rank // 2, chunk), f32),
            jax.ShapeDtypeStruct((1, 1), f32),
        ),
        in_specs=[smem, vmem, hbm, hbm, hbm, hbm, hbm],
        out_specs=(vmem, smem),
        scratch_shapes=[
            pltpu.VMEM((tokens, width), bf16),
            pltpu.VMEM((tokens, width), bf16),
            pltpu.VMEM((rank, width), bf16),
            pltpu.VMEM((rank, width), bf16),
            pltpu.VMEM((2,) * bits + (rows, width), bf16),
            pltpu.VMEM((tokens, width), f32),
            pltpu.VMEM((pairs, width), bf16),
            pltpu.VMEM((2,) * bits + (2, 2, 2, rank // 4, chunk), bf16),
            pltpu.VMEM((queries, width), f32),
            pltpu.VMEM((queries, width), f32),
            pltpu.VMEM((8, 8, pairs), f32),
            pltpu.VMEM((groups // 4, 8, pairs), f32),
            rx,
            pltpu.SemaphoreType.DMA((5,)),
            pltpu.SemaphoreType.DMA((copies,)),
            pltpu.SemaphoreType.DMA((copies,)),
        ],
        compiler_params=pltpu.CompilerParams(
            collective_id=0, has_side_effects=True, vmem_limit_bytes=56 * 2 ** 20
        ),
    )(positive, gain.reshape(1, width), adapter_in, frozen, adapter_a.T, adapter_up_matrix, passages)
    return grads, loss.reshape(())


def solution(mesh):
    placed = (
        P(("dp", "fsdp"), None),
        P(("dp", "fsdp"), None),
        P(),
        P("fsdp", None),
        P(None, "fsdp"),
        P("dp", "fsdp"),
        P("dp"),
    )
    groups = mesh.shape["dp"]
    bits = groups.bit_length() - 1
    body = shards
    if mesh.shape["fsdp"] == 2 and groups == 16:
        body = functools.partial(fused_shards, bits)
    return jax.shard_map(
        body, mesh=mesh, in_specs=placed, out_specs=(P(None, "fsdp", "dp"), P()), check_vma=False
    )
```
